32 devices in a mesh: section: 2 (over x), dp: 2 (over y), ctx: 8 (over z, core).
Axes of the slice: x: 2, y: 2, z: 4, core: 2. Of those that a mesh axis runs over, the one named last changes fastest.
Arguments:
- tokens: bfloat16 [4, 2048, 960], P('dp', 'ctx'), may hold values from -6 to 6
- cotangent: bfloat16 [4, 2048, 960], P('dp', 'ctx'), may hold values from -6 to 6
- positions: int32 [4, 2048], P('dp', 'ctx'), may hold values from 0 to 2047, as said below
- attn_gain: bfloat16 [2, 960], P('section', ('dp', 'ctx')), may hold values from 0.5 to 1.5
- w_query: bfloat16 [2, 960, 960], P('section', ('dp', 'ctx')), may hold values from -0.1875 to 0.1875
- w_key: bfloat16 [2, 960, 320], P('section', ('dp', 'ctx')), may hold values from -0.1875 to 0.1875
- w_value: bfloat16 [2, 960, 320], P('section', ('dp', 'ctx')), may hold values from -0.1875 to 0.1875
- w_out: bfloat16 [2, 960, 960], P('section', ('dp', 'ctx')), may hold values from -3.5 to 3.5
- ffn_gain: bfloat16 [2, 960], P('section', ('dp', 'ctx')), may hold values from 0.5 to 1.5
- w_gate: bfloat16 [2, 960, 2560], P('section', ('dp', 'ctx')), may hold values from -0.1875 to 0.1875
- w_up: bfloat16 [2, 960, 2560], P('section', ('dp', 'ctx')), may hold values from -0.1875 to 0.1875
- w_down: bfloat16 [2, 2560, 960], P('section', ('dp', 'ctx')), may hold values from -0.125 to 0.125
Outputs:
- section_outputs: bfloat16 [2, 4, 2048, 960], P('section', 'dp', 'ctx')
- input_grads: float32 [2, 4, 2048, 960], P('section', 'dp', 'ctx')
- grad_attn_gain: float32 [2, 960], P('section', ('dp', 'ctx'))
- grad_query: float32 [2, 960, 960], P('section', ('dp', 'ctx'))
- grad_key: float32 [2, 960, 320], P('section', ('dp', 'ctx'))
- grad_value: float32 [2, 960, 320], P('section', ('dp', 'ctx'))
- grad_out: float32 [2, 960, 960], P('section', ('dp', 'ctx'))
- grad_ffn_gain: float32 [2, 960], P('section', ('dp', 'ctx'))
- grad_gate: float32 [2, 960, 2560], P('section', ('dp', 'ctx'))
- grad_up: float32 [2, 960, 2560], P('section', ('dp', 'ctx'))
- grad_down: float32 [2, 2560, 960], P('section', ('dp', 'ctx'))
The draws below stay inside these ranges and needn't reach their ends.
Inputs may be any that keep to these rules, and one draw needn't show every extreme that they name: `positions`: each sequence is a pack of documents: a token's position counts from its document's first token, and every sequence begins a document at its first token.
All inputs are finite; a program needn't handle non-finite values.
Results may differ from the reference program's by a relative error of at most 0.023.
Values may be sent and summed in bfloat16 or wider, within the bound.
No kernel may reach another device: no remote copies, remote signals or barrier semaphores. Data moves between devices by JAX's collectives and lax.ppermute only.
A program may use at most 192 MiB of HBM per device.

```python
import jax
import jax.numpy as jnp
from jax import lax

D = 960
H = 15
KV = 5
HD = 64
FF = 2560
LEN = 2048
SEQS = 4
SECTIONS = 2


def draw_positions(key, part):
    key = jax.random.fold_in(key, 11)
    key_one, key_two = jax.random.split(key, 2)
    column = jnp.arange(LEN, dtype=jnp.int32)
    starts = jax.random.randint(key_one, (SEQS, LEN), 0, LEN) < 4
    unbroken = jax.random.randint(key_two, (), 0, SEQS)
    starts = starts & (jnp.arange(SEQS, dtype=jnp.int32)[:, None] != unbroken)
    starts = starts | (column[None, :] == 0)
    doc_start = lax.cummax(jnp.where(starts, column[None, :], 0), axis=1)
    return (column[None, :] - doc_start).astype(jnp.int32)


def block_levels(stream_key, shape, cuts, low, largest):
    factor_of, own = 1.0, jax.random.fold_in(stream_key, 6)
    for axis_at, blocks in cuts:
        draws = jnp.exp(jax.random.uniform(jax.random.fold_in(own, axis_at), (blocks,), jnp.float32, low / len(cuts), largest / len(cuts)))
        factor_of = factor_of * jnp.repeat(draws, shape[axis_at] // blocks).reshape([-1 if axis == axis_at else 1 for axis in range(len(shape))])
    return factor_of


def noise(own_key, dims, width, bound, cuts=(), kind=jnp.bfloat16):
    entries = width * jax.random.normal(own_key, dims, jnp.float32)
    if cuts:
        entries = entries * block_levels(own_key, dims, cuts, -0.22, 0.18)
    return jnp.clip(entries, -bound, bound).astype(kind)


def setup_inputs(seed: int = 0) -> dict:
    splits = jax.random.split(jax.random.key(seed), 13)
    return {
        "tokens": noise(splits[0], (SEQS, LEN, D), 1.0, 6.0, ((0, 2), (1, 8))),
        "cotangent": noise(splits[1], (SEQS, LEN, D), 1.0, 6.0, ((0, 2), (1, 8))),
        "positions": draw_positions(jax.random.fold_in(splits[12], 71), 0),
        "attn_gain": jnp.clip(1.0 + 0.1 * jax.random.normal(splits[3], (SECTIONS, D), jnp.float32), 0.5, 1.5).astype(jnp.bfloat16),
        "w_query": noise(splits[4], (SECTIONS, D, H * HD), D ** -0.5, 0.1875, ((0, 2), (1, 16))),
        "w_key": noise(splits[5], (SECTIONS, D, KV * HD), D ** -0.5, 0.1875, ((0, 2), (1, 16))),
        "w_value": noise(splits[6], (SECTIONS, D, KV * HD), D ** -0.5, 0.1875, ((0, 2), (1, 16))),
        "w_out": noise(splits[7], (SECTIONS, H * HD, D), (max(D // 256, 1)) ** -0.5, 3.5, ((0, 2), (1, 16))),
        "ffn_gain": jnp.clip(1.0 + 0.1 * jax.random.normal(splits[8], (SECTIONS, D), jnp.float32), 0.5, 1.5).astype(jnp.bfloat16),
        "w_gate": noise(splits[9], (SECTIONS, D, FF), D ** -0.5, 0.1875, ((0, 2), (1, 16))),
        "w_up": noise(splits[10], (SECTIONS, D, FF), D ** -0.5, 0.1875, ((0, 2), (1, 16))),
        "w_down": noise(splits[11], (SECTIONS, FF, D), FF ** -0.5, 0.125, ((0, 2), (1, 16))),
    }


EPS = 1e-05

@jax.custom_vjp
def low(v):
    return lax.optimization_barrier(v.astype(jnp.bfloat16)).astype(jnp.float32)

@jax.custom_vjp
def low_back(v):
    return v

def low_keep(v):
    return (low(v), None)

def low_pass(kept, grad):
    return (grad,)

def back_keep(v):
    return (v, None)

def back_low(kept, grad):
    return (low(grad),)
low.defvjp(low_keep, low_pass)
low_back.defvjp(back_keep, back_low)

def matmul_hi(left_arr, right_arr):
    return jnp.einsum('bld,df->blf', left_arr, right_arr, precision=lax.Precision.HIGHEST)

def rotate_half(vector):
    half_dim = vector.shape[-1] // 2
    return jnp.concatenate([-vector[..., half_dim:], vector[..., :half_dim]], -1)

def rope_tables(seq_pos):
    half_dim = HD // 2
    inv_freq = 10000.0 ** (-(jnp.arange(half_dim, dtype=jnp.float32) * 2.0) / HD)
    angles = seq_pos.astype(jnp.float32)[..., None] * inv_freq
    angle_pair = jnp.concatenate([angles, angles], -1)[..., None, :]
    return (jnp.cos(angle_pair), jnp.sin(angle_pair))

def rmsnorm(values_in, gain_vec):
    factor = lax.rsqrt(lax.optimization_barrier(jnp.mean(values_in * values_in, -1, keepdims=True)) + EPS)
    return values_in * factor * gain_vec

def attention(queries, keys, values):
    batch_size, length = (queries.shape[0], queries.shape[1])
    block_rows = min(512, length)
    block_count = length // block_rows
    groups = H // KV
    blocks = jnp.moveaxis(queries.reshape(batch_size, block_count, block_rows, KV, groups, HD), 1, 0)
    block_starts = jnp.arange(block_count, dtype=jnp.int32) * block_rows
    column = jnp.arange(length, dtype=jnp.int32)

    @jax.checkpoint
    def one_block(operands):
        query_block, block_start = operands
        scores = jnp.einsum('bqkgd,bjkd->bkgqj', query_block, keys, precision=lax.Precision.HIGHEST) * HD ** (-0.5)
        scores = low_back(scores)
        row_ids = block_start + jnp.arange(block_rows, dtype=jnp.int32)
        visible = column[None, :] <= row_ids[:, None]
        scores = jnp.where(visible, scores, -1e+30)
        probs = low(jax.nn.softmax(scores, axis=-1))
        return jnp.einsum('bkgqj,bjkd->bqkgd', probs, values, precision=lax.Precision.HIGHEST)
    result = lax.map(one_block, (blocks, block_starts))
    return jnp.moveaxis(result, 0, 1).reshape(batch_size, length, H, HD)

def layer(layer_in, cosine, sine, params):
    gain_a, w_q, w_k, w_v, w_o, gain_f, w_g, w_u, w_d = params
    batch_size, length = (layer_in.shape[0], layer_in.shape[1])
    normed = low(rmsnorm(layer_in, gain_a))
    queries = low_back(matmul_hi(normed, w_q)).reshape(batch_size, length, H, HD)
    queries = low(queries * cosine + rotate_half(queries) * sine)
    keys = low_back(matmul_hi(normed, w_k)).reshape(batch_size, length, KV, HD)
    keys = low(keys * cosine + rotate_half(keys) * sine)
    values = low(low_back(matmul_hi(normed, w_v))).reshape(batch_size, length, KV, HD)
    attended = low(low_back(attention(queries, keys, values))).reshape(batch_size, length, H * HD)
    mixed_res = layer_in + low_back(matmul_hi(attended, w_o))
    normed_f = low(rmsnorm(mixed_res, gain_f))
    gate_act = low_back(matmul_hi(normed_f, w_g))
    up_proj = low_back(matmul_hi(normed_f, w_u))
    hidden = low(jax.nn.silu(gate_act) * up_proj)
    return mixed_res + low_back(matmul_hi(hidden, w_d))

def reference(tokens, cotangent, positions, attn_gain, w_query, w_key, w_value, w_out, ffn_gain, w_gate, w_up, w_down):
    params = tuple((weight_arr.astype(jnp.float32) for weight_arr in (attn_gain, w_query, w_key, w_value, w_out, ffn_gain, w_gate, w_up, w_down)))
    pair_count = SEQS // 2

    def in_pairs(array_in):
        return array_in.reshape((pair_count, 2) + array_in.shape[1:])

    def step(grad_total, step_items):
        seq_input, seq_grad, seq_pos = step_items
        cosine, sine = rope_tables(seq_pos)

        def forward(layer_in, probe_add, weights):
            first_out = low(layer(layer_in, cosine, sine, tuple((weight_arr[0] for weight_arr in weights))))
            second_out = layer(low_back(first_out + probe_add), cosine, sine, tuple((weight_arr[1] for weight_arr in weights)))
            return (second_out, first_out)
        layer_in = seq_input.astype(jnp.float32)
        second_out, pullback, first_out = jax.vjp(forward, layer_in, jnp.zeros_like(layer_in), params, has_aux=True)
        d_first, d_second, d_weights = pullback(seq_grad.astype(jnp.float32))
        grad_total = tuple((left_arr + right_arr for left_arr, right_arr in zip(grad_total, d_weights)))
        return (grad_total, (first_out.astype(jnp.bfloat16), second_out.astype(jnp.bfloat16), d_first, d_second))
    grad_zero = tuple((jnp.zeros_like(weight_arr) for weight_arr in params))
    grads, (firsts, seconds, d_firsts, d_seconds) = lax.scan(step, grad_zero, (in_pairs(tokens), in_pairs(cotangent), in_pairs(positions)))
    full_shape = (SEQS, LEN, D)
    section_outputs = jnp.stack([firsts.reshape(full_shape), seconds.reshape(full_shape)])
    input_grads = jnp.stack([d_firsts.reshape(full_shape), d_seconds.reshape(full_shape)])
    return (section_outputs, input_grads, grads[0], grads[1], grads[2], grads[3], grads[4], grads[5], grads[6], grads[7], grads[8])
```

```python
import functools

import jax
import jax.numpy as jnp
from jax import lax
from jax.experimental import pallas as pl
from jax.experimental.pallas import tpu as pltpu
from jax.sharding import Mesh
from jax.sharding import PartitionSpec as P

D = 960
H = 15
KV = 5
G = H // KV
HD = 64
FF = 2560
EPS = 1e-05
F32 = jnp.float32
BF = jnp.bfloat16


def dot(a,b): return jnp.dot(a,b,preferred_element_type=F32)

def fwd_kernel(rng, q_ref, kv_ref, o_ref, lse_ref, qt, vt, m_s, l_s, acc):
    T=q_ref.shape[0]; W=G*T
    qt[...]=q_ref[...].astype(F32).T.astype(BF)
    nb=kv_ref.shape[0]
    def step(b, first):
        vt[...]=kv_ref[b,:,KV*HD:].astype(F32).T.astype(BF)
        for g in range(KV):
            qg=jnp.concatenate([qt[(g*G+j)*HD:(g*G+j+1)*HD,:] for j in range(G)],1)
            s=dot(kv_ref[b,:,g*HD:(g+1)*HD],qg)
            if first:
                key=lax.broadcasted_iota(jnp.int32,(T,W),0)
                qry=lax.broadcasted_iota(jnp.int32,(T,W),1)%T
                s=jnp.where(key<=qry,s,-1e30)
                m=jnp.max(s,0,keepdims=True)
                p=jnp.exp(s-m)
                l_s[g:g+1,:]=jnp.sum(p,0,keepdims=True)
                acc[g*HD:(g+1)*HD,:]=dot(vt[g*HD:(g+1)*HD,:],p.astype(BF))
            else:
                mo=m_s[g:g+1,:]
                m=jnp.maximum(mo,jnp.max(s,0,keepdims=True))
                p=jnp.exp(s-m); al=jnp.exp(mo-m)
                l_s[g:g+1,:]=l_s[g:g+1,:]*al+jnp.sum(p,0,keepdims=True)
                acc[g*HD:(g+1)*HD,:]=acc[g*HD:(g+1)*HD,:]*al+dot(vt[g*HD:(g+1)*HD,:],p.astype(BF))
            m_s[g:g+1,:]=m
    step(0,True)
    def body(b,_):
        step(b,False); return 0
    lax.fori_loop(rng[0],rng[1],body,0)
    for g in range(KV):
        inv=1.0/l_s[g:g+1,:]
        lse_ref[g:g+1,:]=m_s[g:g+1,:]+jnp.log(l_s[g:g+1,:])
        og=acc[g*HD:(g+1)*HD,:]*inv
        for j in range(G):
            h=g*G+j
            o_ref[:,h*HD:(h+1)*HD]=og[:,j*T:(j+1)*T].T.astype(BF)

def attn_fwd(rng,q,kv):
    T=q.shape[0]; W=G*T
    return pl.pallas_call(fwd_kernel,
      out_shape=(jax.ShapeDtypeStruct((T,H*HD),BF),jax.ShapeDtypeStruct((KV,W),F32)),
      in_specs=[pl.BlockSpec(memory_space=pltpu.SMEM)]+[pl.BlockSpec(memory_space=pltpu.VMEM)]*2,
      out_specs=[pl.BlockSpec(memory_space=pltpu.VMEM)]*2,
      scratch_shapes=[pltpu.VMEM((H*HD,T),BF),pltpu.VMEM((KV*HD,T),BF),pltpu.VMEM((KV,W),F32),pltpu.VMEM((KV,W),F32),pltpu.VMEM((KV*HD,W),F32)],
      compiler_params=pltpu.CompilerParams(vmem_limit_bytes=48<<20),
    )(rng,q,kv)

def bwd_kernel(rng, q_ref, kv_ref, o_ref, do_ref, lse_ref, dq_ref, dkv_ref, qt, dot_, qn, don, kt, dl, dqa):
    T=q_ref.shape[0]; W=G*T
    nb=kv_ref.shape[0]
    qt[...]=q_ref[...].astype(F32).T.astype(BF)
    doT=do_ref[...].astype(F32).T
    dot_[...]=doT.astype(BF)
    oT=o_ref[...].astype(F32).T
    prod=doT*oT
    for h in range(H):
        g,j=divmod(h,G)
        dl[g:g+1,j*T:(j+1)*T]=jnp.sum(prod[h*HD:(h+1)*HD,:],0,keepdims=True)
        qn[g,j*T:(j+1)*T,:]=q_ref[:,h*HD:(h+1)*HD]
        don[g,j*T:(j+1)*T,:]=do_ref[:,h*HD:(h+1)*HD]
    def step(b, first):
        kt[...]=kv_ref[b,:,:KV*HD].astype(F32).T.astype(BF)
        for g in range(KV):
            qg=jnp.concatenate([qt[(g*G+j)*HD:(g*G+j+1)*HD,:] for j in range(G)],1)
            dg=jnp.concatenate([dot_[(g*G+j)*HD:(g*G+j+1)*HD,:] for j in range(G)],1)
            s=dot(kv_ref[b,:,g*HD:(g+1)*HD],qg)
            p=jnp.exp(s-lse_ref[g:g+1,:])
            if first:
                key=lax.broadcasted_iota(jnp.int32,(T,W),0)
                qry=lax.broadcasted_iota(jnp.int32,(T,W),1)%T
                p=jnp.where(key<=qry,p,0.0)
            dp=dot(kv_ref[b,:,(KV+g)*HD:(KV+g+1)*HD],dg)
            dz=(p*(dp-dl[g:g+1,:])).astype(BF)
            dkv_ref[b,:,(KV+g)*HD:(KV+g+1)*HD]=dot(p.astype(BF),don[g]).astype(BF)
            dkv_ref[b,:,g*HD:(g+1)*HD]=dot(dz,qn[g]).astype(BF)
            dq=dot(kt[g*HD:(g+1)*HD,:],dz)
            if first: dqa[g*HD:(g+1)*HD,:]=dq
            else: dqa[g*HD:(g+1)*HD,:]+=dq
    step(0,True)
    def body(b,_):
        step(b,False); return 0
    lax.fori_loop(rng[0],rng[1],body,0)
    def zero(b,_):
        dkv_ref[b]=jnp.zeros((T,2*KV*HD),BF); return 0
    lax.fori_loop(1,rng[0],zero,0)
    lax.fori_loop(rng[1],nb,zero,0)
    for g in range(KV):
        for j in range(G):
            h=g*G+j
            dq_ref[:,h*HD:(h+1)*HD]=(dqa[g*HD:(g+1)*HD,j*T:(j+1)*T]*HD**-0.5).T

def attn_bwd(rng,q,kv,o,do,lse):
    T=q.shape[0]; W=G*T
    return pl.pallas_call(bwd_kernel,
      out_shape=(jax.ShapeDtypeStruct((T,H*HD),F32),jax.ShapeDtypeStruct(kv.shape,BF)),
      in_specs=[pl.BlockSpec(memory_space=pltpu.SMEM)]+[pl.BlockSpec(memory_space=pltpu.VMEM)]*5,
      out_specs=[pl.BlockSpec(memory_space=pltpu.VMEM)]*2,
      scratch_shapes=[pltpu.VMEM((H*HD,T),BF),pltpu.VMEM((H*HD,T),BF),pltpu.VMEM((KV,W,HD),BF),pltpu.VMEM((KV,W,HD),BF),
        pltpu.VMEM((KV*HD,T),BF),pltpu.VMEM((KV,W),F32),pltpu.VMEM((KV*HD,W),F32)],
      compiler_params=pltpu.CompilerParams(vmem_limit_bytes=48<<20),
    )(rng,q,kv,o,do,lse)


def rotate_half(vector):
    half_dim = vector.shape[-1] // 2
    return jnp.concatenate([-vector[..., half_dim:], vector[..., :half_dim]], -1)


def rope_tables(seq_pos):
    half_dim = HD // 2
    inv_freq = 10000.0 ** (-(jnp.arange(half_dim, dtype=F32) * 2.0) / HD)
    angles = seq_pos.astype(F32)[..., None] * inv_freq
    angle_pair = jnp.concatenate([angles, angles], -1)[..., None, :]
    return (jnp.cos(angle_pair), jnp.sin(angle_pair))


def norm_forward(values_in, gain_vec):
    factor = lax.rsqrt(jnp.mean(values_in * values_in, -1, keepdims=True) + EPS)
    return (values_in * factor * gain_vec, factor)


def norm_backward(grad_in, values_in, factor, gain_vec):
    scaled = grad_in * gain_vec
    grad_back = factor * scaled - values_in * factor * factor * factor * jnp.mean(
        scaled * values_in, -1, keepdims=True
    )
    return (grad_back, jnp.sum(grad_in * values_in * factor, 0))


def swap(block, axis):
    return lax.ppermute(block, axis, [(0, 1), (1, 0)])


def move_z(block, distance):
    count = lax.axis_size("z")
    route = [(i, i + distance) for i in range(count) if 0 <= i + distance < count]
    return lax.ppermute(block, "z", route)


def gather_kv(block):
    count = lax.axis_size("z")
    own = [block] + [move_z(block, d) for d in range(1, count)]
    own = jnp.stack(own)
    other = swap(own, "core")
    return jnp.stack([own, other], 1).reshape((2 * count,) + block.shape)


def reduce_kv(blocks):
    count = lax.axis_size("z")
    blocks = blocks.reshape((count, 2) + blocks.shape[1:])
    mine = blocks[:, 0].astype(F32) + swap(blocks[:, 1], "core").astype(F32)
    total = mine[0]
    for d in range(1, count):
        total = total + move_z(mine[d].astype(BF), -d).astype(F32)
    return total


def project(left, right):
    return jnp.dot(left, right, preferred_element_type=F32)


def project_t(left, right):
    return lax.dot_general(left, right, (((1,), (1,)), ((), ())), preferred_element_type=F32)


def outer(left, right):
    return lax.dot_general(left, right, (((0,), (0,)), ((), ())), preferred_element_type=F32)


def rope(values, cosine, sine):
    count = values.shape[0]
    values = values.reshape(count, -1, HD)
    return (values * cosine + rotate_half(values) * sine).reshape(count, -1)


def rope_t(values, cosine, sine):
    count = values.shape[0]
    values = values.reshape(count, -1, HD)
    return (values * cosine - rotate_half(values * sine)).reshape(count, -1)


def layer_forward(rows, tables, weights, block_range):
    gain_a, w_qkv, w_o, gain_f, w_g, w_u, w_d = weights
    cosine, sine = tables
    normed_a, factor_a = norm_forward(rows, gain_a)
    normed_a = normed_a.astype(BF)
    qkv = project(normed_a, w_qkv)
    queries = (rope(qkv[:, :D], cosine, sine)).astype(BF) * BF(HD**-0.5)
    keys = rope(qkv[:, D : D + KV * HD], cosine, sine).astype(BF)
    values = qkv[:, D + KV * HD :].astype(BF)
    kv_all = gather_kv(jnp.concatenate([keys, values], -1))
    attended, log_total = attn_fwd(block_range, queries, kv_all)
    mixed = rows + project(attended, w_o)
    normed_f, factor_f = norm_forward(mixed, gain_f)
    normed_f = normed_f.astype(BF)
    gate_act = project(normed_f, w_g)
    up_proj = project(normed_f, w_u)
    hidden = (jax.nn.silu(gate_act) * up_proj).astype(BF)
    out = (mixed + project(hidden, w_d)).astype(BF)
    saved = (rows, factor_a, normed_a, queries, kv_all, log_total, attended, mixed, factor_f, normed_f, gate_act, up_proj, hidden)
    return out, saved


def layer_backward(grad_low, saved, tables, weights, block_range):
    gain_a, w_qkv, w_o, gain_f, w_g, w_u, w_d = weights
    cosine, sine = tables
    rows, factor_a, normed_a, queries, kv_all, log_total, attended, mixed, factor_f, normed_f, gate_act, up_proj, hidden = saved
    d_hidden = project_t(grad_low, w_d)
    sig = jax.nn.sigmoid(gate_act)
    d_gate = (d_hidden * up_proj * sig * (1.0 + gate_act * (1.0 - sig))).astype(BF)
    d_up = (d_hidden * gate_act * sig).astype(BF)
    d_normed_f = project_t(d_gate, w_g) + project_t(d_up, w_u)
    d_norm, d_gain_f = norm_backward(d_normed_f, mixed, factor_f, gain_f)
    d_mixed = grad_low.astype(F32) + d_norm
    mix_low = d_mixed.astype(BF)
    d_attended = project_t(mix_low, w_o).astype(BF)
    d_query, d_kv = attn_bwd(block_range, queries, kv_all, attended, d_attended, log_total)
    d_kv = reduce_kv(d_kv)
    d_query = rope_t(d_query, cosine, sine).astype(BF)
    d_key = rope_t(d_kv[:, : KV * HD], cosine, sine).astype(BF)
    d_value = d_kv[:, KV * HD :].astype(BF)
    d_qkv = jnp.concatenate([d_query, d_key, d_value], -1)
    d_normed_a = project_t(d_qkv, w_qkv)
    d_norm_a, d_gain_a = norm_backward(d_normed_a, rows, factor_a, gain_a)
    d_rows = d_mixed + d_norm_a
    grads = dict(
        gate=outer(normed_f, d_gate).astype(BF),
        up=outer(normed_f, d_up).astype(BF),
        down=outer(hidden, grad_low).astype(BF),
        out=outer(attended, mix_low).astype(BF),
        qkv=outer(normed_a, d_qkv).astype(BF),
        gains=jnp.stack([d_gain_a, d_gain_f]),
    )
    return d_rows, grads


def per_device(tokens, cotangent, positions, attn_gain, w_query, w_key, w_value, w_out, ffn_gain, w_gate, w_up, w_down):
    section = lax.axis_index("section")
    z_index, core = lax.axis_index("z"), lax.axis_index("core")
    plane = ("dp", "z", "core")
    group = tokens.shape[0]
    local = tokens.shape[1]
    block_range = jnp.stack([2 - core, 2 * z_index + 2]).astype(jnp.int32)

    def mine(array_in):
        return lax.dynamic_index_in_dim(array_in, section, 0, keepdims=False)

    rows = tokens.shape[1]
    shard_rows = w_query.shape[1]
    ff_rows = w_down.shape[1]
    half = ff_rows // 2
    qkvo = jnp.concatenate([w_query[0], w_key[0], w_value[0], w_out[0]], -1)
    down = jnp.concatenate([w_down[0, :half], jnp.zeros((half, 64), BF), w_down[0, half:], jnp.zeros((half, 576), BF)], -1)
    gains = jnp.concatenate([attn_gain, ffn_gain], -1)
    shard = jnp.concatenate([qkvo, w_gate[0], w_up[0], down], 0)
    shard = lax.dynamic_update_slice(shard, gains, (3 * shard_rows, 2048))
    other = swap(shard, "section")

    def assemble(block):
        whole = lax.all_gather(block, plane, axis=0)
        n = shard_rows

        def piece(lo, hi):
            return whole[:, lo : lo + n, :hi].reshape(-1, hi) if hi <= FF else None

        attn = whole[:, :n, :].reshape(n * whole.shape[0], FF)
        w_g = whole[:, n : 2 * n, :].reshape(-1, FF)
        w_u = whole[:, 2 * n : 3 * n, :].reshape(-1, FF)
        w_d = jnp.concatenate([whole[:, 3 * n :, :D], whole[:, 3 * n :, 1024 : 1024 + D]], 1).reshape(-1, D)
        gain_rows = whole[:, 3 * n, 2048 : 2048 + 2 * n].astype(F32)
        gain_a = gain_rows[:, :n].reshape(-1)
        gain_f = gain_rows[:, n:].reshape(-1)
        return gain_a, attn[:, : D + 2 * KV * HD], attn[:, D + 2 * KV * HD :], gain_f, w_g, w_u, w_d

    w0 = assemble(jnp.where(section == 0, shard, other))
    w1 = assemble(jnp.where(section == 1, shard, other))
    tables = rope_tables(mine(positions))
    out0, saved0 = layer_forward(mine(tokens).astype(F32), tables, w0, block_range)
    out1, saved1 = layer_forward(out0.astype(F32), tables, w1, block_range)
    d1, g1 = layer_backward(mine(cotangent), saved1, tables, w1, block_range)
    d1_low = d1.astype(BF)
    d0, g0 = layer_backward(d1_low, saved0, tables, w0, block_range)

    def pair(own, got):
        return jnp.where(section == 0, jnp.stack([own, got]), jnp.stack([got, own]))

    got = swap(jnp.where(section == 0, out1, out0), "section")
    section_out = pair(jnp.where(section == 0, out0, out1), got)
    got = swap(jnp.where(section == 0, d1_low, d0.astype(BF)), "section").astype(F32)
    input_grad = pair(jnp.where(section == 0, d0, d1_low.astype(F32)), got)

    def reduce(first, second):
        def scatter(part):
            return lax.psum_scatter(part, plane, scatter_dimension=0, tiled=True)

        s0, s1 = scatter(first), scatter(second)
        got = swap(jnp.where(section == 0, s1, s0), "section")
        return jnp.where(section == 0, s0, s1).astype(F32) + got.astype(F32)

    grads = {name: reduce(g0[name], g1[name]) for name in ("gate", "up", "down", "out", "qkv")}
    gain_grad = reduce(g0["gains"].T, g1["gains"].T)
    qkv = grads["qkv"]
    kd = KV * HD
    outs = (
        section_out,
        input_grad,
        gain_grad[:, 0],
        qkv[:, :D],
        qkv[:, D : D + kd],
        qkv[:, D + kd :],
        grads["out"],
        gain_grad[:, 1],
        grads["gate"],
        grads["up"],
        grads["down"],
    )
    return tuple(part[None] for part in outs)


LANES = 128
PADDED = 1024
CHUNK = 640
KVW = 2 * KV * HD
QKV_BLOCKS = 13
ACTS = FF + 3 * PADDED
BACK = 2 * FF + 2 * PADDED
OUT_BLOCKS = PADDED // LANES
FF_BLOCKS = FF // LANES
VMEM = pl.BlockSpec(memory_space=pltpu.VMEM)
ANY = pl.BlockSpec(memory_space=pl.ANY)
SMEM = pl.BlockSpec(memory_space=pltpu.SMEM)
BIG = pltpu.CompilerParams(vmem_limit_bytes=56 << 20)


def dot_nt(left, right):
    return lax.dot_general(left, right, (((1,), (1,)), ((), ())), preferred_element_type=F32)


def columns(ref, first, count, rows):
    parts = [
        ref[:, first + i * rows : first + (i + 1) * rows, :].reshape(-1, LANES) for i in range(count)
    ]
    return parts[0] if count == 1 else jnp.concatenate(parts, 1)


def half_of(values):
    lane = lax.broadcasted_iota(jnp.int32, values.shape, 1)
    back = pltpu.roll(values, LANES - HD // 2, 1)
    ahead = pltpu.roll(values, HD // 2, 1)
    return jnp.where(lane % HD < HD // 2, -back, ahead)


def rms(values):
    return lax.rsqrt(jnp.sum(values * values, -1, keepdims=True) / D + EPS)


def norm_back(grad, values, gain):
    factor = rms(values)
    scaled = grad * gain
    mean = jnp.sum(scaled * values, -1, keepdims=True) / D
    back = factor * scaled - values * (factor * factor * factor * mean)
    return back, jnp.sum(grad * values * factor, 0, keepdims=True)


def load_kv(blocks, other, kv_s, sems):
    copies = [pltpu.make_async_copy(block, kv_s.at[0, d], sems.at[d]) for d, block in enumerate(blocks)]
    copies.append(pltpu.make_async_copy(other, kv_s.at[1], sems.at[len(blocks)]))
    for copy in copies:
        copy.start()
    return copies


def attend_kernel(zs, rng, q_ref, *refs):
    blocks, (other, o_ref, lse_ref, kv_s, qt, vt, m_s, l_s, acc, sems) = refs[:zs], refs[zs:]
    T = q_ref.shape[0]
    W = G * T
    copies = load_kv(blocks, other, kv_s, sems)
    qt[...] = q_ref[...].astype(F32).T.astype(BF)
    for copy in copies:
        copy.wait()

    def step(b, first):
        kv = kv_s.at[lax.rem(b, 2), lax.div(b, 2)] if not first else kv_s.at[0, 0]
        vt[...] = kv[:, KV * HD :].astype(F32).T.astype(BF)
        for g in range(KV):
            at = slice(g * HD, (g + 1) * HD)
            qg = jnp.concatenate([qt[(g * G + j) * HD : (g * G + j + 1) * HD, :] for j in range(G)], 1)
            s = dot(kv[:, at], qg)
            if first:
                key = lax.broadcasted_iota(jnp.int32, (T, W), 0)
                query = lax.broadcasted_iota(jnp.int32, (T, W), 1) % T
                s = jnp.where(key <= query, s, -1e30)
                m = jnp.max(s, 0, keepdims=True)
                p = jnp.exp(s - m)
                l_s[g : g + 1, :] = jnp.sum(p, 0, keepdims=True)
                acc[at, :] = dot(vt[at, :], p.astype(BF))
            else:
                old = m_s[g : g + 1, :]
                m = jnp.maximum(old, jnp.max(s, 0, keepdims=True))
                p = jnp.exp(s - m)
                scale = jnp.exp(old - m)
                l_s[g : g + 1, :] = l_s[g : g + 1, :] * scale + jnp.sum(p, 0, keepdims=True)
                acc[at, :] = acc[at, :] * scale + dot(vt[at, :], p.astype(BF))
            m_s[g : g + 1, :] = m

    step(0, True)

    def body(b, _):
        step(b, False)
        return 0

    lax.fori_loop(rng[0], rng[1], body, 0)
    for g in range(KV):
        lse_ref[g : g + 1, :] = m_s[g : g + 1, :] + jnp.log(l_s[g : g + 1, :])
        og = acc[g * HD : (g + 1) * HD, :] / l_s[g : g + 1, :]
        for j in range(G):
            h = g * G + j
            o_ref[:, h * HD : (h + 1) * HD] = og[:, j * T : (j + 1) * T].T.astype(BF)


def attend(rng, q, kv_all):
    blocks, other = kv_all
    T, zs = q.shape[0], len(blocks)
    W = G * T
    return pl.pallas_call(
        functools.partial(attend_kernel, zs),
        out_shape=(jax.ShapeDtypeStruct((T, D), BF), jax.ShapeDtypeStruct((KV, W), F32)),
        in_specs=[SMEM, VMEM] + [ANY] * (zs + 1),
        out_specs=[VMEM] * 2,
        scratch_shapes=[
            pltpu.VMEM((2, zs, T, KVW), BF),
            pltpu.VMEM((D, T), BF),
            pltpu.VMEM((KV * HD, T), BF),
            pltpu.VMEM((KV, W), F32),
            pltpu.VMEM((KV, W), F32),
            pltpu.VMEM((KV * HD, W), F32),
            pltpu.SemaphoreType.DMA((zs + 1,)),
        ],
        compiler_params=BIG,
        name="attend",
    )(rng, q, *blocks, other)


def attend_back_kernel(zs, rng, q_ref, o_ref, do_ref, lse_ref, cos_ref, sin_ref, *refs):
    blocks, (other, dq_ref, dkv_ref, kv_s, qt, dot_, qn, don, kt, dl, dqa, sems) = refs[:zs], refs[zs:]
    T = q_ref.shape[0]
    W = G * T
    copies = load_kv(blocks, other, kv_s, sems)
    qt[...] = q_ref[...].astype(F32).T.astype(BF)
    do_t = do_ref[...].astype(F32).T
    dot_[...] = do_t.astype(BF)
    prod = do_t * o_ref[...].astype(F32).T
    for h in range(H):
        g, j = divmod(h, G)
        rows = slice(j * T, (j + 1) * T)
        dl[g : g + 1, rows] = jnp.sum(prod[h * HD : (h + 1) * HD, :], 0, keepdims=True)
        qn[g, rows, :] = q_ref[:, h * HD : (h + 1) * HD]
        don[g, rows, :] = do_ref[:, h * HD : (h + 1) * HD]
    for copy in copies:
        copy.wait()

    def step(b, first):
        side, far = (0, 0) if first else (lax.rem(b, 2), lax.div(b, 2))
        kv = kv_s.at[side, far]
        out = dkv_ref.at[side, far]
        kt[...] = kv[:, : KV * HD].astype(F32).T.astype(BF)
        for g in range(KV):
            at = slice(g * HD, (g + 1) * HD)
            vat = slice((KV + g) * HD, (KV + g + 1) * HD)
            heads = [slice((g * G + j) * HD, (g * G + j + 1) * HD) for j in range(G)]
            s = dot(kv[:, at], jnp.concatenate([qt[h, :] for h in heads], 1))
            p = jnp.exp(s - lse_ref[g : g + 1, :])
            if first:
                key = lax.broadcasted_iota(jnp.int32, (T, W), 0)
                query = lax.broadcasted_iota(jnp.int32, (T, W), 1) % T
                p = jnp.where(key <= query, p, 0.0)
            dp = dot(kv[:, vat], jnp.concatenate([dot_[h, :] for h in heads], 1))
            dz = (p * (dp - dl[g : g + 1, :])).astype(BF)
            out[:, vat] = dot(p.astype(BF), don[g]).astype(BF)
            out[:, at] = dot(dz, qn[g]).astype(BF)
            dq = dot(kt[at, :], dz)
            if first:
                dqa[at, :] = dq
            else:
                dqa[at, :] += dq

    step(0, True)

    def body(b, _):
        step(b, False)
        return 0

    def zero(b, _):
        dkv_ref[lax.rem(b, 2), lax.div(b, 2)] = jnp.zeros((T, KVW), BF)
        return 0

    lax.fori_loop(rng[0], rng[1], body, 0)
    lax.fori_loop(1, rng[0], zero, 0)
    lax.fori_loop(rng[1], 2 * zs, zero, 0)
    cos, sin = cos_ref[...], sin_ref[...]
    for pair in range(PADDED // LANES):
        parts = []
        for h in (2 * pair, 2 * pair + 1):
            g, j = divmod(h, G)
            if h < H:
                parts.append(dqa[g * HD : (g + 1) * HD, j * T : (j + 1) * T] * HD**-0.5)
            else:
                parts.append(jnp.zeros((HD, T), F32))
        grad = jnp.concatenate(parts, 0).T
        turned = grad * cos - half_of(grad * sin)
        dq_ref[:, pair * LANES : (pair + 1) * LANES] = turned.astype(BF)


def attend_back(rng, q, o, do, lse, cos, sin, kv_all):
    blocks, other = kv_all
    T, zs = q.shape[0], len(blocks)
    W = G * T
    return pl.pallas_call(
        functools.partial(attend_back_kernel, zs),
        out_shape=(jax.ShapeDtypeStruct((T, PADDED), BF), jax.ShapeDtypeStruct((2, zs, T, KVW), BF)),
        in_specs=[SMEM] + [VMEM] * 6 + [ANY] * (zs + 1),
        out_specs=[VMEM] * 2,
        scratch_shapes=[
            pltpu.VMEM((2, zs, T, KVW), BF),
            pltpu.VMEM((D, T), BF),
            pltpu.VMEM((D, T), BF),
            pltpu.VMEM((KV, W, HD), BF),
            pltpu.VMEM((KV, W, HD), BF),
            pltpu.VMEM((KV * HD, T), BF),
            pltpu.VMEM((KV, W), F32),
            pltpu.VMEM((KV * HD, W), F32),
            pltpu.SemaphoreType.DMA((zs + 1,)),
        ],
        compiler_params=BIG,
        name="attend_back",
    )(rng, q, o, do, lse, cos, sin, *blocks, other)


def spread_kv(block):
    blocks = [block] + [move_z(block, d) for d in range(1, lax.axis_size("z"))]
    return blocks, swap(jnp.stack(blocks), "core")


def collect_kv(grads):
    mine = grads[0].astype(F32) + swap(grads[1], "core").astype(F32)
    mine = mine.astype(BF)
    return [mine[0]] + [move_z(mine[d], -d) for d in range(1, lax.axis_size("z"))]


def qkv_kernel(base, x_ref, gain_ref, cos_ref, sin_ref, w_hbm, na_ref, q_ref, kv_ref, w_s, sem):
    rows = w_s.shape[1] // QKV_BLOCKS
    copy = pltpu.make_async_copy(w_hbm.at[:, pl.ds(base, w_s.shape[1]), :], w_s, sem)
    copy.start()
    x = x_ref[...].astype(F32)
    normed = (x * rms(x) * gain_ref[...]).astype(BF)
    na_ref[...] = normed
    copy.wait()
    cos, sin = cos_ref[...], sin_ref[...]
    for j in range(QKV_BLOCKS):
        out = dot(normed, columns(w_s, j * rows, 1, rows))
        if j < 5:
            turned = out * cos + half_of(out) * sin if j < 3 else out
            if j == 2:
                lane = lax.broadcasted_iota(jnp.int32, out.shape, 1)
                turned = jnp.where(lane < HD, turned, out)
            kv_ref[:, j * LANES : (j + 1) * LANES] = turned.astype(BF)
        else:
            turned = (out * cos + half_of(out) * sin).astype(BF) * BF(HD**-0.5)
            at = (j - 5) * LANES
            width = min(LANES, D - at)
            q_ref[:, at : at + width] = turned[:, :width]


def qkv_forward(x, gain, cos, sin, weights, base):
    count = x.shape[0]
    shards = weights.shape[0]
    rows = PADDED // shards
    return pl.pallas_call(
        functools.partial(qkv_kernel, base),
        out_shape=(
            jax.ShapeDtypeStruct((count, PADDED), BF),
            jax.ShapeDtypeStruct((count, D), BF),
            jax.ShapeDtypeStruct((count, KVW), BF),
        ),
        in_specs=[VMEM] * 4 + [ANY],
        out_specs=[VMEM] * 3,
        scratch_shapes=[pltpu.VMEM((shards, QKV_BLOCKS * rows, LANES), BF), pltpu.SemaphoreType.DMA],
        compiler_params=BIG,
        name="qkv_forward",
    )(x, gain, cos, sin, weights)


def weight_copies(w_hbm, w_s, sems, rows, ff_rows, first):
    steps = FF // CHUNK
    per = CHUNK // ff_rows
    blocks = CHUNK // LANES * rows
    gate = first + OUT_BLOCKS * rows
    up = gate + FF_BLOCKS * rows
    down = up + FF_BLOCKS * rows
    out = [pltpu.make_async_copy(w_hbm.at[:, pl.ds(first, OUT_BLOCKS * rows), :], w_s.at[:, pl.ds(0, OUT_BLOCKS * rows), :], sems.at[3 * steps])]
    chunks = []
    for j in range(steps):
        parts = []
        for at in (gate + j * blocks, up + j * blocks):
            parts.append((pl.ds(0, w_hbm.shape[0]), pl.ds(at, blocks), pl.ds(at - first, blocks)))
        parts.append((pl.ds(j * per, per), pl.ds(down, OUT_BLOCKS * ff_rows), pl.ds(down - first, OUT_BLOCKS * ff_rows)))
        chunks.append(
            [
                pltpu.make_async_copy(w_hbm.at[who, src, :], w_s.at[who, dst, :], sems.at[3 * j + i])
                for i, (who, src, dst) in enumerate(parts)
            ]
        )
    return out, chunks


def down_of(w_s, j, ff_rows, at):
    per = CHUNK // ff_rows
    parts = [
        w_s[j * per : (j + 1) * per, at + i * ff_rows : at + (i + 1) * ff_rows, :].reshape(CHUNK, LANES)
        for i in range(OUT_BLOCKS)
    ]
    return jnp.concatenate(parts, 1)


def ffn_kernel(first, o_ref, x_ref, na_ref, gain_ref, e_ref, w_hbm, acts_ref, m_ref, g_ref, u_ref, y_ref, w_s, acc, sems):
    step = pl.program_id(0)
    rows = PADDED // w_s.shape[0]
    ff_rows = FF // w_s.shape[0]
    out, chunks = weight_copies(w_hbm, w_s, sems, rows, ff_rows, first)
    gate = OUT_BLOCKS * rows
    up = gate + FF_BLOCKS * rows
    down = up + FF_BLOCKS * rows
    blocks = CHUNK // LANES

    @pl.when(step == 0)
    def _():
        out[0].start()
        for chunk in chunks:
            for copy in chunk:
                copy.start()
        padded = dot(o_ref[...], e_ref[...]).astype(BF)
        acts_ref[:, FF : FF + PADDED] = padded
        acts_ref[:, FF + 2 * PADDED :] = na_ref[...]
        out[0].wait()
        mixed = x_ref[...].astype(F32) + dot(padded, columns(w_s, 0, OUT_BLOCKS, rows))
        m_ref[...] = mixed
        acts_ref[:, FF + PADDED : FF + 2 * PADDED] = (mixed * rms(mixed) * gain_ref[...]).astype(BF)
        acc[...] = mixed

    for j in range(FF // CHUNK):

        @pl.when(step == j)
        def _():
            for copy in chunks[j]:
                copy.wait()
            normed = acts_ref[:, FF + PADDED : FF + 2 * PADDED]
            g = dot(normed, columns(w_s, gate + j * blocks * rows, blocks, rows))
            u = dot(normed, columns(w_s, up + j * blocks * rows, blocks, rows))
            hidden = (g * jax.nn.sigmoid(g) * u).astype(BF)
            g_ref[...] = g
            u_ref[...] = u
            acts_ref[:, j * CHUNK : (j + 1) * CHUNK] = hidden
            acc[...] += dot(hidden, down_of(w_s, j, ff_rows, down))

    @pl.when(step == FF // CHUNK - 1)
    def _():
        y_ref[...] = acc[...].astype(BF)


def ffn_forward(o, x, na, gain, e, weights, first):
    count = x.shape[0]
    shards = weights.shape[0]
    rows = PADDED // shards
    later = (OUT_BLOCKS + 2 * FF_BLOCKS) * rows + OUT_BLOCKS * (FF // shards)
    whole = lambda shape: pl.BlockSpec(shape, lambda j: (0, 0))
    chunk = pl.BlockSpec((count, CHUNK), lambda j: (0, j))
    wide = jax.ShapeDtypeStruct((count, FF), F32)
    return pl.pallas_call(
        functools.partial(ffn_kernel, first),
        grid=(FF // CHUNK,),
        out_shape=(
            jax.ShapeDtypeStruct((count, ACTS), BF),
            jax.ShapeDtypeStruct((count, PADDED), F32),
            wide,
            wide,
            jax.ShapeDtypeStruct((count, PADDED), BF),
        ),
        in_specs=[whole((count, D))] + [whole((count, PADDED))] * 2 + [whole((1, PADDED)), whole((D, PADDED)), ANY],
        out_specs=[whole((count, ACTS)), whole((count, PADDED)), chunk, chunk, whole((count, PADDED))],
        scratch_shapes=[
            pltpu.VMEM((shards, later, LANES), BF),
            pltpu.VMEM((count, PADDED), F32),
            pltpu.SemaphoreType.DMA((3 * (FF // CHUNK) + 1,)),
        ],
        compiler_params=BIG,
        name="ffn_forward",
    )(o, x, na, gain, e, weights)


def ffn_back_kernel(first, dy_ref, g_ref, u_ref, m_ref, gain_ref, e_ref, w_hbm, back_ref, dm_ref, do_ref, dgain_ref, w_s, acc, sems):
    step = pl.program_id(0)
    rows = PADDED // w_s.shape[0]
    ff_rows = FF // w_s.shape[0]
    out, chunks = weight_copies(w_hbm, w_s, sems, rows, ff_rows, first)
    gate = OUT_BLOCKS * rows
    up = gate + FF_BLOCKS * rows
    down = up + FF_BLOCKS * rows
    blocks = CHUNK // LANES

    @pl.when(step == 0)
    def _():
        for chunk in chunks:
            for copy in (chunk[2], chunk[0], chunk[1]):
                copy.start()
        out[0].start()
        acc[...] = jnp.zeros_like(acc)

    for j in range(FF // CHUNK):

        @pl.when(step == j)
        def _():
            chunks[j][2].wait()
            d_hidden = dot_nt(dy_ref[...], down_of(w_s, j, ff_rows, down))
            g = g_ref[...]
            sig = jax.nn.sigmoid(g)
            dg = (d_hidden * u_ref[...] * sig * (1.0 + g * (1.0 - sig))).astype(BF)
            du = (d_hidden * g * sig).astype(BF)
            back_ref[:, j * CHUNK : (j + 1) * CHUNK] = dg
            back_ref[:, FF + j * CHUNK : FF + (j + 1) * CHUNK] = du
            chunks[j][0].wait()
            chunks[j][1].wait()
            acc[...] += dot_nt(dg, columns(w_s, gate + j * blocks * rows, blocks, rows)) + dot_nt(
                du, columns(w_s, up + j * blocks * rows, blocks, rows)
            )

    @pl.when(step == FF // CHUNK - 1)
    def _():
        back, dgain = norm_back(acc[...], m_ref[...], gain_ref[...])
        dgain_ref[...] = dgain
        d_mixed = dy_ref[...].astype(F32) + back
        dm_ref[...] = d_mixed
        low = d_mixed.astype(BF)
        back_ref[:, 2 * FF : 2 * FF + PADDED] = low
        back_ref[:, 2 * FF + PADDED :] = dy_ref[...]
        out[0].wait()
        d_padded = dot_nt(low, columns(w_s, 0, OUT_BLOCKS, rows)).astype(BF)
        do_ref[...] = dot_nt(d_padded, e_ref[...]).astype(BF)


def ffn_backward(dy, g, u, mixed, gain, e, weights, first):
    count = dy.shape[0]
    shards = weights.shape[0]
    rows = PADDED // shards
    later = (OUT_BLOCKS + 2 * FF_BLOCKS) * rows + OUT_BLOCKS * (FF // shards)
    whole = lambda shape: pl.BlockSpec(shape, lambda j: (0, 0))
    chunk = pl.BlockSpec((count, CHUNK), lambda j: (0, j))
    full = whole((count, PADDED))
    return pl.pallas_call(
        functools.partial(ffn_back_kernel, first),
        grid=(FF // CHUNK,),
        out_shape=(
            jax.ShapeDtypeStruct((count, BACK), BF),
            jax.ShapeDtypeStruct((count, PADDED), F32),
            jax.ShapeDtypeStruct((count, D), BF),
            jax.ShapeDtypeStruct((1, PADDED), F32),
        ),
        in_specs=[full, chunk, chunk, full, whole((1, PADDED)), whole((D, PADDED)), ANY],
        out_specs=[whole((count, BACK)), full, whole((count, D)), whole((1, PADDED))],
        scratch_shapes=[
            pltpu.VMEM((shards, later, LANES), BF),
            pltpu.VMEM((count, PADDED), F32),
            pltpu.SemaphoreType.DMA((3 * (FF // CHUNK) + 1,)),
        ],
        compiler_params=BIG,
        name="ffn_backward",
    )(dy, g, u, mixed, gain, e, weights)


def qkv_back_kernel(base, zs, dq_ref, cos_ref, sin_ref, x_ref, gain_ref, dm_ref, *refs):
    shares, (w_hbm, dkv_ref, dx_ref, dgain_ref, w_s, sem) = refs[:zs], refs[zs:]
    rows = w_s.shape[1] // QKV_BLOCKS
    copy = pltpu.make_async_copy(w_hbm.at[:, pl.ds(base, w_s.shape[1]), :], w_s, sem)
    copy.start()
    cos, sin = cos_ref[...], sin_ref[...]
    for j in range(KVW // LANES):
        at = slice(j * LANES, (j + 1) * LANES)
        grad = shares[0][:, at].astype(F32)
        for share in shares[1:]:
            grad = grad + share[:, at].astype(F32)
        turned = grad * cos - half_of(grad * sin) if j < 3 else grad
        if j == 2:
            lane = lax.broadcasted_iota(jnp.int32, grad.shape, 1)
            turned = jnp.where(lane < HD, turned, grad)
        dkv_ref[:, at] = turned.astype(BF)
    copy.wait()
    kv_blocks = KVW // LANES
    d_normed = dot_nt(dkv_ref[...], columns(w_s, 0, kv_blocks, rows))
    d_normed = d_normed + dot_nt(dq_ref[...], columns(w_s, kv_blocks * rows, QKV_BLOCKS - kv_blocks, rows))
    back, dgain = norm_back(d_normed, x_ref[...].astype(F32), gain_ref[...])
    dgain_ref[...] = dgain
    dx_ref[...] = dm_ref[...] + back


def qkv_backward(dq, shares, cos, sin, x, gain, dm, weights, base):
    count = x.shape[0]
    shards = weights.shape[0]
    rows = PADDED // shards
    return pl.pallas_call(
        functools.partial(qkv_back_kernel, base, len(shares)),
        out_shape=(
            jax.ShapeDtypeStruct((count, KVW), BF),
            jax.ShapeDtypeStruct((count, PADDED), F32),
            jax.ShapeDtypeStruct((1, PADDED), F32),
        ),
        in_specs=[VMEM] * (6 + len(shares)) + [ANY],
        out_specs=[VMEM] * 3,
        scratch_shapes=[pltpu.VMEM((shards, QKV_BLOCKS * rows, LANES), BF), pltpu.SemaphoreType.DMA],
        compiler_params=BIG,
        name="qkv_backward",
    )(dq, cos, sin, x, gain, dm, *shares, weights)


def both_t(own, other, at, width):
    parts = [ref[:, at : at + width].astype(F32).T.astype(BF) for ref in (own, other)]
    return jnp.concatenate(parts, 1)


def own_rows(turned, core, rows):
    split = turned.reshape(-1, 2, rows, turned.shape[-1])
    return jnp.where(core == 0, split[:, 0], split[:, 1]).reshape(-1, turned.shape[-1])


def both(own, other, at, width):
    where = pl.ds(pl.multiple_of(at, LANES), width)
    return jnp.concatenate([own[:, where], other[:, where]], 0)


def write_split(out, keep_ref, send_ref, at, rows, half):
    for i in range(out.shape[1] // LANES):
        block = out[:, i * LANES : (i + 1) * LANES].reshape(2, -1, rows, LANES)
        place = slice(at + i * rows, at + (i + 1) * rows)
        keep_ref[:, place, :] = jnp.where(half == 0, block[0], block[1])
        send_ref[:, place, :] = jnp.where(half == 0, block[1], block[0])


def grad_ffn_kernel(place, own, other, back, back_other, keep_a, send_a, keep_u, send_u, keep_o, send_o, nft, opt, hdt):
    step = pl.program_id(0)
    core, half, section = place[0], place[1], place[2]
    chips = keep_a.shape[0]
    rows, ff_rows = PADDED // (2 * chips), FF // (2 * chips)
    steps = FF // CHUNK

    @pl.when(step == 0)
    def _():
        nft[...] = own_rows(both_t(own, other, FF + PADDED, PADDED), core, rows)

    @pl.when(step == steps)
    def _():
        hdt[...] = own_rows(both_t(own, other, 0, FF), core, ff_rows)

    @pl.when(step == 3 * steps)
    def _():
        opt[...] = own_rows(both_t(own, other, FF, PADDED), core, rows)

    def write_a(out, height, to):
        for i in range(out.shape[1] // LANES):
            to[:, i * height : (i + 1) * height, :] = out[:, i * LANES : (i + 1) * LANES].reshape(chips, height, LANES)

    @pl.when(step < steps)
    def _():
        out = dot(nft[...], both(back, back_other, step * CHUNK, CHUNK)).astype(BF)
        pl.when(section == 1)(lambda: write_a(out, rows, keep_a))
        pl.when(section == 0)(lambda: write_a(out, rows, send_a))

    @pl.when((step >= steps) & (step < 2 * steps))
    def _():
        width = PADDED // steps
        out = dot(hdt[...], both(back, back_other, 2 * FF + PADDED + (step - steps) * width, width)).astype(BF)
        pl.when(section == 0)(lambda: write_a(out, ff_rows, keep_a))
        pl.when(section == 1)(lambda: write_a(out, ff_rows, send_a))

    @pl.when((step >= 2 * steps) & (step < 3 * steps))
    def _():
        out = dot(nft[...], both(back, back_other, FF + (step - 2 * steps) * CHUNK, CHUNK)).astype(BF)
        write_split(out, keep_u, send_u, 0, rows, half)

    @pl.when(step == 3 * steps)
    def _():
        out = dot(opt[...], both(back, back_other, 2 * FF, PADDED)).astype(BF)
        write_split(out, keep_o, send_o, 0, rows, half)


def grad_ffn(place, own, other, back, back_other, shards):
    count = own.shape[0]
    chips = shards // 2
    rows, ff_rows = PADDED // shards, FF // shards
    steps = FF // CHUNK
    block = CHUNK // LANES * rows
    whole = lambda shape: pl.BlockSpec(shape, lambda j, place: (0,) * len(shape))
    early = lambda j: jnp.clip(j, 0, steps - 1)
    late = lambda j: jnp.clip(j - steps, 0, steps - 1)
    last = lambda j: jnp.clip(j - 2 * steps, 0, steps - 1)
    a_spec = lambda when: pl.BlockSpec((chips, block, LANES), lambda j, place: (0, jnp.where(place[2] == when, late(j), early(j)), 0))
    u_spec = pl.BlockSpec((chips // 2, block, LANES), lambda j, place: (0, last(j), 0))
    wide = lambda first, height: jax.ShapeDtypeStruct((first, height, LANES), BF)
    return pl.pallas_call(
        grad_ffn_kernel,
        grid_spec=pltpu.PrefetchScalarGridSpec(
            num_scalar_prefetch=1,
            grid=(3 * steps + 1,),
            in_specs=[whole((count, ACTS))] * 2 + [whole((count, BACK))] * 2,
            out_specs=[a_spec(0), a_spec(1), u_spec, u_spec] + [whole((chips // 2, OUT_BLOCKS * rows, LANES))] * 2,
            scratch_shapes=[
                pltpu.VMEM((PADDED // 2, 2 * count), BF),
                pltpu.VMEM((PADDED // 2, 2 * count), BF),
                pltpu.VMEM((FF // 2, 2 * count), BF),
            ],
        ),
        out_shape=[wide(chips, steps * block)] * 2 + [wide(chips // 2, steps * block)] * 2 + [wide(chips // 2, OUT_BLOCKS * rows)] * 2,
        compiler_params=BIG,
        name="grad_ffn",
    )(place, own, other, back, back_other)


def grad_attn_kernel(place, own, other, grad, grad_other, keep, send):
    core, half = place[0], place[1]
    blocks = grad.shape[1] // LANES
    rows = keep.shape[1] // blocks
    turned = own_rows(both_t(own, other, FF + 2 * PADDED, PADDED), core, rows)
    out = dot(turned, jnp.concatenate([grad[...], grad_other[...]], 0)).astype(BF)
    write_split(out, keep, send, 0, rows, half)


def grad_attn(place, own, other, grad, grad_other, shards):
    rows = PADDED // shards
    shape = jax.ShapeDtypeStruct((shards // 4, grad.shape[1] // LANES * rows, LANES), BF)
    return pl.pallas_call(
        grad_attn_kernel,
        out_shape=(shape, shape),
        in_specs=[SMEM] + [VMEM] * 4,
        out_specs=[VMEM] * 2,
        compiler_params=BIG,
        name="grad_attn",
    )(place, own, other, grad, grad_other)


def spread_matrix(shards):
    size, room = D // shards, PADDED // shards
    feature = lax.broadcasted_iota(jnp.int32, (D, PADDED), 0)
    place = lax.broadcasted_iota(jnp.int32, (D, PADDED), 1)
    return (feature // size * room + feature % size == place).astype(BF)


def to_blocks(matrix):
    rows, width = matrix.shape
    return matrix.reshape(rows, width // LANES, LANES).transpose(1, 0, 2).reshape(-1, LANES)


def from_blocks(blocks, rows):
    return blocks.reshape(-1, rows, LANES).transpose(1, 0, 2).reshape(rows, -1)


def plus(left, right):
    return (left.astype(F32) + right.astype(F32)).astype(BF)


def after(value, *earlier):
    return lax.optimization_barrier((value,) + earlier)[0]


def scatter_z(parts):
    return lax.psum_scatter(parts, "z", scatter_dimension=0, tiled=False)


def to_owner(part, layer):
    return lax.ppermute(part, "section", [(1 - layer, layer)])


def total_over(values):
    count = lax.axis_size("z")
    for axis in ("core", "dp"):
        values = values + swap(values, axis)
    step = 1
    while step < count:
        values = values + lax.ppermute(values, "z", [(i, i ^ step) for i in range(count)])
        step *= 2
    return values + swap(values, "section")


def per_device_blocks(tokens, cotangent, positions, attn_gain, w_query, w_key, w_value, w_out, ffn_gain, w_gate, w_up, w_down):
    section, half = lax.axis_index("section"), lax.axis_index("dp")
    z_index, core = lax.axis_index("z"), lax.axis_index("core")
    plane = ("dp", "z", "core")
    size, ff_rows = w_query.shape[1], w_down.shape[1]
    shards = D // size
    room = PADDED // shards
    chips = shards // 2
    qkv_rows = QKV_BLOCKS * room
    block_range = jnp.stack([2 - core, 2 * z_index + 2]).astype(jnp.int32)
    place = jnp.stack([core, half, section]).astype(jnp.int32)
    spread = spread_matrix(shards)

    def mine(array_in):
        return lax.dynamic_index_in_dim(array_in, section, 0, keepdims=False)

    def widen(array_in):
        return project(array_in, spread).astype(BF)

    def padded(array_in):
        return jnp.pad(array_in, ((0, room - size), (0, 0)))

    gains = jnp.concatenate([attn_gain, ffn_gain], 0).T
    qkv = jnp.concatenate([w_key[0], w_value[0], w_query[0], gains, jnp.zeros((size, HD - 2), BF)], -1)
    narrow = jnp.concatenate([qkv, widen(w_out[0]), w_gate[0], w_up[0]], -1)
    shard = jnp.concatenate([to_blocks(padded(narrow)), to_blocks(widen(w_down[0]))], 0)
    got = swap(shard, "section")
    shard0 = jnp.where(section == 0, shard, got)
    shard1 = jnp.where(section == 0, got, shard)

    early = lax.all_gather(jnp.concatenate([shard0, shard1[:qkv_rows]], 0), plane, axis=0)
    late = lax.all_gather(after(shard1[qkv_rows:], early), plane, axis=0)
    base1 = shard0.shape[0]

    def gains_at(base):
        at = base + (QKV_BLOCKS - 1) * room
        gain = early[:, at : at + room, HD : HD + 2].reshape(-1, 2).T.astype(F32)
        return gain[:1], gain[1:]

    w0 = (early, 0, early, qkv_rows) + gains_at(0)
    w1 = (early, base1, late, 0) + gains_at(base1)
    angle_cos, angle_sin = rope_tables(mine(positions))
    cos = jnp.concatenate([angle_cos[:, 0]] * 2, -1)
    sin = jnp.concatenate([angle_sin[:, 0]] * 2, -1)

    def forward(x, layer):
        w_a, at_a, w_f, at_f, gain_a, gain_f = layer
        na, q, kv = qkv_forward(x, gain_a, cos, sin, w_a, at_a)
        kv_all = spread_kv(kv)
        o, lse = attend(block_range, q, kv_all)
        acts, mixed, g, u, y = ffn_forward(o, x, na, gain_f, spread, w_f, at_f)
        return y, (x, q, kv_all, o, lse, acts, mixed, g, u)

    y0, saved0 = forward(widen(mine(tokens)), w0)
    y1, saved1 = forward(y0, w1)

    def backward_ffn(dy, layer, saved):
        w_a, at_a, w_f, at_f, gain_a, gain_f = layer
        x, q, kv_all, o, lse, acts, mixed, g, u = saved
        return ffn_backward(dy, g, u, mixed, gain_f, spread, w_f, at_f)

    def backward_attn(do, saved):
        x, q, kv_all, o, lse, acts, mixed, g, u = saved
        return attend_back(block_range, q, o, do, lse, cos, sin, kv_all)

    def backward_qkv(dq, shares, dm, layer, saved):
        w_a, at_a, w_f, at_f, gain_a, gain_f = layer
        return qkv_backward(dq, shares, cos, sin, saved[0], gain_a, dm, w_a, at_a)

    def halve(total):
        split = total.reshape((2, chips // 2) + total.shape[1:])
        return lax.dynamic_index_in_dim(split, half, 0, False), lax.dynamic_index_in_dim(split, 1 - half, 0, False)

    acts1, acts0 = saved1[5], saved0[5]
    other1, other0 = swap(acts1, "core"), swap(acts0, "core")
    back1, dm1, do1, dgf1 = backward_ffn(widen(mine(cotangent)), w1, saved1)
    back_other1 = swap(back1, "core")
    dq1, dkv1 = backward_attn(do1, saved1)
    shares1 = collect_kv(dkv1)
    dq_other1 = swap(dq1, "core")
    keep_a1, send_a1, keep_u1, send_u1, keep_o1, send_o1 = grad_ffn(place, acts1, other1, back1, back_other1, shards)
    keep_q1, send_q1 = grad_attn(place, acts1, other1, dq1, dq_other1, shards)
    got_a1, got_u1 = swap(send_a1, "section"), swap(send_u1, "dp")
    got_o1, got_q1 = swap(send_o1, "dp"), swap(send_q1, "dp")
    dkv_low1, dx1, dga1 = backward_qkv(dq1, shares1, dm1, w1, saved1)
    dkv_other1 = swap(dkv_low1, "core")
    dx1_low = dx1.astype(BF)
    back0, dm0, do0, dgf0 = backward_ffn(dx1_low, w0, saved0)
    back_other0 = swap(back0, "core")
    keep_k1, send_k1 = grad_attn(place, acts1, other1, dkv_low1, dkv_other1, shards)
    got_k1 = swap(send_k1, "dp")
    do0 = after(do0, got_a1, got_u1, got_o1, got_q1)
    keep_a1, send_a1 = halve(plus(keep_a1, got_a1))
    got_a1 = swap(send_a1, "dp")
    part_u1 = scatter_z(plus(keep_u1, got_u1))
    dq0, dkv0 = backward_attn(do0, saved0)
    shares0 = collect_kv(dkv0)
    dq_other0 = swap(dq0, "core")
    keep_a0, send_a0, keep_u0, send_u0, keep_o0, send_o0 = grad_ffn(place, acts0, other0, back0, back_other0, shards)
    keep_q0, send_q0 = grad_attn(place, acts0, other0, dq0, dq_other0, shards)
    got_a0, got_u0 = swap(send_a0, "section"), swap(send_u0, "dp")
    got_o0, got_q0 = swap(send_o0, "dp"), swap(send_q0, "dp")
    part_a1 = scatter_z(plus(keep_a1, got_a1))
    oqk = lambda keeps, gots: jnp.concatenate([plus(keep, got) for keep, got in zip(keeps, gots)], 1)
    part_s1 = scatter_z(oqk((keep_o1, keep_q1, keep_k1), (got_o1, got_q1, got_k1)))
    dkv_low0, dx0, dga0 = backward_qkv(dq0, shares0, dm0, w0, saved0)
    dkv_other0 = swap(dkv_low0, "core")
    keep_k0, send_k0 = grad_attn(place, acts0, other0, dkv_low0, dkv_other0, shards)
    got_k0 = swap(send_k0, "dp")
    keep_a0, send_a0 = halve(plus(keep_a0, got_a0))
    got_a0 = swap(send_a0, "dp")
    part_u0 = scatter_z(plus(keep_u0, got_u0))
    part_a0 = scatter_z(plus(keep_a0, got_a0))
    part_s0 = scatter_z(oqk((keep_o0, keep_q0, keep_k0), (got_o0, got_q0, got_k0)))

    def whole(part_u, part_s, part_a, layer):
        u = part_u.astype(F32) + to_owner(part_u, layer).astype(F32)
        s = part_s.astype(F32) + to_owner(part_s, layer).astype(F32)
        away = to_owner(part_a, layer)
        down, gate = (part_a, away) if layer == 0 else (away, part_a)
        return u, s, gate.astype(F32), down.astype(F32)

    sums = zip(whole(part_u0, part_s0, part_a0, 0), whole(part_u1, part_s1, part_a1, 1))
    up, small, gate, down = (jnp.where(section == 0, own0, own1) for own0, own1 in sums)

    def narrow_low(array_in):
        return project_t(array_in, spread).astype(BF)

    def narrow_wide(array_in):
        return array_in.reshape(array_in.shape[0], shards, room)[:, :, :size].reshape(array_in.shape[0], D)

    def pair(own, got):
        return jnp.where(section == 0, jnp.stack([own, got]), jnp.stack([got, own]))

    got = swap(narrow_low(jnp.where(section == 0, y1, y0)), "section")
    section_out = pair(narrow_low(jnp.where(section == 0, y0, y1)), got)
    got = swap(narrow_low(jnp.where(section == 0, dx1_low, dx0.astype(BF))), "section").astype(F32)
    input_grad = pair(narrow_wide(jnp.where(section == 0, dx0, dx1_low.astype(F32))), got)
    up = from_blocks(up, room)[:size]
    gate = from_blocks(gate, room)[:size]
    small = from_blocks(small, room)[:size]
    down = narrow_wide(from_blocks(down, ff_rows))
    kd = KV * HD
    gain_grads = total_over(jnp.concatenate([dga0, dgf0, dga1, dgf1], 0)).reshape(2, 2, PADDED)
    gain = lax.dynamic_slice_in_dim(mine(gain_grads), lax.axis_index(plane) * room, room, 1)[:, :size]
    outs = (
        section_out,
        input_grad,
        gain[0],
        small[:, PADDED : PADDED + D],
        small[:, 2 * PADDED : 2 * PADDED + kd],
        small[:, 2 * PADDED + kd :],
        narrow_wide(small[:, :PADDED]),
        gain[1],
        gate,
        up,
        down,
    )
    return tuple(part[None] for part in outs)


def solution(mesh):
    sizes = mesh.devices.shape
    grid = Mesh(mesh.devices.reshape(sizes[0], sizes[1], sizes[2] // 2, 2), ("section", "dp", "z", "core"))
    ctx = ("z", "core")
    plane = ("dp", "z", "core")
    vector = P("section", plane)
    matrix = P("section", plane, None)
    in_specs = (
        P("dp", ctx, None),
        P("dp", ctx, None),
        P("dp", ctx),
        vector,
        matrix,
        matrix,
        matrix,
        matrix,
        vector,
        matrix,
        matrix,
        matrix,
    )
    acts = P("section", "dp", ctx, None)
    out_specs = (acts, acts, vector, matrix, matrix, matrix, matrix, vector, matrix, matrix, matrix)
    shards = sizes[1] * sizes[2]
    aligned = shards == 16
    return jax.shard_map(per_device_blocks if aligned else per_device, mesh=grid, in_specs=in_specs, out_specs=out_specs, check_vma=False)
```

```python
import functools

import jax
import jax.numpy as jnp
from jax import lax
from jax.experimental import pallas as pl
from jax.experimental.pallas import tpu as pltpu
from jax.sharding import Mesh
from jax.sharding import PartitionSpec as P

D = 960
H = 15
KV = 5
G = H // KV
HD = 64
FF = 2560
EPS = 1e-05
F32 = jnp.float32
BF = jnp.bfloat16


def dot(a,b): return jnp.dot(a,b,preferred_element_type=F32)

def fwd_kernel(rng, q_ref, kv_ref, o_ref, lse_ref, qt, vt, m_s, l_s, acc):
    T=q_ref.shape[0]; W=G*T
    qt[...]=q_ref[...].astype(F32).T.astype(BF)
    nb=kv_ref.shape[0]
    def step(b, first):
        vt[...]=kv_ref[b,:,KV*HD:].astype(F32).T.astype(BF)
        for g in range(KV):
            qg=jnp.concatenate([qt[(g*G+j)*HD:(g*G+j+1)*HD,:] for j in range(G)],1)
            s=dot(kv_ref[b,:,g*HD:(g+1)*HD],qg)
            if first:
                key=lax.broadcasted_iota(jnp.int32,(T,W),0)
                qry=lax.broadcasted_iota(jnp.int32,(T,W),1)%T
                s=jnp.where(key<=qry,s,-1e30)
                m=jnp.max(s,0,keepdims=True)
                p=jnp.exp(s-m)
                l_s[g:g+1,:]=jnp.sum(p,0,keepdims=True)
                acc[g*HD:(g+1)*HD,:]=dot(vt[g*HD:(g+1)*HD,:],p.astype(BF))
            else:
                mo=m_s[g:g+1,:]
                m=jnp.maximum(mo,jnp.max(s,0,keepdims=True))
                p=jnp.exp(s-m); al=jnp.exp(mo-m)
                l_s[g:g+1,:]=l_s[g:g+1,:]*al+jnp.sum(p,0,keepdims=True)
                acc[g*HD:(g+1)*HD,:]=acc[g*HD:(g+1)*HD,:]*al+dot(vt[g*HD:(g+1)*HD,:],p.astype(BF))
            m_s[g:g+1,:]=m
    step(0,True)
    def body(b,_):
        step(b,False); return 0
    lax.fori_loop(rng[0],rng[1],body,0)
    for g in range(KV):
        inv=1.0/l_s[g:g+1,:]
        lse_ref[g:g+1,:]=m_s[g:g+1,:]+jnp.log(l_s[g:g+1,:])
        og=acc[g*HD:(g+1)*HD,:]*inv
        for j in range(G):
            h=g*G+j
            o_ref[:,h*HD:(h+1)*HD]=og[:,j*T:(j+1)*T].T.astype(BF)

def attn_fwd(rng,q,kv):
    T=q.shape[0]; W=G*T
    return pl.pallas_call(fwd_kernel,
      out_shape=(jax.ShapeDtypeStruct((T,H*HD),BF),jax.ShapeDtypeStruct((KV,W),F32)),
      in_specs=[pl.BlockSpec(memory_space=pltpu.SMEM)]+[pl.BlockSpec(memory_space=pltpu.VMEM)]*2,
      out_specs=[pl.BlockSpec(memory_space=pltpu.VMEM)]*2,
      scratch_shapes=[pltpu.VMEM((H*HD,T),BF),pltpu.VMEM((KV*HD,T),BF),pltpu.VMEM((KV,W),F32),pltpu.VMEM((KV,W),F32),pltpu.VMEM((KV*HD,W),F32)],
      compiler_params=pltpu.CompilerParams(vmem_limit_bytes=48<<20),
    )(rng,q,kv)

def bwd_kernel(rng, q_ref, kv_ref, o_ref, do_ref, lse_ref, dq_ref, dkv_ref, qt, dot_, qn, don, kt, dl, dqa):
    T=q_ref.shape[0]; W=G*T
    nb=kv_ref.shape[0]
    qt[...]=q_ref[...].astype(F32).T.astype(BF)
    doT=do_ref[...].astype(F32).T
    dot_[...]=doT.astype(BF)
    oT=o_ref[...].astype(F32).T
    prod=doT*oT
    for h in range(H):
        g,j=divmod(h,G)
        dl[g:g+1,j*T:(j+1)*T]=jnp.sum(prod[h*HD:(h+1)*HD,:],0,keepdims=True)
        qn[g,j*T:(j+1)*T,:]=q_ref[:,h*HD:(h+1)*HD]
        don[g,j*T:(j+1)*T,:]=do_ref[:,h*HD:(h+1)*HD]
    def step(b, first):
        kt[...]=kv_ref[b,:,:KV*HD].astype(F32).T.astype(BF)
        for g in range(KV):
            qg=jnp.concatenate([qt[(g*G+j)*HD:(g*G+j+1)*HD,:] for j in range(G)],1)
            dg=jnp.concatenate([dot_[(g*G+j)*HD:(g*G+j+1)*HD,:] for j in range(G)],1)
            s=dot(kv_ref[b,:,g*HD:(g+1)*HD],qg)
            p=jnp.exp(s-lse_ref[g:g+1,:])
            if first:
                key=lax.broadcasted_iota(jnp.int32,(T,W),0)
                qry=lax.broadcasted_iota(jnp.int32,(T,W),1)%T
                p=jnp.where(key<=qry,p,0.0)
            dp=dot(kv_ref[b,:,(KV+g)*HD:(KV+g+1)*HD],dg)
            dz=(p*(dp-dl[g:g+1,:])).astype(BF)
            dkv_ref[b,:,(KV+g)*HD:(KV+g+1)*HD]=dot(p.astype(BF),don[g]).astype(BF)
            dkv_ref[b,:,g*HD:(g+1)*HD]=dot(dz,qn[g]).astype(BF)
            dq=dot(kt[g*HD:(g+1)*HD,:],dz)
            if first: dqa[g*HD:(g+1)*HD,:]=dq
            else: dqa[g*HD:(g+1)*HD,:]+=dq
    step(0,True)
    def body(b,_):
        step(b,False); return 0
    lax.fori_loop(rng[0],rng[1],body,0)
    def zero(b,_):
        dkv_ref[b]=jnp.zeros((T,2*KV*HD),BF); return 0
    lax.fori_loop(1,rng[0],zero,0)
    lax.fori_loop(rng[1],nb,zero,0)
    for g in range(KV):
        for j in range(G):
            h=g*G+j
            dq_ref[:,h*HD:(h+1)*HD]=(dqa[g*HD:(g+1)*HD,j*T:(j+1)*T]*HD**-0.5).T

def attn_bwd(rng,q,kv,o,do,lse):
    T=q.shape[0]; W=G*T
    return pl.pallas_call(bwd_kernel,
      out_shape=(jax.ShapeDtypeStruct((T,H*HD),F32),jax.ShapeDtypeStruct(kv.shape,BF)),
      in_specs=[pl.BlockSpec(memory_space=pltpu.SMEM)]+[pl.BlockSpec(memory_space=pltpu.VMEM)]*5,
      out_specs=[pl.BlockSpec(memory_space=pltpu.VMEM)]*2,
      scratch_shapes=[pltpu.VMEM((H*HD,T),BF),pltpu.VMEM((H*HD,T),BF),pltpu.VMEM((KV,W,HD),BF),pltpu.VMEM((KV,W,HD),BF),
        pltpu.VMEM((KV*HD,T),BF),pltpu.VMEM((KV,W),F32),pltpu.VMEM((KV*HD,W),F32)],
      compiler_params=pltpu.CompilerParams(vmem_limit_bytes=48<<20),
    )(rng,q,kv,o,do,lse)


def rotate_half(vector):
    half_dim = vector.shape[-1] // 2
    return jnp.concatenate([-vector[..., half_dim:], vector[..., :half_dim]], -1)


def rope_tables(seq_pos):
    half_dim = HD // 2
    inv_freq = 10000.0 ** (-(jnp.arange(half_dim, dtype=F32) * 2.0) / HD)
    angles = seq_pos.astype(F32)[..., None] * inv_freq
    angle_pair = jnp.concatenate([angles, angles], -1)[..., None, :]
    return (jnp.cos(angle_pair), jnp.sin(angle_pair))


def norm_forward(values_in, gain_vec):
    factor = lax.rsqrt(jnp.mean(values_in * values_in, -1, keepdims=True) + EPS)
    return (values_in * factor * gain_vec, factor)


def norm_backward(grad_in, values_in, factor, gain_vec):
    scaled = grad_in * gain_vec
    grad_back = factor * scaled - values_in * factor * factor * factor * jnp.mean(
        scaled * values_in, -1, keepdims=True
    )
    return (grad_back, jnp.sum(grad_in * values_in * factor, 0))


def swap(block, axis):
    return lax.ppermute(block, axis, [(0, 1), (1, 0)])


def move_z(block, distance):
    count = lax.axis_size("z")
    route = [(i, i + distance) for i in range(count) if 0 <= i + distance < count]
    return lax.ppermute(block, "z", route)


def gather_kv(block):
    count = lax.axis_size("z")
    own = [block] + [move_z(block, d) for d in range(1, count)]
    own = jnp.stack(own)
    other = swap(own, "core")
    return jnp.stack([own, other], 1).reshape((2 * count,) + block.shape)


def reduce_kv(blocks):
    count = lax.axis_size("z")
    blocks = blocks.reshape((count, 2) + blocks.shape[1:])
    mine = blocks[:, 0].astype(F32) + swap(blocks[:, 1], "core").astype(F32)
    total = mine[0]
    for d in range(1, count):
        total = total + move_z(mine[d].astype(BF), -d).astype(F32)
    return total


def project(left, right):
    return jnp.dot(left, right, preferred_element_type=F32)


def project_t(left, right):
    return lax.dot_general(left, right, (((1,), (1,)), ((), ())), preferred_element_type=F32)


def outer(left, right):
    return lax.dot_general(left, right, (((0,), (0,)), ((), ())), preferred_element_type=F32)


def rope(values, cosine, sine):
    count = values.shape[0]
    values = values.reshape(count, -1, HD)
    return (values * cosine + rotate_half(values) * sine).reshape(count, -1)


def rope_t(values, cosine, sine):
    count = values.shape[0]
    values = values.reshape(count, -1, HD)
    return (values * cosine - rotate_half(values * sine)).reshape(count, -1)


def layer_forward(rows, tables, weights, block_range):
    gain_a, w_qkv, w_o, gain_f, w_g, w_u, w_d = weights
    cosine, sine = tables
    normed_a, factor_a = norm_forward(rows, gain_a)
    normed_a = normed_a.astype(BF)
    qkv = project(normed_a, w_qkv)
    queries = (rope(qkv[:, :D], cosine, sine)).astype(BF) * BF(HD**-0.5)
    keys = rope(qkv[:, D : D + KV * HD], cosine, sine).astype(BF)
    values = qkv[:, D + KV * HD :].astype(BF)
    kv_all = gather_kv(jnp.concatenate([keys, values], -1))
    attended, log_total = attn_fwd(block_range, queries, kv_all)
    mixed = rows + project(attended, w_o)
    normed_f, factor_f = norm_forward(mixed, gain_f)
    normed_f = normed_f.astype(BF)
    gate_act = project(normed_f, w_g)
    up_proj = project(normed_f, w_u)
    hidden = (jax.nn.silu(gate_act) * up_proj).astype(BF)
    out = (mixed + project(hidden, w_d)).astype(BF)
    saved = (rows, factor_a, normed_a, queries, kv_all, log_total, attended, mixed, factor_f, normed_f, gate_act, up_proj, hidden)
    return out, saved


def layer_backward(grad_low, saved, tables, weights, block_range):
    gain_a, w_qkv, w_o, gain_f, w_g, w_u, w_d = weights
    cosine, sine = tables
    rows, factor_a, normed_a, queries, kv_all, log_total, attended, mixed, factor_f, normed_f, gate_act, up_proj, hidden = saved
    d_hidden = project_t(grad_low, w_d)
    sig = jax.nn.sigmoid(gate_act)
    d_gate = (d_hidden * up_proj * sig * (1.0 + gate_act * (1.0 - sig))).astype(BF)
    d_up = (d_hidden * gate_act * sig).astype(BF)
    d_normed_f = project_t(d_gate, w_g) + project_t(d_up, w_u)
    d_norm, d_gain_f = norm_backward(d_normed_f, mixed, factor_f, gain_f)
    d_mixed = grad_low.astype(F32) + d_norm
    mix_low = d_mixed.astype(BF)
    d_attended = project_t(mix_low, w_o).astype(BF)
    d_query, d_kv = attn_bwd(block_range, queries, kv_all, attended, d_attended, log_total)
    d_kv = reduce_kv(d_kv)
    d_query = rope_t(d_query, cosine, sine).astype(BF)
    d_key = rope_t(d_kv[:, : KV * HD], cosine, sine).astype(BF)
    d_value = d_kv[:, KV * HD :].astype(BF)
    d_qkv = jnp.concatenate([d_query, d_key, d_value], -1)
    d_normed_a = project_t(d_qkv, w_qkv)
    d_norm_a, d_gain_a = norm_backward(d_normed_a, rows, factor_a, gain_a)
    d_rows = d_mixed + d_norm_a
    grads = dict(
        gate=outer(normed_f, d_gate).astype(BF),
        up=outer(normed_f, d_up).astype(BF),
        down=outer(hidden, grad_low).astype(BF),
        out=outer(attended, mix_low).astype(BF),
        qkv=outer(normed_a, d_qkv).astype(BF),
        gains=jnp.stack([d_gain_a, d_gain_f]),
    )
    return d_rows, grads


def per_device(tokens, cotangent, positions, attn_gain, w_query, w_key, w_value, w_out, ffn_gain, w_gate, w_up, w_down):
    section = lax.axis_index("section")
    z_index, core = lax.axis_index("z"), lax.axis_index("core")
    plane = ("dp", "z", "core")
    group = tokens.shape[0]
    local = tokens.shape[1]
    block_range = jnp.stack([2 - core, 2 * z_index + 2]).astype(jnp.int32)

    def mine(array_in):
        return lax.dynamic_index_in_dim(array_in, section, 0, keepdims=False)

    rows = tokens.shape[1]
    shard_rows = w_query.shape[1]
    ff_rows = w_down.shape[1]
    half = ff_rows // 2
    qkvo = jnp.concatenate([w_query[0], w_key[0], w_value[0], w_out[0]], -1)
    down = jnp.concatenate([w_down[0, :half], jnp.zeros((half, 64), BF), w_down[0, half:], jnp.zeros((half, 576), BF)], -1)
    gains = jnp.concatenate([attn_gain, ffn_gain], -1)
    shard = jnp.concatenate([qkvo, w_gate[0], w_up[0], down], 0)
    shard = lax.dynamic_update_slice(shard, gains, (3 * shard_rows, 2048))
    other = swap(shard, "section")

    def assemble(block):
        whole = lax.all_gather(block, plane, axis=0)
        n = shard_rows

        def piece(lo, hi):
            return whole[:, lo : lo + n, :hi].reshape(-1, hi) if hi <= FF else None

        attn = whole[:, :n, :].reshape(n * whole.shape[0], FF)
        w_g = whole[:, n : 2 * n, :].reshape(-1, FF)
        w_u = whole[:, 2 * n : 3 * n, :].reshape(-1, FF)
        w_d = jnp.concatenate([whole[:, 3 * n :, :D], whole[:, 3 * n :, 1024 : 1024 + D]], 1).reshape(-1, D)
        gain_rows = whole[:, 3 * n, 2048 : 2048 + 2 * n].astype(F32)
        gain_a = gain_rows[:, :n].reshape(-1)
        gain_f = gain_rows[:, n:].reshape(-1)
        return gain_a, attn[:, : D + 2 * KV * HD], attn[:, D + 2 * KV * HD :], gain_f, w_g, w_u, w_d

    w0 = assemble(jnp.where(section == 0, shard, other))
    w1 = assemble(jnp.where(section == 1, shard, other))
    tables = rope_tables(mine(positions))
    out0, saved0 = layer_forward(mine(tokens).astype(F32), tables, w0, block_range)
    out1, saved1 = layer_forward(out0.astype(F32), tables, w1, block_range)
    d1, g1 = layer_backward(mine(cotangent), saved1, tables, w1, block_range)
    d1_low = d1.astype(BF)
    d0, g0 = layer_backward(d1_low, saved0, tables, w0, block_range)

    def pair(own, got):
        return jnp.where(section == 0, jnp.stack([own, got]), jnp.stack([got, own]))

    got = swap(jnp.where(section == 0, out1, out0), "section")
    section_out = pair(jnp.where(section == 0, out0, out1), got)
    got = swap(jnp.where(section == 0, d1_low, d0.astype(BF)), "section").astype(F32)
    input_grad = pair(jnp.where(section == 0, d0, d1_low.astype(F32)), got)

    def reduce(first, second):
        def scatter(part):
            return lax.psum_scatter(part, plane, scatter_dimension=0, tiled=True)

        s0, s1 = scatter(first), scatter(second)
        got = swap(jnp.where(section == 0, s1, s0), "section")
        return jnp.where(section == 0, s0, s1).astype(F32) + got.astype(F32)

    grads = {name: reduce(g0[name], g1[name]) for name in ("gate", "up", "down", "out", "qkv")}
    gain_grad = reduce(g0["gains"].T, g1["gains"].T)
    qkv = grads["qkv"]
    kd = KV * HD
    outs = (
        section_out,
        input_grad,
        gain_grad[:, 0],
        qkv[:, :D],
        qkv[:, D : D + kd],
        qkv[:, D + kd :],
        grads["out"],
        gain_grad[:, 1],
        grads["gate"],
        grads["up"],
        grads["down"],
    )
    return tuple(part[None] for part in outs)


LANES = 128
PADDED = 1024
CHUNK = 640
WIDE = 512
KVW = 2 * KV * HD
QKV_BLOCKS = 13
EXTRA = 16
ACTS = FF + 3 * PADDED
BACK = 2 * FF + 2 * PADDED
OUT_BLOCKS = PADDED // LANES
FF_BLOCKS = FF // LANES
VMEM = pl.BlockSpec(memory_space=pltpu.VMEM)
ANY = pl.BlockSpec(memory_space=pl.ANY)
SMEM = pl.BlockSpec(memory_space=pltpu.SMEM)
BIG = pltpu.CompilerParams(vmem_limit_bytes=56 << 20)


def cost(microseconds):
    return pl.CostEstimate(flops=int(microseconds * 1.15e9), bytes_accessed=int(microseconds * 3.69e6), transcendentals=0)


def dot_nt(left, right):
    return lax.dot_general(left, right, (((1,), (1,)), ((), ())), preferred_element_type=F32)


def columns(ref, first, count, rows):
    parts = [
        ref[:, first + i * rows : first + (i + 1) * rows, :].reshape(-1, LANES) for i in range(count)
    ]
    return parts[0] if count == 1 else jnp.concatenate(parts, 1)


def half_of(values):
    lane = lax.broadcasted_iota(jnp.int32, values.shape, 1)
    back = pltpu.roll(values, LANES - HD // 2, 1)
    ahead = pltpu.roll(values, HD // 2, 1)
    return jnp.where(lane % HD < HD // 2, -back, ahead)


def rms(values):
    return lax.rsqrt(jnp.sum(values * values, -1, keepdims=True) / D + EPS)


def norm_back(grad, values, gain):
    factor = rms(values)
    scaled = grad * gain
    mean = jnp.sum(scaled * values, -1, keepdims=True) / D
    back = factor * scaled - values * (factor * factor * factor * mean)
    return back, jnp.sum(grad * values * factor, 0, keepdims=True)


def load_kv(blocks, other, kv_s, sems):
    copies = [pltpu.make_async_copy(block, kv_s.at[0, d], sems.at[d]) for d, block in enumerate(blocks)]
    copies.append(pltpu.make_async_copy(other, kv_s.at[1], sems.at[len(blocks)]))
    for copy in copies:
        copy.start()
    return copies


def attend_kernel(zs, rng, q_ref, *refs):
    blocks, (other, e_hbm, o_ref, op_ref, lse_ref, kv_s, qt, vt, m_s, l_s, acc, e_s, sems) = refs[:zs], refs[zs:]
    T = q_ref.shape[0]
    W = G * T
    copies = load_kv(blocks, other, kv_s, sems)
    spread = pltpu.make_async_copy(e_hbm, e_s, sems.at[zs + 1])
    spread.start()
    qt[...] = q_ref[...].astype(F32).T.astype(BF)
    for copy in copies:
        copy.wait()

    def step(b, first):
        kv = kv_s.at[lax.rem(b, 2), lax.div(b, 2)] if not first else kv_s.at[0, 0]
        vt[...] = kv[:, KV * HD :].astype(F32).T.astype(BF)
        ats = [slice(g * HD, (g + 1) * HD) for g in range(KV)]
        scores = []
        for g in range(KV):
            qg = jnp.concatenate([qt[(g * G + j) * HD : (g * G + j + 1) * HD, :] for j in range(G)], 1)
            s = dot(kv[:, ats[g]], qg)
            if first:
                key = lax.broadcasted_iota(jnp.int32, (T, W), 0)
                query = lax.broadcasted_iota(jnp.int32, (T, W), 1) % T
                s = jnp.where(key <= query, s, -1e30)
            scores.append(s)
        probs, scales = [], []
        for g in range(KV):
            top = jnp.max(scores[g], 0, keepdims=True)
            if not first:
                old = m_s[g : g + 1, :]
                top = jnp.maximum(old, top)
                scales.append(jnp.exp(old - top))
            p = jnp.exp(scores[g] - top)
            total = jnp.sum(p, 0, keepdims=True)
            l_s[g : g + 1, :] = total if first else l_s[g : g + 1, :] * scales[g] + total
            m_s[g : g + 1, :] = top
            probs.append(p.astype(BF))
        for g in range(KV):
            out = dot(vt[ats[g], :], probs[g])
            acc[ats[g], :] = out if first else acc[ats[g], :] * scales[g] + out

    step(0, True)

    def body(b, _):
        step(b, False)
        return 0

    lax.fori_loop(rng[0], rng[1], body, 0)
    for g in range(KV):
        lse_ref[g : g + 1, :] = m_s[g : g + 1, :] + jnp.log(l_s[g : g + 1, :])
        og = acc[g * HD : (g + 1) * HD, :] / l_s[g : g + 1, :]
        for j in range(G):
            h = g * G + j
            o_ref[:, h * HD : (h + 1) * HD] = og[:, j * T : (j + 1) * T].T.astype(BF)
    spread.wait()
    op_ref[...] = dot(o_ref[...], e_s[...]).astype(BF)


def attend(rng, q, kv_all, e):
    blocks, other = kv_all
    T, zs = q.shape[0], len(blocks)
    W = G * T
    return pl.pallas_call(
        functools.partial(attend_kernel, zs),
        out_shape=(
            jax.ShapeDtypeStruct((T, D), BF),
            jax.ShapeDtypeStruct((T, PADDED), BF),
            jax.ShapeDtypeStruct((KV, W), F32),
        ),
        in_specs=[SMEM, VMEM] + [ANY] * (zs + 2),
        out_specs=[VMEM] * 3,
        scratch_shapes=[
            pltpu.VMEM((2, zs, T, KVW), BF),
            pltpu.VMEM((D, T), BF),
            pltpu.VMEM((KV * HD, T), BF),
            pltpu.VMEM((KV, W), F32),
            pltpu.VMEM((KV, W), F32),
            pltpu.VMEM((KV * HD, W), F32),
            pltpu.VMEM((D, PADDED), BF),
            pltpu.SemaphoreType.DMA((zs + 2,)),
        ],
        compiler_params=BIG,
        cost_estimate=cost(24),
        name="attend",
    )(rng, q, *blocks, other, e)


def attend_back_kernel(zs, rng, q_ref, o_ref, do_ref, lse_ref, cos_ref, sin_ref, *refs):
    blocks, (other, dq_ref, own_ref, send_ref, kv_s, qt, dot_, qn, don, kt, dl, dqa, sems, dkv_ref, out_sems) = (
        refs[:zs],
        refs[zs:],
    )
    T = q_ref.shape[0]
    W = G * T
    copies = load_kv(blocks, other, kv_s, sems)
    qt[...] = q_ref[...].astype(F32).T.astype(BF)
    do_t = do_ref[...].astype(F32).T
    dot_[...] = do_t.astype(BF)
    prod = do_t * o_ref[...].astype(F32).T
    for h in range(H):
        g, j = divmod(h, G)
        rows = slice(j * T, (j + 1) * T)
        dl[g : g + 1, rows] = jnp.sum(prod[h * HD : (h + 1) * HD, :], 0, keepdims=True)
        qn[g, rows, :] = q_ref[:, h * HD : (h + 1) * HD]
        don[g, rows, :] = do_ref[:, h * HD : (h + 1) * HD]
    for copy in copies:
        copy.wait()

    def step(b, first):
        side, far = (0, 0) if first else (lax.rem(b, 2), lax.div(b, 2))
        kv = kv_s.at[side, far]
        out = dkv_ref.at[side, far]
        kt[...] = kv[:, : KV * HD].astype(F32).T.astype(BF)
        for g in range(KV):
            at = slice(g * HD, (g + 1) * HD)
            vat = slice((KV + g) * HD, (KV + g + 1) * HD)
            heads = [slice((g * G + j) * HD, (g * G + j + 1) * HD) for j in range(G)]
            s = dot(kv[:, at], jnp.concatenate([qt[h, :] for h in heads], 1))
            p = jnp.exp(s - lse_ref[g : g + 1, :])
            if first:
                key = lax.broadcasted_iota(jnp.int32, (T, W), 0)
                query = lax.broadcasted_iota(jnp.int32, (T, W), 1) % T
                p = jnp.where(key <= query, p, 0.0)
            dp = dot(kv[:, vat], jnp.concatenate([dot_[h, :] for h in heads], 1))
            dz = (p * (dp - dl[g : g + 1, :])).astype(BF)
            out[:, vat] = dot(p.astype(BF), don[g]).astype(BF)
            out[:, at] = dot(dz, qn[g]).astype(BF)
            dq = dot(kt[at, :], dz)
            if first:
                dqa[at, :] = dq
            else:
                dqa[at, :] += dq

    step(0, True)

    def body(b, _):
        step(b, False)
        return 0

    def zero(b, _):
        dkv_ref[lax.rem(b, 2), lax.div(b, 2)] = jnp.zeros((T, KVW), BF)
        return 0

    lax.fori_loop(rng[0], rng[1], body, 0)
    lax.fori_loop(1, rng[0], zero, 0)
    lax.fori_loop(rng[1], 2 * zs, zero, 0)
    cos, sin = cos_ref[...], sin_ref[...]
    for pair in range(PADDED // LANES):
        parts = []
        for h in (2 * pair, 2 * pair + 1):
            g, j = divmod(h, G)
            if h < H:
                parts.append(dqa[g * HD : (g + 1) * HD, j * T : (j + 1) * T] * HD**-0.5)
            else:
                parts.append(jnp.zeros((HD, T), F32))
        grad = jnp.concatenate(parts, 0).T
        turned = grad * cos - half_of(grad * sin)
        dq_ref[:, pair * LANES : (pair + 1) * LANES] = turned.astype(BF)
    kv_s[0, 0] = dq_ref[:, :KVW]
    kv_s[0, 1, :, : PADDED - KVW] = dq_ref[:, KVW:]
    copies = [
        pltpu.make_async_copy(dkv_ref.at[0], own_ref, out_sems.at[0]),
        pltpu.make_async_copy(dkv_ref.at[1], send_ref.at[pl.ds(0, zs)], out_sems.at[1]),
        pltpu.make_async_copy(kv_s.at[0, pl.ds(0, 2)], send_ref.at[pl.ds(zs, 2)], out_sems.at[2]),
    ]
    for copy in copies:
        copy.start()
    for copy in copies:
        copy.wait()


def attend_back(rng, q, o, do, lse, cos, sin, kv_all):
    blocks, other = kv_all
    T, zs = q.shape[0], len(blocks)
    W = G * T
    return pl.pallas_call(
        functools.partial(attend_back_kernel, zs),
        out_shape=(
            jax.ShapeDtypeStruct((T, PADDED), BF),
            jax.ShapeDtypeStruct((zs, T, KVW), BF),
            jax.ShapeDtypeStruct((zs + 2, T, KVW), BF),
        ),
        in_specs=[SMEM] + [VMEM] * 6 + [ANY] * (zs + 1),
        out_specs=[VMEM, ANY, ANY],
        scratch_shapes=[
            pltpu.VMEM((2, zs, T, KVW), BF),
            pltpu.VMEM((D, T), BF),
            pltpu.VMEM((D, T), BF),
            pltpu.VMEM((KV, W, HD), BF),
            pltpu.VMEM((KV, W, HD), BF),
            pltpu.VMEM((KV * HD, T), BF),
            pltpu.VMEM((KV, W), F32),
            pltpu.VMEM((KV * HD, W), F32),
            pltpu.SemaphoreType.DMA((zs + 1,)),
            pltpu.VMEM((2, zs, T, KVW), BF),
            pltpu.SemaphoreType.DMA((3,)),
        ],
        compiler_params=BIG,
        cost_estimate=cost(24),
        name="attend_back",
    )(rng, q, o, do, lse, cos, sin, *blocks, other)


def spread_kv(block):
    blocks = [block] + [move_z(block, d) for d in range(1, lax.axis_size("z"))]
    return blocks, swap(jnp.stack(blocks), "core")


def collect_kv(grads, got, before=()):
    count = lax.axis_size("z")
    moving = plus(grads[count - 1], got[count - 1])
    for d in range(count - 2, -1, -1):
        moved = move_z(after(moving, *before[d]) if d < len(before) else moving, -1)
        own = plus(grads[d], got[d])
        if d == 0:
            return [own, moved]
        moving = plus(own, moved)


def qkv_kernel(base, x_ref, gain_ref, cos_ref, sin_ref, w_hbm, na_ref, q_ref, kv_ref, w_s, sem):
    rows = w_s.shape[1] // QKV_BLOCKS
    copy = pltpu.make_async_copy(w_hbm.at[:, pl.ds(base, w_s.shape[1]), :], w_s, sem)
    copy.start()
    x = x_ref[...].astype(F32)
    normed = (x * rms(x) * gain_ref[...]).astype(BF)
    na_ref[...] = normed
    copy.wait()
    cos, sin = cos_ref[...], sin_ref[...]
    for j in range(QKV_BLOCKS):
        out = dot(normed, columns(w_s, j * rows, 1, rows))
        if j < 5:
            turned = out * cos + half_of(out) * sin if j < 3 else out
            if j == 2:
                lane = lax.broadcasted_iota(jnp.int32, out.shape, 1)
                turned = jnp.where(lane < HD, turned, out)
            kv_ref[:, j * LANES : (j + 1) * LANES] = turned.astype(BF)
        else:
            turned = (out * cos + half_of(out) * sin).astype(BF) * BF(HD**-0.5)
            at = (j - 5) * LANES
            width = min(LANES, D - at)
            q_ref[:, at : at + width] = turned[:, :width]


def qkv_forward(x, gain, cos, sin, weights, base):
    count = x.shape[0]
    shards = weights.shape[0]
    rows = PADDED // shards
    return pl.pallas_call(
        functools.partial(qkv_kernel, base),
        out_shape=(
            jax.ShapeDtypeStruct((count, PADDED), BF),
            jax.ShapeDtypeStruct((count, D), BF),
            jax.ShapeDtypeStruct((count, KVW), BF),
        ),
        in_specs=[VMEM] * 4 + [ANY],
        out_specs=[VMEM] * 3,
        scratch_shapes=[pltpu.VMEM((shards, QKV_BLOCKS * rows, LANES), BF), pltpu.SemaphoreType.DMA],
        compiler_params=BIG,
        cost_estimate=cost(6),
        name="qkv_forward",
    )(x, gain, cos, sin, weights)


def weight_copies(w_hbm, w_s, sems, first):
    shards = w_hbm.shape[0]
    rows, ff_rows = PADDED // shards, FF // shards
    gate = OUT_BLOCKS * rows
    up = gate + FF_BLOCKS * rows
    down = up + FF_BLOCKS * rows
    step = WIDE // LANES * rows
    everyone = pl.ds(0, shards)
    places = [(everyone, 0, gate)]
    places += [(everyone, at + i * step, step) for i in range(FF // WIDE) for at in (gate, up)]
    places += [(pl.ds(h * shards // 2, shards // 2), down, OUT_BLOCKS * ff_rows) for h in range(2)]
    copies = []
    for i, (who, at, height) in enumerate(places):
        source, target = w_hbm.at[who, pl.ds(first + at, height), :], w_s.at[who, pl.ds(at, height), :]
        copies.append(pltpu.make_async_copy(source, target, sems.at[i]))
    pairs = [copies[1 + 2 * i : 3 + 2 * i] for i in range(FF // WIDE)]
    return copies[0], pairs, copies[-2:]


def gate_up(w_s, i):
    rows = PADDED // w_s.shape[0]
    at = OUT_BLOCKS * rows + i * (WIDE // LANES) * rows
    return [columns(w_s, at + j * FF_BLOCKS * rows, WIDE // LANES, rows) for j in range(2)]


def down_half(w_s, h):
    shards = w_s.shape[0]
    rows, ff_rows = PADDED // shards, FF // shards
    at = (OUT_BLOCKS + 2 * FF_BLOCKS) * rows
    who = slice(h * shards // 2, (h + 1) * shards // 2)
    parts = [w_s[who, at + i * ff_rows : at + (i + 1) * ff_rows, :].reshape(-1, LANES) for i in range(OUT_BLOCKS)]
    return jnp.concatenate(parts, 1)


def ffn_up(x, op, na, gain, w_s, acts, loads):
    out, pairs, downs = loads
    rows = PADDED // w_s.shape[0]
    acts[:, FF : FF + PADDED] = op
    acts[:, FF + 2 * PADDED :] = na
    out.wait()
    mixed = x.astype(F32) + dot(op, columns(w_s, 0, OUT_BLOCKS, rows))
    normed = (mixed * rms(mixed) * gain).astype(BF)
    acts[:, FF + PADDED : FF + 2 * PADDED] = normed
    gates = []
    for i in range(FF // WIDE):
        for copy in pairs[i]:
            copy.wait()
        gate, up = gate_up(w_s, i)
        g, u = dot(normed, gate), dot(normed, up)
        acts[:, i * WIDE : (i + 1) * WIDE] = (g * jax.nn.sigmoid(g) * u).astype(BF)
        gates.append((g.astype(BF), u.astype(BF)))
    return mixed, gates


def ffn_down(mixed, w_s, acts, downs):
    total = mixed
    for h in range(2):
        downs[h].wait()
        total = total + dot(acts[:, h * FF // 2 : (h + 1) * FF // 2], down_half(w_s, h))
    return total.astype(BF)


def ffn_kernel(first, op_ref, x_ref, na_ref, gain_ref, w_hbm, acts_hbm, m_ref, gu_hbm, y_ref, w_s, acts, gu, sems, outs):
    loads = weight_copies(w_hbm, w_s, sems, first)
    for copy in [loads[0]] + sum(loads[1], []) + loads[2]:
        copy.start()
    mixed, gates = ffn_up(x_ref[...], op_ref[...], na_ref[...], gain_ref[...], w_s, acts, loads)
    m_ref[...] = mixed
    for i, pair in enumerate(gates):
        for j in range(2):
            gu[j, :, i * WIDE : (i + 1) * WIDE] = pair[j]
    sends = [pltpu.make_async_copy(acts, acts_hbm, outs.at[0]), pltpu.make_async_copy(gu, gu_hbm, outs.at[1])]
    for copy in sends:
        copy.start()
    y_ref[...] = ffn_down(mixed, w_s, acts, loads[2])
    for copy in sends:
        copy.wait()


def ffn_forward(op, x, na, gain, weights, first):
    count = x.shape[0]
    shards = weights.shape[0]
    later = (OUT_BLOCKS + 2 * FF_BLOCKS) * (PADDED // shards) + OUT_BLOCKS * (FF // shards)
    return pl.pallas_call(
        functools.partial(ffn_kernel, first),
        out_shape=(
            jax.ShapeDtypeStruct((count, ACTS), BF),
            jax.ShapeDtypeStruct((count, PADDED), F32),
            jax.ShapeDtypeStruct((2, count, FF), BF),
            jax.ShapeDtypeStruct((count, PADDED), BF),
        ),
        in_specs=[VMEM] * 4 + [ANY],
        out_specs=[ANY, VMEM, ANY, VMEM],
        scratch_shapes=[
            pltpu.VMEM((shards, later, LANES), BF),
            pltpu.VMEM((count, ACTS), BF),
            pltpu.VMEM((2, count, FF), BF),
            pltpu.SemaphoreType.DMA((3 + 2 * (FF // WIDE),)),
            pltpu.SemaphoreType.DMA((2,)),
        ],
        compiler_params=BIG,
        cost_estimate=cost(9),
        name="ffn_forward",
    )(op, x, na, gain, weights)


def ffn_back_body(dy, mixed, gain, gates, e_s, w_s, back, loads, spread):
    out, pairs, downs = loads
    rows = PADDED // w_s.shape[0]
    back[:, 2 * FF + PADDED :] = dy
    for h in range(2):
        downs[h].wait()
        at = h * FF // 2
        d_hidden = dot_nt(dy, down_half(w_s, h))
        g, u = (part.astype(F32) for part in gates(h))
        sig = jax.nn.sigmoid(g)
        back[:, at : at + FF // 2] = (d_hidden * u * sig * (1.0 + g * (1.0 - sig))).astype(BF)
        back[:, FF + at : FF + at + FF // 2] = (d_hidden * g * sig).astype(BF)
    grad = None
    for i in range(FF // WIDE):
        for copy in pairs[i]:
            copy.wait()
        gate, up = gate_up(w_s, i)
        part = dot_nt(back[:, i * WIDE : (i + 1) * WIDE], gate) + dot_nt(back[:, FF + i * WIDE : FF + (i + 1) * WIDE], up)
        grad = part if grad is None else grad + part
    norm, dgain = norm_back(grad, mixed, gain)
    d_mixed = dy.astype(F32) + norm
    low = d_mixed.astype(BF)
    back[:, 2 * FF : 2 * FF + PADDED] = low
    out.wait()
    d_padded = dot_nt(low, columns(w_s, 0, OUT_BLOCKS, rows)).astype(BF)
    spread.wait()
    return d_mixed, dgain, dot_nt(d_padded, e_s[...]).astype(BF)


class Loaded:
    def wait(self):
        pass


def turn_acts(core, acts, own_ref, send_ref):
    at, to = 0, 0
    for width in (FF, PADDED, PADDED, PADDED):
        turned = acts[:, at : at + width].astype(F32).T.astype(BF)
        own, send = own_rows(turned, core, width // 16)
        own_ref[to : to + width // 2, :] = own
        send_ref[to : to + width // 2, :] = send
        at, to = at + width, to + width // 2


def ffn_both_kernel(first, place, op_ref, x_ref, na_ref, gain_ref, dy_ref, e_hbm, w_hbm, *refs):
    y_ref, own_ref, send_ref, back_hbm, dm_ref, do_ref, dgain_ref, w_s, acts, gu, back, e_s, sems, others = refs
    loads = weight_copies(w_hbm, w_s, sems, first)
    spread = pltpu.make_async_copy(e_hbm, e_s, others.at[0])
    for copy in [loads[0]] + sum(loads[1], []) + loads[2] + [spread]:
        copy.start()
    mixed, gates = ffn_up(x_ref[...], op_ref[...], na_ref[...], gain_ref[...], w_s, acts, loads)
    for i, pair in enumerate(gates):
        for j in range(2):
            gu[j, :, i * WIDE : (i + 1) * WIDE] = pair[j]
    y_ref[...] = ffn_down(mixed, w_s, acts, loads[2])
    done = Loaded()
    loads = (done, [[done, done]] * (FF // WIDE), [done, done])
    halves = lambda h: [gu[j, :, h * FF // 2 : (h + 1) * FF // 2] for j in range(2)]
    dm_ref[...], dgain_ref[...], do_ref[...] = ffn_back_body(
        dy_ref[...], mixed, gain_ref[...], halves, e_s, w_s, back, loads, spread
    )
    send = pltpu.make_async_copy(back, back_hbm, others.at[1])
    send.start()
    turn_acts(place[0], acts, own_ref, send_ref)
    send.wait()


def ffn_both(place, op, x, na, gain, dy, e, weights, first):
    count = x.shape[0]
    shards = weights.shape[0]
    later = (OUT_BLOCKS + 2 * FF_BLOCKS) * (PADDED // shards) + OUT_BLOCKS * (FF // shards)
    turned = jax.ShapeDtypeStruct((ACTS // 2, count), BF)
    return pl.pallas_call(
        functools.partial(ffn_both_kernel, first),
        out_shape=(
            jax.ShapeDtypeStruct((count, PADDED), BF),
            turned,
            turned,
            jax.ShapeDtypeStruct((count, BACK), BF),
            jax.ShapeDtypeStruct((count, PADDED), F32),
            jax.ShapeDtypeStruct((count, D), BF),
            jax.ShapeDtypeStruct((1, PADDED), F32),
        ),
        in_specs=[SMEM] + [VMEM] * 5 + [ANY] * 2,
        out_specs=[VMEM] * 3 + [ANY] + [VMEM] * 3,
        scratch_shapes=[
            pltpu.VMEM((shards, later, LANES), BF),
            pltpu.VMEM((count, ACTS), BF),
            pltpu.VMEM((2, count, FF), BF),
            pltpu.VMEM((count, BACK), BF),
            pltpu.VMEM((D, PADDED), BF),
            pltpu.SemaphoreType.DMA((3 + 2 * (FF // WIDE),)),
            pltpu.SemaphoreType.DMA((2,)),
        ],
        compiler_params=BIG,
        cost_estimate=cost(20),
        name="ffn_both",
    )(place, op, x, na, gain, dy, e, weights)


def both_back_kernel(base, first, zs, dq_ref, cos_ref, sin_ref, x_ref, gain_ref, dm_ref, *refs):
    shares, refs = refs[:zs], refs[zs:]
    dgf_ref, m_ref, gain_f_ref, gu_hbm, e_hbm, wa_hbm, wf_hbm = refs[:7]
    dkv_ref, low_ref, back_hbm, dm_out, do_ref, dgain_ref, wa_s, wf_s, back, gu, e_s, sem, sems, others = refs[7:]
    copy = pltpu.make_async_copy(wa_hbm.at[:, pl.ds(base, wa_s.shape[1]), :], wa_s, sem)
    loads = weight_copies(wf_hbm, wf_s, sems, first)
    load = pltpu.make_async_copy(gu_hbm, gu, others.at[0])
    spread = pltpu.make_async_copy(e_hbm, e_s, others.at[1])
    for each in [copy] + loads[2] + [load] + sum(loads[1], []) + [loads[0], spread]:
        each.start()
    dx = qkv_back_body(dq_ref, shares, cos_ref[...], sin_ref[...], x_ref, gain_ref, dm_ref, dgf_ref, copy, wa_s, dkv_ref)
    low = dx.astype(BF)
    low_ref[...] = low
    load.wait()
    halves = lambda h: [gu[j, :, h * FF // 2 : (h + 1) * FF // 2] for j in range(2)]
    dm_out[...], dgain_ref[...], do_ref[...] = ffn_back_body(
        low, m_ref[...], gain_f_ref[...], halves, e_s, wf_s, back, loads, spread
    )
    send = pltpu.make_async_copy(back, back_hbm, others.at[2])
    send.start()
    send.wait()


def both_back(dq, shares, cos, sin, x, gain, dm, dgf, w_a, base, mixed, gain_f, gu, e, w_f, first):
    count = x.shape[0]
    shards = w_a.shape[0]
    rows = PADDED // shards
    later = (OUT_BLOCKS + 2 * FF_BLOCKS) * rows + OUT_BLOCKS * (FF // shards)
    return pl.pallas_call(
        functools.partial(both_back_kernel, base, first, len(shares)),
        out_shape=(
            jax.ShapeDtypeStruct((count + EXTRA, KVW), BF),
            jax.ShapeDtypeStruct((count, PADDED), BF),
            jax.ShapeDtypeStruct((count, BACK), BF),
            jax.ShapeDtypeStruct((count, PADDED), F32),
            jax.ShapeDtypeStruct((count, D), BF),
            jax.ShapeDtypeStruct((1, PADDED), F32),
        ),
        in_specs=[VMEM] * (9 + len(shares)) + [ANY] * 4,
        out_specs=[VMEM, VMEM, ANY] + [VMEM] * 3,
        scratch_shapes=[
            pltpu.VMEM((shards, QKV_BLOCKS * rows, LANES), BF),
            pltpu.VMEM((shards, later, LANES), BF),
            pltpu.VMEM((count, BACK), BF),
            pltpu.VMEM((2, count, FF), BF),
            pltpu.VMEM((D, PADDED), BF),
            pltpu.SemaphoreType.DMA,
            pltpu.SemaphoreType.DMA((3 + 2 * (FF // WIDE),)),
            pltpu.SemaphoreType.DMA((3,)),
        ],
        compiler_params=BIG,
        cost_estimate=cost(18),
        name="both_back",
    )(dq, cos, sin, x, gain, dm, *shares, dgf, mixed, gain_f, gu, e, w_a, w_f)


def qkv_back_body(dq_ref, shares, cos, sin, x_ref, gain_ref, dm_ref, dgf_ref, copy, w_s, dkv_ref):
    count = x_ref.shape[0]
    rows = w_s.shape[1] // QKV_BLOCKS
    for j in range(KVW // LANES):
        at = slice(j * LANES, (j + 1) * LANES)
        grad = shares[0][:, at].astype(F32)
        for share in shares[1:]:
            grad = grad + share[:, at].astype(F32)
        turned = grad * cos - half_of(grad * sin) if j < 3 else grad
        if j == 2:
            lane = lax.broadcasted_iota(jnp.int32, grad.shape, 1)
            turned = jnp.where(lane < HD, turned, grad)
        dkv_ref[:count, at] = turned.astype(BF)
    copy.wait()
    kv_blocks = KVW // LANES
    d_normed = dot_nt(dkv_ref[:count, :], columns(w_s, 0, kv_blocks, rows))
    d_normed = d_normed + dot_nt(dq_ref[...], columns(w_s, kv_blocks * rows, QKV_BLOCKS - kv_blocks, rows))
    back, dgain = norm_back(d_normed, x_ref[...].astype(F32), gain_ref[...])
    dkv_ref[count:, :] = gain_rows(dgain, dgf_ref[...])
    return dm_ref[...] + back


def qkv_back_kernel(base, zs, dq_ref, cos_ref, sin_ref, x_ref, gain_ref, dm_ref, *refs):
    shares, (dgf_ref, w_hbm, dkv_ref, dx_ref, low_ref, w_s, sem) = refs[:zs], refs[zs:]
    copy = pltpu.make_async_copy(w_hbm.at[:, pl.ds(base, w_s.shape[1]), :], w_s, sem)
    copy.start()
    dx = qkv_back_body(dq_ref, shares, cos_ref[...], sin_ref[...], x_ref, gain_ref, dm_ref, dgf_ref, copy, w_s, dkv_ref)
    dx_ref[...] = dx
    low_ref[...] = dx.astype(BF)


def gain_rows(first, second):
    half = PADDED // 2
    rows = [first[:, :half], first[:, half:], second[:, :half], second[:, half:]]
    rows = jnp.concatenate(rows + [jnp.zeros((EXTRA - 4, half), F32)], 0)
    return jnp.concatenate([rows, jnp.zeros((EXTRA, KVW - half), F32)], 1).astype(BF)


def gain_columns(own, other):
    total = own.astype(F32) + other.astype(F32)
    half = PADDED // 2
    rows = [jnp.concatenate([total[2 * i : 2 * i + 1, :half], total[2 * i + 1 : 2 * i + 2, :half]], 1) for i in range(2)]
    return jnp.concatenate(rows + [jnp.zeros((LANES - 2, PADDED), F32)], 0).T.astype(BF)


def qkv_backward(dq, shares, cos, sin, x, gain, dm, dgf, weights, base):
    count = x.shape[0]
    shards = weights.shape[0]
    rows = PADDED // shards
    return pl.pallas_call(
        functools.partial(qkv_back_kernel, base, len(shares)),
        out_shape=(
            jax.ShapeDtypeStruct((count + EXTRA, KVW), BF),
            jax.ShapeDtypeStruct((count, PADDED), F32),
            jax.ShapeDtypeStruct((count, PADDED), BF),
        ),
        in_specs=[VMEM] * (7 + len(shares)) + [ANY],
        out_specs=[VMEM] * 3,
        scratch_shapes=[pltpu.VMEM((shards, QKV_BLOCKS * rows, LANES), BF), pltpu.SemaphoreType.DMA],
        compiler_params=BIG,
        cost_estimate=cost(6),
        name="qkv_backward",
    )(dq, cos, sin, x, gain, dm, *shares, dgf, weights)


def own_rows(turned, core, rows):
    split = turned.reshape(-1, 2, rows, turned.shape[-1])
    first, second = split[:, 0].reshape(-1, turned.shape[-1]), split[:, 1].reshape(-1, turned.shape[-1])
    return jnp.where(core == 0, first, second), jnp.where(core == 0, second, first)


def turn_kernel(place, acts_ref, own_ref, send_ref):
    turn_acts(place[0], acts_ref, own_ref, send_ref)


def turn(place, acts):
    shape = jax.ShapeDtypeStruct((ACTS // 2, acts.shape[0]), BF)
    return pl.pallas_call(
        turn_kernel,
        out_shape=(shape, shape),
        in_specs=[SMEM, VMEM],
        out_specs=[VMEM] * 2,
        compiler_params=BIG,
        cost_estimate=cost(4),
        name="turn",
    )(place, acts)


def write_split(out, keep_ref, send_ref, at, rows, half):
    for i in range(out.shape[1] // LANES):
        block = out[:, i * LANES : (i + 1) * LANES].reshape(2, -1, rows, LANES)
        place = slice(at + i * rows, at + (i + 1) * rows)
        keep_ref[:, place, :] = jnp.where(half == 0, block[0], block[1])
        send_ref[:, place, :] = jnp.where(half == 0, block[1], block[0])


def grad_ffn_kernel(place, own_hbm, other_hbm, back_hbm, back_other_hbm, *refs):
    outs, (left, back, *held, sems, out_sems) = refs[:8], refs[8:]
    keep_a, send_a, keep_u, send_u = held[:2], held[2:4], held[4:6], held[6:8]
    half, section = place[1], place[2]
    count = back.shape[0] // 2
    chips = keep_a[0].shape[0]
    rows, ff_rows = PADDED // (2 * chips), FF // (2 * chips)
    steps = FF // CHUNK
    hd, op, nf = (0, FF // 2), (FF // 2, PADDED // 2), ((FF + PADDED) // 2, PADDED // 2)
    loads = []

    def load(at, width, height, first):
        group = []
        for side, (turned, wide) in enumerate(((own_hbm, back_hbm), (other_hbm, back_other_hbm))):
            place_l = (pl.ds(height[0], height[1]), pl.ds(side * count, count))
            place_b = (pl.ds(side * count, count), pl.ds(at, width))
            if first:
                group.append(pltpu.make_async_copy(turned.at[place_l[0], :], left.at[place_l], sems.at[4 * len(loads) + 2 * side]))
            group.append(pltpu.make_async_copy(wide.at[:, place_b[1]], back.at[place_b], sems.at[4 * len(loads) + 2 * side + 1]))
        loads.append(group)
        for copy in group:
            copy.start()

    load(0, FF, nf, True)
    load(2 * FF + PADDED, PADDED, hd, True)
    load(FF, FF, nf, False)
    load(2 * FF, PADDED, op, True)

    def ready(i):
        for copy in loads[i]:
            copy.wait()

    def product(which, at, width):
        return dot(left[which[0] : which[0] + which[1], :], back[:, at : at + width]).astype(BF)

    def as_blocks(out, height):
        width = out.shape[1] // LANES
        return [out[:, i * LANES : (i + 1) * LANES].reshape(chips, height, LANES) for i in range(width)]

    sent = []

    def finish(*which):
        for i in which:
            sent.append(pltpu.make_async_copy(held[i], outs[i], out_sems.at[i]))
            sent[-1].start()

    ready(0)
    ready(1)
    block = CHUNK // LANES * rows
    narrow_width = PADDED // steps
    for j in range(steps):
        gate = jnp.concatenate(as_blocks(product(nf, j * CHUNK, CHUNK), rows), 1)
        down = jnp.concatenate(as_blocks(product(hd, 2 * FF + PADDED + j * narrow_width, narrow_width), ff_rows), 1)
        at = slice(j % 2 * block, (j % 2 + 1) * block)
        keep_a[j // 2][:, at, :] = jnp.where(section == 0, down, gate)
        send_a[j // 2][:, at, :] = jnp.where(section == 0, gate, down)
        if j % 2:
            finish(j // 2, 2 + j // 2)
    ready(2)
    for j in range(steps):
        h = j // (steps - 1)
        write_split(product(nf, FF + j * CHUNK, CHUNK), keep_u[h], send_u[h], (j - h * (steps - 1)) * block, rows, half)
        if j == steps - 2:
            finish(4, 6)
    ready(3)
    write_split(product(op, 2 * FF, PADDED), keep_u[1], send_u[1], block, rows, half)
    finish(5, 7)
    for copy in sent:
        copy.wait()


def grad_ffn(place, own, other, back, back_other, shards):
    count = own.shape[1]
    chips = shards // 2
    rows = PADDED // shards
    steps = FF // CHUNK
    block = CHUNK // LANES * rows
    shapes = [(chips, 2 * block, LANES)] * 4
    shapes += [(chips // 2, height, LANES) for height in ((steps - 1) * block, block + OUT_BLOCKS * rows) * 2]
    return pl.pallas_call(
        grad_ffn_kernel,
        out_shape=[jax.ShapeDtypeStruct(shape, BF) for shape in shapes],
        in_specs=[SMEM] + [ANY] * 4,
        out_specs=[ANY] * 8,
        scratch_shapes=[pltpu.VMEM((ACTS // 2, 2 * count), BF), pltpu.VMEM((2 * count, BACK), BF)]
        + [pltpu.VMEM(shape, BF) for shape in shapes]
        + [pltpu.SemaphoreType.DMA((16,)), pltpu.SemaphoreType.DMA((8,))],
        compiler_params=BIG,
        cost_estimate=cost(11),
        name="grad_ffn",
    )(place, own, other, back, back_other)


def grad_attn_kernel(place, own, other, *refs):
    grads, keep, send = refs[:-2], refs[-2], refs[-1]
    core, half = place[0], place[1]
    count = own.shape[1]
    rows = PADDED // 16
    na = slice((FF + 2 * PADDED) // 2, ACTS // 2)
    at = 0
    for grad, grad_other in zip(grads[::2], grads[1::2]):
        if len(grad_other.shape) == 3:
            right = jnp.concatenate([grad_other[0], grad_other[1, :, : PADDED - KVW]], 1)
        else:
            right = grad_other[:count, :]
        out = (dot(own[na, :], grad[:count, :]) + dot(other[na, :], right)).astype(BF)
        write_split(out, keep, send, at, rows, half)
        at += grad.shape[1] // LANES * rows
        if grad.shape[0] > count:
            gains = gain_columns(grad[count:, :], grad_other[count:, :])
            write_split(own_rows(gains, core, rows)[0], keep, send, at, rows, half)
            at += rows


def grad_attn(place, own, other, *grads):
    rows = PADDED // 16
    blocks = sum(grad.shape[1] // LANES + (grad.shape[0] > own.shape[1]) for grad in grads[::2])
    shape = jax.ShapeDtypeStruct((4, blocks * rows, LANES), BF)
    return pl.pallas_call(
        grad_attn_kernel,
        out_shape=(shape, shape),
        in_specs=[SMEM] + [VMEM] * (2 + len(grads)),
        out_specs=[VMEM] * 2,
        compiler_params=BIG,
        cost_estimate=cost(4),
        name="grad_attn",
    )(place, own, other, *grads)


def narrow(values, spread):
    if values.dtype == BF:
        return dot_nt(values, spread)
    total, left = None, values
    for _ in range(3):
        part = left.astype(BF)
        left = left - part.astype(F32)
        out = dot_nt(part, spread)
        total = out if total is None else total + out
    return total


def narrow_t(values, spread):
    if values.dtype == BF:
        return dot_nt(spread, values)
    total, left = None, values
    for _ in range(3):
        part = left.astype(BF)
        left = left - part.astype(F32)
        out = dot_nt(spread, part)
        total = out if total is None else total + out
    return total


def sum_block(ref, other, j, height):
    at = slice(j * height, (j + 1) * height)
    out = ref[at, :].astype(F32)
    return out if other is None else out + other[at, :].astype(F32)


def sum_matrix(ref, other, first, count, height):
    return jnp.concatenate([sum_block(ref, other, first + j, height) for j in range(count)], 1)


def unpack_up_kernel(place, *refs):
    parts, (e_ref, up_ref, o_ref) = refs[:-3], refs[-3:]
    size, rows = up_ref.shape[0], parts[0].shape[0] // (FF_BLOCKS - CHUNK // LANES)
    cut = FF_BLOCKS - CHUNK // LANES
    for layer in range(2):

        @pl.when(place[2] == layer)
        def _():
            u, got_u, v, got_v = parts[4 * layer : 4 * layer + 4]
            for j in range(FF_BLOCKS):
                block = sum_block(u, got_u, j, rows) if j < cut else sum_block(v, got_v, j - cut, rows)
                up_ref[:, 0, j * LANES : (j + 1) * LANES] = block[:size]
            o_ref[:, 0, :] = narrow(sum_matrix(v, got_v, FF_BLOCKS - cut, OUT_BLOCKS, rows), e_ref[...])[:size]


def unpack_down_kernel(place, *refs):
    parts, (e_ref, gate_ref, down_ref) = refs[:-3], refs[-3:]
    size, ff_rows = gate_ref.shape[0], down_ref.shape[0]
    rows = parts[0].shape[0] // FF_BLOCKS
    for layer in range(2):

        @pl.when(place[2] == layer)
        def _():
            a, got_a = parts[2 * layer : 2 * layer + 2]
            down, gate = (a, got_a) if layer == 0 else (got_a, a)
            for j in range(FF_BLOCKS):
                gate_ref[:, 0, j * LANES : (j + 1) * LANES] = sum_block(gate, None, j, rows)[:size]
            down_ref[...] = narrow(sum_matrix(down, None, 0, OUT_BLOCKS, ff_rows), e_ref[...])


def unpack_qkv_kernel(place, *refs):
    parts, (q_ref, k_ref, v_ref, gain_ref) = refs[:-4], refs[-4:]
    size = q_ref.shape[0]
    kv_blocks = KVW // LANES
    rows = parts[0].shape[0] // (OUT_BLOCKS + kv_blocks + 1)
    for layer in range(2):

        @pl.when(place[2] == layer)
        def _():
            s, got = parts[2 * layer : 2 * layer + 2]
            q_ref[:, 0, :] = sum_matrix(s, got, 0, OUT_BLOCKS, rows)[:size, :D]
            both = sum_matrix(s, got, OUT_BLOCKS, kv_blocks, rows)
            k_ref[:, 0, :] = both[:size, : KV * HD]
            v_ref[:, 0, :] = both[:size, KV * HD :]
            gain_ref[...] = sum_block(s, got, OUT_BLOCKS + kv_blocks, rows).T


def unpack(kernel, name, place, parts, shapes):
    return pl.pallas_call(
        kernel,
        out_shape=[jax.ShapeDtypeStruct(shape, F32) for shape in shapes],
        in_specs=[SMEM] + [VMEM] * len(parts),
        out_specs=[VMEM] * len(shapes),
        compiler_params=BIG,
        cost_estimate=cost(4),
        name=name,
    )(place, *parts)


def join_kernel(place, own0, own1, got, e_ref, out_ref):
    section = place[2]
    for layer, own in enumerate((own0, own1)):

        @pl.when(section == layer)
        def _():
            out_ref[layer] = narrow_t(own[...], e_ref[...]).astype(out_ref.dtype)
            out_ref[1 - layer] = narrow_t(got[...], e_ref[...]).astype(out_ref.dtype)


def join(place, own0, own1, got, spread, dtype):
    return pl.pallas_call(
        join_kernel,
        out_shape=jax.ShapeDtypeStruct((2, D, own0.shape[0]), dtype),
        in_specs=[SMEM] + [VMEM] * 4,
        out_specs=VMEM,
        compiler_params=BIG,
        cost_estimate=cost(4),
        name="join",
    )(place, own0, own1, got, spread).transpose(0, 2, 1)


def spread_matrix(shards):
    size, room = D // shards, PADDED // shards
    feature = lax.broadcasted_iota(jnp.int32, (D, PADDED), 0)
    place = lax.broadcasted_iota(jnp.int32, (D, PADDED), 1)
    return (feature // size * room + feature % size == place).astype(BF)


def to_blocks(matrix):
    rows, width = matrix.shape
    return matrix.reshape(rows, width // LANES, LANES).transpose(1, 0, 2).reshape(-1, LANES)


def from_blocks(blocks, rows):
    return blocks.reshape(-1, rows, LANES).transpose(1, 0, 2).reshape(rows, -1)


def plus(left, right):
    return (left.astype(F32) + right.astype(F32)).astype(BF)


def after(value, *earlier):
    return lax.optimization_barrier((value,) + earlier)[0]


def scatter_z(parts):
    return lax.psum_scatter(parts, "z", scatter_dimension=0, tiled=False)


def scatter_z_small(parts, *before_last):
    count, me = lax.axis_size("z"), lax.axis_index("z")
    while parts.shape[0] > 1:
        step = parts.shape[0] // 2
        split = parts.reshape((2, step) + parts.shape[1:])
        bit = lax.rem(lax.div(me, step), 2)
        keep = lax.dynamic_index_in_dim(split, bit, 0, False)
        send = lax.dynamic_index_in_dim(split, 1 - bit, 0, False)
        if step == 1 and before_last:
            send = after(send, *before_last)
        parts = plus(keep, lax.ppermute(send, "z", [(i, i ^ step) for i in range(count)]))
    return parts[0]


def to_owner(part, layer):
    return lax.ppermute(part, "section", [(1 - layer, layer)])


def per_device_blocks(tokens, cotangent, positions, attn_gain, w_query, w_key, w_value, w_out, ffn_gain, w_gate, w_up, w_down):
    section, half = lax.axis_index("section"), lax.axis_index("dp")
    z_index, core = lax.axis_index("z"), lax.axis_index("core")
    plane = ("dp", "z", "core")
    size, ff_rows = w_query.shape[1], w_down.shape[1]
    shards = D // size
    room = PADDED // shards
    chips = shards // 2
    qkv_rows = QKV_BLOCKS * room
    block_range = jnp.stack([2 - core, 2 * z_index + 2]).astype(jnp.int32)
    place = jnp.stack([core, half, section]).astype(jnp.int32)
    spread = spread_matrix(shards)

    def mine(array_in):
        return lax.dynamic_index_in_dim(array_in, section, 0, keepdims=False)

    def widen(array_in):
        return project(array_in, spread).astype(BF)

    def padded(array_in):
        return jnp.pad(array_in, ((0, room - size), (0, 0)))

    gains = jnp.concatenate([attn_gain, ffn_gain], 0).T
    qkv = jnp.concatenate([w_key[0], w_value[0], w_query[0], gains, jnp.zeros((size, HD - 2), BF)], -1)
    narrow = jnp.concatenate([qkv, widen(w_out[0]), w_gate[0], w_up[0]], -1)
    shard = jnp.concatenate([to_blocks(padded(narrow)), to_blocks(widen(w_down[0]))], 0)
    first, rest = shard[:qkv_rows], shard[qkv_rows:]
    got_first = swap(first, "section")
    got_rest = swap(after(rest, got_first), "section")

    def layer_shard(own, got, layer):
        return jnp.where(section == layer, own, got)

    def gathered(*pieces):
        block = pieces[0] if len(pieces) == 1 else jnp.concatenate(pieces, 0)
        return lax.all_gather(block, plane, axis=0)

    def gains_at(whole, base):
        at = base + (QKV_BLOCKS - 1) * room
        gain = whole[:, at : at + room, HD : HD + 2].reshape(-1, 2).T.astype(F32)
        return gain[:1], gain[1:]

    early = gathered(layer_shard(first, got_first, 0))
    middle = gathered(layer_shard(rest, got_rest, 0), after(layer_shard(first, got_first, 1), early))
    base1 = rest.shape[0]
    w0 = (early, 0, middle, 0) + gains_at(early, 0)
    angle_cos, angle_sin = rope_tables(mine(positions))
    cos = jnp.concatenate([angle_cos[:, 0]] * 2, -1)
    sin = jnp.concatenate([angle_sin[:, 0]] * 2, -1)

    def attention(x, layer, *earlier):
        w_a, at_a, gain_a = layer[0], layer[1], layer[4]
        na, q, kv = qkv_forward(x, gain_a, cos, sin, w_a, at_a)
        kv_all = spread_kv(kv)
        o, op, lse = attend(block_range, after(q, *earlier) if earlier else q, kv_all, spread)
        return na, op, (x, q, kv_all, o, lse)

    x0 = widen(mine(tokens))
    na0, op0, saved0 = attention(x0, w0)
    late = gathered(after(layer_shard(rest, got_rest, 1), *saved0[2][0]))
    w1 = (middle, base1, late, 0) + gains_at(middle, base1)
    acts0, mixed0, gu0, y0 = ffn_forward(op0, x0, na0, w0[5], w0[2], w0[3])
    own0, send0 = turn(place, acts0)
    na1, op1, saved1 = attention(y0, w1, own0)
    y1, own1, send1, back1, dm1, do1, dgf1 = ffn_both(
        place, op1, y0, na1, w1[5], widen(mine(cotangent)), spread, w1[2], w1[3]
    )

    def backward_attn(do, saved):
        x, q, kv_all, o, lse = saved
        return attend_back(block_range, q, o, do, lse, cos, sin, kv_all)

    def backward_qkv(dq, shares, dm, dgf, layer, saved):
        w_a, at_a, w_f, at_f, gain_a, gain_f = layer
        return qkv_backward(dq, shares, cos, sin, saved[0], gain_a, dm, dgf, w_a, at_a)

    def halve(total):
        split = total.reshape((2, chips // 2) + total.shape[1:])
        return lax.dynamic_index_in_dim(split, half, 0, False), lax.dynamic_index_in_dim(split, 1 - half, 0, False)

    def scatter(*pieces):
        total = scatter_z(jnp.concatenate(pieces, 1) if len(pieces) > 1 else pieces[0])
        cuts, at = [], 0
        for piece in pieces:
            cuts.append(total[at : at + piece.shape[1]])
            at += piece.shape[1]
        return cuts

    def cross(keep, got):
        keep, send = halve(plus(keep, got))
        return keep, swap(send, "dp")

    def swap_all(sends, axis):
        return [swap(send, axis) for send in sends]

    def all_after(values, *earlier):
        return [after(value, *earlier) for value in values]

    other0, other1 = swap(send0, "core"), swap(send1, "core")

    def swap_all(sends, axis):
        return [swap(send, axis) for send in sends]

    def query_grads(own, got):
        return own, got[-2:]

    grads1 = grad_ffn(place, own1, other1, back1, swap(back1, "core"), shards)
    keep_a1, send_a1, keep_u1, send_u1 = grads1[:2], grads1[2:4], grads1[4:6], grads1[6:8]
    got_a1, got_u1 = swap_all(send_a1, "section"), swap_all(send_u1, "dp")
    got_y = swap(jnp.where(section == 0, y1, y0), "section")
    dq1, dkv1, away1 = backward_attn(after(do1, send_u1[0], got_y), saved1)
    dkv1, away1 = after(dkv1, got_a1[0], got_u1[0]), after(away1, got_a1[0], got_u1[0])
    got1 = swap(away1, "core")
    shares1 = collect_kv(dkv1, got1)
    dq1 = after(dq1, got_a1[1], got_u1[1])
    keep_a1, keep_u1 = all_after(keep_a1, shares1[-1]), all_after(keep_u1, shares1[-1])
    sum_u1 = scatter(*map(plus, keep_u1, got_u1))

    (keep_b1, got_b1), (keep_c1, got_c1) = map(cross, keep_a1, got_a1)
    dkv_low1, dx1_low, back0, dm0, do0, dgf0 = both_back(
        dq1, shares1, cos, sin, y0, w1[4], dm1, dgf1, w1[0], w1[1], mixed0, w0[5], gu0, spread, w0[2], w0[3]
    )
    back0 = after(back0, got_b1, got_c1)
    keep_s1, send_s1 = grad_attn(place, own1, other1, *query_grads(dq1, got1), dkv_low1, swap(dkv_low1, "core"))
    grads0 = grad_ffn(place, own0, other0, after(back0, send_s1), swap(back0, "core"), shards)
    keep_a0, send_a0, keep_u0, send_u0 = grads0[:2], grads0[2:4], grads0[4:6], grads0[6:8]
    got_a0 = swap_all(send_a0, "section")
    got_u0 = [swap(send_u0[0], "dp"), swap(jnp.concatenate([send_u0[1], send_s1], 1), "dp")]
    away_u1 = to_owner(jnp.concatenate(sum_u1, 0), 1)
    dq0, dkv0, away0 = backward_attn(after(do0, send_u0[0], away_u1), saved0)
    away0 = after(away0, got_a0[0], got_u0[0])
    sum_a1 = scatter(plus(keep_b1, got_b1), plus(keep_c1, got_c1))
    (sum_v0,) = scatter(plus(after(keep_u0[0], dkv0), got_u0[0]))
    got0 = swap(away0, "core")
    shares0 = collect_kv(dkv0, got0, [(got_a0[1], got_u0[1]), tuple(sum_a1)])
    keep_q0, send_q0 = grad_attn(place, own0, other0, *query_grads(dq0, got0))
    keep_b0, got_b0 = cross(after(keep_a0[0], dkv0), got_a0[0])
    kept = after(jnp.concatenate([keep_u0[1], keep_s1], 1), shares0[-1], sum_v0)
    late0 = plus(kept, got_u0[1])
    away_a1 = to_owner(jnp.concatenate(sum_a1, 0), 1)
    dq0 = after(dq0, send_q0, late0, away_a1, got_b0)
    dkv_low0, dx0, dx0_low = backward_qkv(dq0, shares0, dm0, dgf0, w0, saved0)
    got_q0 = swap(after(send_q0, shares0[-1]), "dp")
    keep_c0, got_c0 = cross(after(keep_a0[1], shares0[-1]), got_a0[1])
    (sum_w0,) = scatter(late0)
    keep_k0, send_k0 = grad_attn(place, own0, other0, after(dkv_low0, got_c0), swap(dkv_low0, "core"))
    last0 = [plus(after(keep, sum_w0), got) for keep, got in ((keep_b0, got_b0), (keep_c0, got_c0))]
    sum_a0 = jnp.concatenate(scatter(*last0), 0)
    got_k0 = swap(send_k0, "dp")
    keep_q0, keep_k0 = after(keep_q0, *last0), after(keep_k0, *last0)
    pieces = [plus(keep_q0, got_q0), plus(keep_k0, got_k0)]

    cut = send_u0[1].shape[1]
    sum_s1, sum_w0 = sum_w0[cut:], sum_w0[:cut]
    away_s1 = to_owner(sum_s1, 1)
    wide = lambda width: (size, 1, width)
    parts = [part for own in (sum_v0, sum_w0) for part in (own, to_owner(own, 0))]
    cut_u = sum_u1[0].shape[0]
    parts += [sum_u1[0], away_u1[:cut_u], sum_u1[1], away_u1[cut_u:]]
    g_up, g_o = unpack(unpack_up_kernel, "unpack_up", place, parts + [spread], (wide(FF), wide(D)))
    sum_s0 = scatter_z_small(jnp.concatenate(pieces, 1), g_up)
    parts = [sum_s0, to_owner(sum_s0, 0), sum_s1, away_s1]
    shapes = (wide(D), wide(KV * HD), wide(KV * HD), (LANES, room))
    g_q, g_k, g_v, gains = unpack(unpack_qkv_kernel, "unpack_qkv", place, parts, shapes)
    parts = [after(sum_a0, g_up, g_q), to_owner(sum_a0, 0), jnp.concatenate(sum_a1, 0), away_a1]
    g_gate, g_down = unpack(unpack_down_kernel, "unpack_down", place, parts + [spread], (wide(FF), (ff_rows, D)))
    section_out = join(place, y0, y1, got_y, spread, BF)
    got = swap(jnp.where(section == 0, dx1_low, dx0_low), "section")
    input_grad = join(place, dx0, dx1_low, got, spread, F32)
    flat = lambda part: part.transpose(1, 0, 2)[0]
    g_q, g_k, g_v, g_o, g_gate, g_up = map(flat, (g_q, g_k, g_v, g_o, g_gate, g_up))
    outs = (section_out, input_grad, gains[0, :size], g_q, g_k, g_v, g_o, gains[1, :size], g_gate, g_up, g_down)
    return tuple(part[None] for part in outs)


def solution(mesh):
    sizes = mesh.devices.shape
    grid = Mesh(mesh.devices.reshape(sizes[0], sizes[1], sizes[2] // 2, 2), ("section", "dp", "z", "core"))
    ctx = ("z", "core")
    plane = ("dp", "z", "core")
    vector = P("section", plane)
    matrix = P("section", plane, None)
    in_specs = (
        P("dp", ctx, None),
        P("dp", ctx, None),
        P("dp", ctx),
        vector,
        matrix,
        matrix,
        matrix,
        matrix,
        vector,
        matrix,
        matrix,
        matrix,
    )
    acts = P("section", "dp", ctx, None)
    out_specs = (acts, acts, vector, matrix, matrix, matrix, matrix, vector, matrix, matrix, matrix)
    shards = sizes[1] * sizes[2]
    aligned = shards == 16
    return jax.shard_map(per_device_blocks if aligned else per_device, mesh=grid, in_specs=in_specs, out_specs=out_specs, check_vma=False)
```

```python
import functools

import jax
import jax.numpy as jnp
from jax import lax
from jax.experimental import pallas as pl
from jax.experimental.pallas import tpu as pltpu
from jax.sharding import Mesh
from jax.sharding import PartitionSpec as P

D = 960
H = 15
KV = 5
G = H // KV
HD = 64
FF = 2560
EPS = 1e-05
F32 = jnp.float32
BF = jnp.bfloat16


def dot(a,b): return jnp.dot(a,b,preferred_element_type=F32)

def fwd_kernel(rng, q_ref, kv_ref, o_ref, lse_ref, qt, vt, m_s, l_s, acc):
    T=q_ref.shape[0]; W=G*T
    qt[...]=q_ref[...].astype(F32).T.astype(BF)
    nb=kv_ref.shape[0]
    def step(b, first):
        vt[...]=kv_ref[b,:,KV*HD:].astype(F32).T.astype(BF)
        for g in range(KV):
            qg=jnp.concatenate([qt[(g*G+j)*HD:(g*G+j+1)*HD,:] for j in range(G)],1)
            s=dot(kv_ref[b,:,g*HD:(g+1)*HD],qg)
            if first:
                key=lax.broadcasted_iota(jnp.int32,(T,W),0)
                qry=lax.broadcasted_iota(jnp.int32,(T,W),1)%T
                s=jnp.where(key<=qry,s,-1e30)
                m=jnp.max(s,0,keepdims=True)
                p=jnp.exp(s-m)
                l_s[g:g+1,:]=jnp.sum(p,0,keepdims=True)
                acc[g*HD:(g+1)*HD,:]=dot(vt[g*HD:(g+1)*HD,:],p.astype(BF))
            else:
                mo=m_s[g:g+1,:]
                m=jnp.maximum(mo,jnp.max(s,0,keepdims=True))
                p=jnp.exp(s-m); al=jnp.exp(mo-m)
                l_s[g:g+1,:]=l_s[g:g+1,:]*al+jnp.sum(p,0,keepdims=True)
                acc[g*HD:(g+1)*HD,:]=acc[g*HD:(g+1)*HD,:]*al+dot(vt[g*HD:(g+1)*HD,:],p.astype(BF))
            m_s[g:g+1,:]=m
    step(0,True)
    def body(b,_):
        step(b,False); return 0
    lax.fori_loop(rng[0],rng[1],body,0)
    for g in range(KV):
        inv=1.0/l_s[g:g+1,:]
        lse_ref[g:g+1,:]=m_s[g:g+1,:]+jnp.log(l_s[g:g+1,:])
        og=acc[g*HD:(g+1)*HD,:]*inv
        for j in range(G):
            h=g*G+j
            o_ref[:,h*HD:(h+1)*HD]=og[:,j*T:(j+1)*T].T.astype(BF)

def attn_fwd(rng,q,kv):
    T=q.shape[0]; W=G*T
    return pl.pallas_call(fwd_kernel,
      out_shape=(jax.ShapeDtypeStruct((T,H*HD),BF),jax.ShapeDtypeStruct((KV,W),F32)),
      in_specs=[pl.BlockSpec(memory_space=pltpu.SMEM)]+[pl.BlockSpec(memory_space=pltpu.VMEM)]*2,
      out_specs=[pl.BlockSpec(memory_space=pltpu.VMEM)]*2,
      scratch_shapes=[pltpu.VMEM((H*HD,T),BF),pltpu.VMEM((KV*HD,T),BF),pltpu.VMEM((KV,W),F32),pltpu.VMEM((KV,W),F32),pltpu.VMEM((KV*HD,W),F32)],
      compiler_params=pltpu.CompilerParams(vmem_limit_bytes=48<<20),
    )(rng,q,kv)

def bwd_kernel(rng, q_ref, kv_ref, o_ref, do_ref, lse_ref, dq_ref, dkv_ref, qt, dot_, qn, don, kt, dl, dqa):
    T=q_ref.shape[0]; W=G*T
    nb=kv_ref.shape[0]
    qt[...]=q_ref[...].astype(F32).T.astype(BF)
    doT=do_ref[...].astype(F32).T
    dot_[...]=doT.astype(BF)
    oT=o_ref[...].astype(F32).T
    prod=doT*oT
    for h in range(H):
        g,j=divmod(h,G)
        dl[g:g+1,j*T:(j+1)*T]=jnp.sum(prod[h*HD:(h+1)*HD,:],0,keepdims=True)
        qn[g,j*T:(j+1)*T,:]=q_ref[:,h*HD:(h+1)*HD]
        don[g,j*T:(j+1)*T,:]=do_ref[:,h*HD:(h+1)*HD]
    def step(b, first):
        kt[...]=kv_ref[b,:,:KV*HD].astype(F32).T.astype(BF)
        for g in range(KV):
            qg=jnp.concatenate([qt[(g*G+j)*HD:(g*G+j+1)*HD,:] for j in range(G)],1)
            dg=jnp.concatenate([dot_[(g*G+j)*HD:(g*G+j+1)*HD,:] for j in range(G)],1)
            s=dot(kv_ref[b,:,g*HD:(g+1)*HD],qg)
            p=jnp.exp(s-lse_ref[g:g+1,:])
            if first:
                key=lax.broadcasted_iota(jnp.int32,(T,W),0)
                qry=lax.broadcasted_iota(jnp.int32,(T,W),1)%T
                p=jnp.where(key<=qry,p,0.0)
            dp=dot(kv_ref[b,:,(KV+g)*HD:(KV+g+1)*HD],dg)
            dz=(p*(dp-dl[g:g+1,:])).astype(BF)
            dkv_ref[b,:,(KV+g)*HD:(KV+g+1)*HD]=dot(p.astype(BF),don[g]).astype(BF)
            dkv_ref[b,:,g*HD:(g+1)*HD]=dot(dz,qn[g]).astype(BF)
            dq=dot(kt[g*HD:(g+1)*HD,:],dz)
            if first: dqa[g*HD:(g+1)*HD,:]=dq
            else: dqa[g*HD:(g+1)*HD,:]+=dq
    step(0,True)
    def body(b,_):
        step(b,False); return 0
    lax.fori_loop(rng[0],rng[1],body,0)
    def zero(b,_):
        dkv_ref[b]=jnp.zeros((T,2*KV*HD),BF); return 0
    lax.fori_loop(1,rng[0],zero,0)
    lax.fori_loop(rng[1],nb,zero,0)
    for g in range(KV):
        for j in range(G):
            h=g*G+j
            dq_ref[:,h*HD:(h+1)*HD]=(dqa[g*HD:(g+1)*HD,j*T:(j+1)*T]*HD**-0.5).T

def attn_bwd(rng,q,kv,o,do,lse):
    T=q.shape[0]; W=G*T
    return pl.pallas_call(bwd_kernel,
      out_shape=(jax.ShapeDtypeStruct((T,H*HD),F32),jax.ShapeDtypeStruct(kv.shape,BF)),
      in_specs=[pl.BlockSpec(memory_space=pltpu.SMEM)]+[pl.BlockSpec(memory_space=pltpu.VMEM)]*5,
      out_specs=[pl.BlockSpec(memory_space=pltpu.VMEM)]*2,
      scratch_shapes=[pltpu.VMEM((H*HD,T),BF),pltpu.VMEM((H*HD,T),BF),pltpu.VMEM((KV,W,HD),BF),pltpu.VMEM((KV,W,HD),BF),
        pltpu.VMEM((KV*HD,T),BF),pltpu.VMEM((KV,W),F32),pltpu.VMEM((KV*HD,W),F32)],
      compiler_params=pltpu.CompilerParams(vmem_limit_bytes=48<<20),
    )(rng,q,kv,o,do,lse)


def rotate_half(vector):
    half_dim = vector.shape[-1] // 2
    return jnp.concatenate([-vector[..., half_dim:], vector[..., :half_dim]], -1)


def rope_tables(seq_pos):
    half_dim = HD // 2
    inv_freq = 10000.0 ** (-(jnp.arange(half_dim, dtype=F32) * 2.0) / HD)
    angles = seq_pos.astype(F32)[..., None] * inv_freq
    angle_pair = jnp.concatenate([angles, angles], -1)[..., None, :]
    return (jnp.cos(angle_pair), jnp.sin(angle_pair))


def norm_forward(values_in, gain_vec):
    factor = lax.rsqrt(jnp.mean(values_in * values_in, -1, keepdims=True) + EPS)
    return (values_in * factor * gain_vec, factor)


def norm_backward(grad_in, values_in, factor, gain_vec):
    scaled = grad_in * gain_vec
    grad_back = factor * scaled - values_in * factor * factor * factor * jnp.mean(
        scaled * values_in, -1, keepdims=True
    )
    return (grad_back, jnp.sum(grad_in * values_in * factor, 0))


def swap(block, axis):
    return lax.ppermute(block, axis, [(0, 1), (1, 0)])


def move_z(block, distance):
    count = lax.axis_size("z")
    route = [(i, i + distance) for i in range(count) if 0 <= i + distance < count]
    return lax.ppermute(block, "z", route)


def gather_kv(block):
    count = lax.axis_size("z")
    own = [block] + [move_z(block, d) for d in range(1, count)]
    own = jnp.stack(own)
    other = swap(own, "core")
    return jnp.stack([own, other], 1).reshape((2 * count,) + block.shape)


def reduce_kv(blocks):
    count = lax.axis_size("z")
    blocks = blocks.reshape((count, 2) + blocks.shape[1:])
    mine = blocks[:, 0].astype(F32) + swap(blocks[:, 1], "core").astype(F32)
    total = mine[0]
    for d in range(1, count):
        total = total + move_z(mine[d].astype(BF), -d).astype(F32)
    return total


def project(left, right):
    return jnp.dot(left, right, preferred_element_type=F32)


def project_t(left, right):
    return lax.dot_general(left, right, (((1,), (1,)), ((), ())), preferred_element_type=F32)


def outer(left, right):
    return lax.dot_general(left, right, (((0,), (0,)), ((), ())), preferred_element_type=F32)


def rope(values, cosine, sine):
    count = values.shape[0]
    values = values.reshape(count, -1, HD)
    return (values * cosine + rotate_half(values) * sine).reshape(count, -1)


def rope_t(values, cosine, sine):
    count = values.shape[0]
    values = values.reshape(count, -1, HD)
    return (values * cosine - rotate_half(values * sine)).reshape(count, -1)


def layer_forward(rows, tables, weights, block_range):
    gain_a, w_qkv, w_o, gain_f, w_g, w_u, w_d = weights
    cosine, sine = tables
    normed_a, factor_a = norm_forward(rows, gain_a)
    normed_a = normed_a.astype(BF)
    qkv = project(normed_a, w_qkv)
    queries = (rope(qkv[:, :D], cosine, sine)).astype(BF) * BF(HD**-0.5)
    keys = rope(qkv[:, D : D + KV * HD], cosine, sine).astype(BF)
    values = qkv[:, D + KV * HD :].astype(BF)
    kv_all = gather_kv(jnp.concatenate([keys, values], -1))
    attended, log_total = attn_fwd(block_range, queries, kv_all)
    mixed = rows + project(attended, w_o)
    normed_f, factor_f = norm_forward(mixed, gain_f)
    normed_f = normed_f.astype(BF)
    gate_act = project(normed_f, w_g)
    up_proj = project(normed_f, w_u)
    hidden = (jax.nn.silu(gate_act) * up_proj).astype(BF)
    out = (mixed + project(hidden, w_d)).astype(BF)
    saved = (rows, factor_a, normed_a, queries, kv_all, log_total, attended, mixed, factor_f, normed_f, gate_act, up_proj, hidden)
    return out, saved


def layer_backward(grad_low, saved, tables, weights, block_range):
    gain_a, w_qkv, w_o, gain_f, w_g, w_u, w_d = weights
    cosine, sine = tables
    rows, factor_a, normed_a, queries, kv_all, log_total, attended, mixed, factor_f, normed_f, gate_act, up_proj, hidden = saved
    d_hidden = project_t(grad_low, w_d)
    sig = jax.nn.sigmoid(gate_act)
    d_gate = (d_hidden * up_proj * sig * (1.0 + gate_act * (1.0 - sig))).astype(BF)
    d_up = (d_hidden * gate_act * sig).astype(BF)
    d_normed_f = project_t(d_gate, w_g) + project_t(d_up, w_u)
    d_norm, d_gain_f = norm_backward(d_normed_f, mixed, factor_f, gain_f)
    d_mixed = grad_low.astype(F32) + d_norm
    mix_low = d_mixed.astype(BF)
    d_attended = project_t(mix_low, w_o).astype(BF)
    d_query, d_kv = attn_bwd(block_range, queries, kv_all, attended, d_attended, log_total)
    d_kv = reduce_kv(d_kv)
    d_query = rope_t(d_query, cosine, sine).astype(BF)
    d_key = rope_t(d_kv[:, : KV * HD], cosine, sine).astype(BF)
    d_value = d_kv[:, KV * HD :].astype(BF)
    d_qkv = jnp.concatenate([d_query, d_key, d_value], -1)
    d_normed_a = project_t(d_qkv, w_qkv)
    d_norm_a, d_gain_a = norm_backward(d_normed_a, rows, factor_a, gain_a)
    d_rows = d_mixed + d_norm_a
    grads = dict(
        gate=outer(normed_f, d_gate).astype(BF),
        up=outer(normed_f, d_up).astype(BF),
        down=outer(hidden, grad_low).astype(BF),
        out=outer(attended, mix_low).astype(BF),
        qkv=outer(normed_a, d_qkv).astype(BF),
        gains=jnp.stack([d_gain_a, d_gain_f]),
    )
    return d_rows, grads


def per_device(tokens, cotangent, positions, attn_gain, w_query, w_key, w_value, w_out, ffn_gain, w_gate, w_up, w_down):
    section = lax.axis_index("section")
    z_index, core = lax.axis_index("z"), lax.axis_index("core")
    plane = ("dp", "z", "core")
    group = tokens.shape[0]
    local = tokens.shape[1]
    block_range = jnp.stack([2 - core, 2 * z_index + 2]).astype(jnp.int32)

    def mine(array_in):
        return lax.dynamic_index_in_dim(array_in, section, 0, keepdims=False)

    rows = tokens.shape[1]
    shard_rows = w_query.shape[1]
    ff_rows = w_down.shape[1]
    half = ff_rows // 2
    qkvo = jnp.concatenate([w_query[0], w_key[0], w_value[0], w_out[0]], -1)
    down = jnp.concatenate([w_down[0, :half], jnp.zeros((half, 64), BF), w_down[0, half:], jnp.zeros((half, 576), BF)], -1)
    gains = jnp.concatenate([attn_gain, ffn_gain], -1)
    shard = jnp.concatenate([qkvo, w_gate[0], w_up[0], down], 0)
    shard = lax.dynamic_update_slice(shard, gains, (3 * shard_rows, 2048))
    other = swap(shard, "section")

    def assemble(block):
        whole = lax.all_gather(block, plane, axis=0)
        n = shard_rows

        def piece(lo, hi):
            return whole[:, lo : lo + n, :hi].reshape(-1, hi) if hi <= FF else None

        attn = whole[:, :n, :].reshape(n * whole.shape[0], FF)
        w_g = whole[:, n : 2 * n, :].reshape(-1, FF)
        w_u = whole[:, 2 * n : 3 * n, :].reshape(-1, FF)
        w_d = jnp.concatenate([whole[:, 3 * n :, :D], whole[:, 3 * n :, 1024 : 1024 + D]], 1).reshape(-1, D)
        gain_rows = whole[:, 3 * n, 2048 : 2048 + 2 * n].astype(F32)
        gain_a = gain_rows[:, :n].reshape(-1)
        gain_f = gain_rows[:, n:].reshape(-1)
        return gain_a, attn[:, : D + 2 * KV * HD], attn[:, D + 2 * KV * HD :], gain_f, w_g, w_u, w_d

    w0 = assemble(jnp.where(section == 0, shard, other))
    w1 = assemble(jnp.where(section == 1, shard, other))
    tables = rope_tables(mine(positions))
    out0, saved0 = layer_forward(mine(tokens).astype(F32), tables, w0, block_range)
    out1, saved1 = layer_forward(out0.astype(F32), tables, w1, block_range)
    d1, g1 = layer_backward(mine(cotangent), saved1, tables, w1, block_range)
    d1_low = d1.astype(BF)
    d0, g0 = layer_backward(d1_low, saved0, tables, w0, block_range)

    def pair(own, got):
        return jnp.where(section == 0, jnp.stack([own, got]), jnp.stack([got, own]))

    got = swap(jnp.where(section == 0, out1, out0), "section")
    section_out = pair(jnp.where(section == 0, out0, out1), got)
    got = swap(jnp.where(section == 0, d1_low, d0.astype(BF)), "section").astype(F32)
    input_grad = pair(jnp.where(section == 0, d0, d1_low.astype(F32)), got)

    def reduce(first, second):
        def scatter(part):
            return lax.psum_scatter(part, plane, scatter_dimension=0, tiled=True)

        s0, s1 = scatter(first), scatter(second)
        got = swap(jnp.where(section == 0, s1, s0), "section")
        return jnp.where(section == 0, s0, s1).astype(F32) + got.astype(F32)

    grads = {name: reduce(g0[name], g1[name]) for name in ("gate", "up", "down", "out", "qkv")}
    gain_grad = reduce(g0["gains"].T, g1["gains"].T)
    qkv = grads["qkv"]
    kd = KV * HD
    outs = (
        section_out,
        input_grad,
        gain_grad[:, 0],
        qkv[:, :D],
        qkv[:, D : D + kd],
        qkv[:, D + kd :],
        grads["out"],
        gain_grad[:, 1],
        grads["gate"],
        grads["up"],
        grads["down"],
    )
    return tuple(part[None] for part in outs)


LANES = 128
PADDED = 1024
CHUNK = 640
WIDE = 512
KVW = 2 * KV * HD
QKV_BLOCKS = 13
EXTRA = 16
ACTS = FF + 3 * PADDED
BACK = 2 * FF + 2 * PADDED
OUT_BLOCKS = PADDED // LANES
FF_BLOCKS = FF // LANES
VMEM = pl.BlockSpec(memory_space=pltpu.VMEM)
ANY = pl.BlockSpec(memory_space=pl.ANY)
SMEM = pl.BlockSpec(memory_space=pltpu.SMEM)
BIG = pltpu.CompilerParams(vmem_limit_bytes=56 << 20)


def cost(microseconds):
    return pl.CostEstimate(flops=int(microseconds * 1.15e9), bytes_accessed=int(microseconds * 3.69e6), transcendentals=0)


def dot_nt(left, right):
    return lax.dot_general(left, right, (((1,), (1,)), ((), ())), preferred_element_type=F32)


def columns(ref, first, count, rows):
    parts = [
        ref[:, first + i * rows : first + (i + 1) * rows, :].reshape(-1, LANES) for i in range(count)
    ]
    return parts[0] if count == 1 else jnp.concatenate(parts, 1)


def half_of(values):
    lane = lax.broadcasted_iota(jnp.int32, values.shape, 1)
    back = pltpu.roll(values, LANES - HD // 2, 1)
    ahead = pltpu.roll(values, HD // 2, 1)
    return jnp.where(lane % HD < HD // 2, -back, ahead)


def rms(values):
    return lax.rsqrt(jnp.sum(values * values, -1, keepdims=True) / D + EPS)


def norm_back(grad, values, gain):
    factor = rms(values)
    scaled = grad * gain
    mean = jnp.sum(scaled * values, -1, keepdims=True) / D
    back = factor * scaled - values * (factor * factor * factor * mean)
    return back, jnp.sum(grad * values * factor, 0, keepdims=True)


def load_kv(blocks, other, kv_s, sems):
    copies = [pltpu.make_async_copy(block, kv_s.at[0, d], sems.at[d]) for d, block in enumerate(blocks)]
    copies.append(pltpu.make_async_copy(other, kv_s.at[1], sems.at[len(blocks)]))
    for copy in copies:
        copy.start()
    return copies


def attend_kernel(zs, rng, q_ref, *refs):
    blocks, (other, e_hbm, o_ref, op_ref, lse_ref, kv_s, qt, vt, m_s, l_s, acc, e_s, sems) = refs[:zs], refs[zs:]
    T = q_ref.shape[0]
    W = G * T
    copies = load_kv(blocks, other, kv_s, sems)
    spread = pltpu.make_async_copy(e_hbm, e_s, sems.at[zs + 1])
    spread.start()
    qt[...] = q_ref[...].astype(F32).T.astype(BF)
    for copy in copies:
        copy.wait()

    def step(b, first):
        kv = kv_s.at[lax.rem(b, 2), lax.div(b, 2)] if not first else kv_s.at[0, 0]
        vt[...] = kv[:, KV * HD :].astype(F32).T.astype(BF)
        ats = [slice(g * HD, (g + 1) * HD) for g in range(KV)]
        scores = []
        for g in range(KV):
            qg = jnp.concatenate([qt[(g * G + j) * HD : (g * G + j + 1) * HD, :] for j in range(G)], 1)
            s = dot(kv[:, ats[g]], qg)
            if first:
                key = lax.broadcasted_iota(jnp.int32, (T, W), 0)
                query = lax.broadcasted_iota(jnp.int32, (T, W), 1) % T
                s = jnp.where(key <= query, s, -1e30)
            scores.append(s)
        probs, scales = [], []
        for g in range(KV):
            top = jnp.max(scores[g], 0, keepdims=True)
            if not first:
                old = m_s[g : g + 1, :]
                top = jnp.maximum(old, top)
                scales.append(jnp.exp(old - top))
            p = jnp.exp(scores[g] - top)
            total = jnp.sum(p, 0, keepdims=True)
            l_s[g : g + 1, :] = total if first else l_s[g : g + 1, :] * scales[g] + total
            m_s[g : g + 1, :] = top
            probs.append(p.astype(BF))
        for g in range(KV):
            out = dot(vt[ats[g], :], probs[g])
            acc[ats[g], :] = out if first else acc[ats[g], :] * scales[g] + out

    step(0, True)

    def body(b, _):
        step(b, False)
        return 0

    lax.fori_loop(rng[0], rng[1], body, 0)
    for g in range(KV):
        lse_ref[g : g + 1, :] = m_s[g : g + 1, :] + jnp.log(l_s[g : g + 1, :])
        og = acc[g * HD : (g + 1) * HD, :] / l_s[g : g + 1, :]
        for j in range(G):
            h = g * G + j
            o_ref[:, h * HD : (h + 1) * HD] = og[:, j * T : (j + 1) * T].T.astype(BF)
    spread.wait()
    op_ref[...] = dot(o_ref[...], e_s[...]).astype(BF)


def attend(rng, q, kv_all, e):
    blocks, other = kv_all
    T, zs = q.shape[0], len(blocks)
    W = G * T
    return pl.pallas_call(
        functools.partial(attend_kernel, zs),
        out_shape=(
            jax.ShapeDtypeStruct((T, D), BF),
            jax.ShapeDtypeStruct((T, PADDED), BF),
            jax.ShapeDtypeStruct((KV, W), F32),
        ),
        in_specs=[SMEM, VMEM] + [ANY] * (zs + 2),
        out_specs=[VMEM] * 3,
        scratch_shapes=[
            pltpu.VMEM((2, zs, T, KVW), BF),
            pltpu.VMEM((D, T), BF),
            pltpu.VMEM((KV * HD, T), BF),
            pltpu.VMEM((KV, W), F32),
            pltpu.VMEM((KV, W), F32),
            pltpu.VMEM((KV * HD, W), F32),
            pltpu.VMEM((D, PADDED), BF),
            pltpu.SemaphoreType.DMA((zs + 2,)),
        ],
        compiler_params=BIG,
        cost_estimate=cost(24),
        name="attend",
    )(rng, q, *blocks, other, e)


def attend_back_kernel(zs, rng, q_ref, o_ref, do_ref, lse_ref, cos_ref, sin_ref, *refs):
    blocks, (other, dq_ref, own_ref, send_ref, kv_s, qt, dot_, qn, don, kt, dl, dqa, sems, dkv_ref, out_sems) = (
        refs[:zs],
        refs[zs:],
    )
    T = q_ref.shape[0]
    W = G * T
    copies = load_kv(blocks, other, kv_s, sems)
    qt[...] = q_ref[...].astype(F32).T.astype(BF)
    do_t = do_ref[...].astype(F32).T
    dot_[...] = do_t.astype(BF)
    prod = do_t * o_ref[...].astype(F32).T
    for h in range(H):
        g, j = divmod(h, G)
        rows = slice(j * T, (j + 1) * T)
        dl[g : g + 1, rows] = jnp.sum(prod[h * HD : (h + 1) * HD, :], 0, keepdims=True)
        qn[g, rows, :] = q_ref[:, h * HD : (h + 1) * HD]
        don[g, rows, :] = do_ref[:, h * HD : (h + 1) * HD]
    for copy in copies:
        copy.wait()

    def step(b, first):
        side, far = (0, 0) if first else (lax.rem(b, 2), lax.div(b, 2))
        kv = kv_s.at[side, far]
        out = dkv_ref.at[side, far]
        kt[...] = kv[:, : KV * HD].astype(F32).T.astype(BF)
        for g in range(KV):
            at = slice(g * HD, (g + 1) * HD)
            vat = slice((KV + g) * HD, (KV + g + 1) * HD)
            heads = [slice((g * G + j) * HD, (g * G + j + 1) * HD) for j in range(G)]
            s = dot(kv[:, at], jnp.concatenate([qt[h, :] for h in heads], 1))
            p = jnp.exp(s - lse_ref[g : g + 1, :])
            if first:
                key = lax.broadcasted_iota(jnp.int32, (T, W), 0)
                query = lax.broadcasted_iota(jnp.int32, (T, W), 1) % T
                p = jnp.where(key <= query, p, 0.0)
            dp = dot(kv[:, vat], jnp.concatenate([dot_[h, :] for h in heads], 1))
            dz = (p * (dp - dl[g : g + 1, :])).astype(BF)
            out[:, vat] = dot(p.astype(BF), don[g]).astype(BF)
            out[:, at] = dot(dz, qn[g]).astype(BF)
            dq = dot(kt[at, :], dz)
            if first:
                dqa[at, :] = dq
            else:
                dqa[at, :] += dq

    step(0, True)

    def body(b, _):
        step(b, False)
        return 0

    def zero(b, _):
        dkv_ref[lax.rem(b, 2), lax.div(b, 2)] = jnp.zeros((T, KVW), BF)
        return 0

    lax.fori_loop(rng[0], rng[1], body, 0)
    lax.fori_loop(1, rng[0], zero, 0)
    lax.fori_loop(rng[1], 2 * zs, zero, 0)
    cos, sin = cos_ref[...], sin_ref[...]
    for pair in range(PADDED // LANES):
        parts = []
        for h in (2 * pair, 2 * pair + 1):
            g, j = divmod(h, G)
            if h < H:
                parts.append(dqa[g * HD : (g + 1) * HD, j * T : (j + 1) * T] * HD**-0.5)
            else:
                parts.append(jnp.zeros((HD, T), F32))
        grad = jnp.concatenate(parts, 0).T
        turned = grad * cos - half_of(grad * sin)
        dq_ref[:, pair * LANES : (pair + 1) * LANES] = turned.astype(BF)
    kv_s[0, 0] = dq_ref[:, :KVW]
    kv_s[0, 1, :, : PADDED - KVW] = dq_ref[:, KVW:]
    copies = [
        pltpu.make_async_copy(dkv_ref.at[0], own_ref, out_sems.at[0]),
        pltpu.make_async_copy(dkv_ref.at[1], send_ref.at[pl.ds(0, zs)], out_sems.at[1]),
        pltpu.make_async_copy(kv_s.at[0, pl.ds(0, 2)], send_ref.at[pl.ds(zs, 2)], out_sems.at[2]),
    ]
    for copy in copies:
        copy.start()
    for copy in copies:
        copy.wait()


def attend_back(rng, q, o, do, lse, cos, sin, kv_all):
    blocks, other = kv_all
    T, zs = q.shape[0], len(blocks)
    W = G * T
    return pl.pallas_call(
        functools.partial(attend_back_kernel, zs),
        out_shape=(
            jax.ShapeDtypeStruct((T, PADDED), BF),
            jax.ShapeDtypeStruct((zs, T, KVW), BF),
            jax.ShapeDtypeStruct((zs + 2, T, KVW), BF),
        ),
        in_specs=[SMEM] + [VMEM] * 6 + [ANY] * (zs + 1),
        out_specs=[VMEM, ANY, ANY],
        scratch_shapes=[
            pltpu.VMEM((2, zs, T, KVW), BF),
            pltpu.VMEM((D, T), BF),
            pltpu.VMEM((D, T), BF),
            pltpu.VMEM((KV, W, HD), BF),
            pltpu.VMEM((KV, W, HD), BF),
            pltpu.VMEM((KV * HD, T), BF),
            pltpu.VMEM((KV, W), F32),
            pltpu.VMEM((KV * HD, W), F32),
            pltpu.SemaphoreType.DMA((zs + 1,)),
            pltpu.VMEM((2, zs, T, KVW), BF),
            pltpu.SemaphoreType.DMA((3,)),
        ],
        compiler_params=BIG,
        cost_estimate=cost(24),
        name="attend_back",
    )(rng, q, o, do, lse, cos, sin, *blocks, other)


def spread_kv(block):
    blocks = [block] + [move_z(block, d) for d in range(1, lax.axis_size("z"))]
    return blocks, swap(jnp.stack(blocks), "core")


def collect_kv(grads, got, before=()):
    count = lax.axis_size("z")
    moving = plus(grads[count - 1], got[count - 1])
    for d in range(count - 2, -1, -1):
        moving = after(moving, *before[d]) if d < len(before) else moving
        moved = move_z(moving, -1)
        own = plus(grads[d], got[d])
        if d == 0:
            return [own, moved], moving
        moving = plus(own, moved)


def qkv_kernel(base, x_ref, gain_ref, cos_ref, sin_ref, w_hbm, na_ref, q_ref, kv_ref, w_s, sem):
    rows = w_s.shape[1] // QKV_BLOCKS
    copy = pltpu.make_async_copy(w_hbm.at[:, pl.ds(base, w_s.shape[1]), :], w_s, sem)
    copy.start()
    x = x_ref[...].astype(F32)
    normed = (x * rms(x) * gain_ref[...]).astype(BF)
    na_ref[...] = normed
    copy.wait()
    cos, sin = cos_ref[...], sin_ref[...]
    for j in range(QKV_BLOCKS):
        out = dot(normed, columns(w_s, j * rows, 1, rows))
        if j < 5:
            turned = out * cos + half_of(out) * sin if j < 3 else out
            if j == 2:
                lane = lax.broadcasted_iota(jnp.int32, out.shape, 1)
                turned = jnp.where(lane < HD, turned, out)
            kv_ref[:, j * LANES : (j + 1) * LANES] = turned.astype(BF)
        else:
            turned = (out * cos + half_of(out) * sin).astype(BF) * BF(HD**-0.5)
            at = (j - 5) * LANES
            width = min(LANES, D - at)
            q_ref[:, at : at + width] = turned[:, :width]


def qkv_forward(x, gain, cos, sin, weights, base):
    count = x.shape[0]
    shards = weights.shape[0]
    rows = PADDED // shards
    return pl.pallas_call(
        functools.partial(qkv_kernel, base),
        out_shape=(
            jax.ShapeDtypeStruct((count, PADDED), BF),
            jax.ShapeDtypeStruct((count, D), BF),
            jax.ShapeDtypeStruct((count, KVW), BF),
        ),
        in_specs=[VMEM] * 4 + [ANY],
        out_specs=[VMEM] * 3,
        scratch_shapes=[pltpu.VMEM((shards, QKV_BLOCKS * rows, LANES), BF), pltpu.SemaphoreType.DMA],
        compiler_params=BIG,
        cost_estimate=cost(6),
        name="qkv_forward",
    )(x, gain, cos, sin, weights)


def weight_copies(w_hbm, w_s, sems, first):
    shards = w_hbm.shape[0]
    rows, ff_rows = PADDED // shards, FF // shards
    gate = OUT_BLOCKS * rows
    up = gate + FF_BLOCKS * rows
    down = up + FF_BLOCKS * rows
    step = WIDE // LANES * rows
    everyone = pl.ds(0, shards)
    places = [(everyone, 0, gate)]
    places += [(everyone, at + i * step, step) for i in range(FF // WIDE) for at in (gate, up)]
    places += [(pl.ds(h * shards // 2, shards // 2), down, OUT_BLOCKS * ff_rows) for h in range(2)]
    copies = []
    for i, (who, at, height) in enumerate(places):
        source, target = w_hbm.at[who, pl.ds(first + at, height), :], w_s.at[who, pl.ds(at, height), :]
        copies.append(pltpu.make_async_copy(source, target, sems.at[i]))
    pairs = [copies[1 + 2 * i : 3 + 2 * i] for i in range(FF // WIDE)]
    return copies[0], pairs, copies[-2:]


def gate_up(w_s, i):
    rows = PADDED // w_s.shape[0]
    at = OUT_BLOCKS * rows + i * (WIDE // LANES) * rows
    return [columns(w_s, at + j * FF_BLOCKS * rows, WIDE // LANES, rows) for j in range(2)]


def down_half(w_s, h):
    shards = w_s.shape[0]
    rows, ff_rows = PADDED // shards, FF // shards
    at = (OUT_BLOCKS + 2 * FF_BLOCKS) * rows
    who = slice(h * shards // 2, (h + 1) * shards // 2)
    parts = [w_s[who, at + i * ff_rows : at + (i + 1) * ff_rows, :].reshape(-1, LANES) for i in range(OUT_BLOCKS)]
    return jnp.concatenate(parts, 1)


def ffn_up(x, op, na, gain, w_s, acts, loads):
    out, pairs, downs = loads
    rows = PADDED // w_s.shape[0]
    acts[:, FF : FF + PADDED] = op
    acts[:, FF + 2 * PADDED :] = na
    out.wait()
    mixed = x.astype(F32) + dot(op, columns(w_s, 0, OUT_BLOCKS, rows))
    normed = (mixed * rms(mixed) * gain).astype(BF)
    acts[:, FF + PADDED : FF + 2 * PADDED] = normed
    gates = []
    for i in range(FF // WIDE):
        for copy in pairs[i]:
            copy.wait()
        gate, up = gate_up(w_s, i)
        g, u = dot(normed, gate), dot(normed, up)
        acts[:, i * WIDE : (i + 1) * WIDE] = (g * jax.nn.sigmoid(g) * u).astype(BF)
        gates.append((g.astype(BF), u.astype(BF)))
    return mixed, gates


def ffn_down(mixed, w_s, acts, downs):
    total = mixed
    for h in range(2):
        downs[h].wait()
        total = total + dot(acts[:, h * FF // 2 : (h + 1) * FF // 2], down_half(w_s, h))
    return total.astype(BF)


def ffn_kernel(first, op_ref, x_ref, na_ref, gain_ref, w_hbm, acts_hbm, m_ref, gu_hbm, y_ref, w_s, acts, gu, sems, outs):
    loads = weight_copies(w_hbm, w_s, sems, first)
    for copy in [loads[0]] + sum(loads[1], []) + loads[2]:
        copy.start()
    mixed, gates = ffn_up(x_ref[...], op_ref[...], na_ref[...], gain_ref[...], w_s, acts, loads)
    m_ref[...] = mixed
    for i, pair in enumerate(gates):
        for j in range(2):
            gu[j, :, i * WIDE : (i + 1) * WIDE] = pair[j]
    sends = [pltpu.make_async_copy(acts, acts_hbm, outs.at[0]), pltpu.make_async_copy(gu, gu_hbm, outs.at[1])]
    for copy in sends:
        copy.start()
    y_ref[...] = ffn_down(mixed, w_s, acts, loads[2])
    for copy in sends:
        copy.wait()


def ffn_forward(op, x, na, gain, weights, first):
    count = x.shape[0]
    shards = weights.shape[0]
    later = (OUT_BLOCKS + 2 * FF_BLOCKS) * (PADDED // shards) + OUT_BLOCKS * (FF // shards)
    return pl.pallas_call(
        functools.partial(ffn_kernel, first),
        out_shape=(
            jax.ShapeDtypeStruct((count, ACTS), BF),
            jax.ShapeDtypeStruct((count, PADDED), F32),
            jax.ShapeDtypeStruct((2, count, FF), BF),
            jax.ShapeDtypeStruct((count, PADDED), BF),
        ),
        in_specs=[VMEM] * 4 + [ANY],
        out_specs=[ANY, VMEM, ANY, VMEM],
        scratch_shapes=[
            pltpu.VMEM((shards, later, LANES), BF),
            pltpu.VMEM((count, ACTS), BF),
            pltpu.VMEM((2, count, FF), BF),
            pltpu.SemaphoreType.DMA((3 + 2 * (FF // WIDE),)),
            pltpu.SemaphoreType.DMA((2,)),
        ],
        compiler_params=BIG,
        cost_estimate=cost(9),
        name="ffn_forward",
    )(op, x, na, gain, weights)


def ffn_back_body(dy, mixed, gain, gates, e_s, w_s, back, loads, spread):
    out, pairs, downs = loads
    rows = PADDED // w_s.shape[0]
    back[:, 2 * FF + PADDED :] = dy
    for h in range(2):
        downs[h].wait()
        at = h * FF // 2
        d_hidden = dot_nt(dy, down_half(w_s, h))
        g, u = (part.astype(F32) for part in gates(h))
        sig = jax.nn.sigmoid(g)
        back[:, at : at + FF // 2] = (d_hidden * u * sig * (1.0 + g * (1.0 - sig))).astype(BF)
        back[:, FF + at : FF + at + FF // 2] = (d_hidden * g * sig).astype(BF)
    grad = None
    for i in range(FF // WIDE):
        for copy in pairs[i]:
            copy.wait()
        gate, up = gate_up(w_s, i)
        part = dot_nt(back[:, i * WIDE : (i + 1) * WIDE], gate) + dot_nt(back[:, FF + i * WIDE : FF + (i + 1) * WIDE], up)
        grad = part if grad is None else grad + part
    norm, dgain = norm_back(grad, mixed, gain)
    d_mixed = dy.astype(F32) + norm
    low = d_mixed.astype(BF)
    back[:, 2 * FF : 2 * FF + PADDED] = low
    out.wait()
    d_padded = dot_nt(low, columns(w_s, 0, OUT_BLOCKS, rows)).astype(BF)
    spread.wait()
    return d_mixed, dgain, dot_nt(d_padded, e_s[...]).astype(BF)


class Loaded:
    def wait(self):
        pass


def turn_acts(core, acts, own_ref, send_ref):
    at, to = 0, 0
    for width in (FF, PADDED, PADDED, PADDED):
        turned = acts[:, at : at + width].astype(F32).T.astype(BF)
        own, send = own_rows(turned, core, width // 16)
        own_ref[to : to + width // 2, :] = own
        send_ref[to : to + width // 2, :] = send
        at, to = at + width, to + width // 2


def ffn_both_kernel(first, place, op_ref, x_ref, na_ref, gain_ref, dy_ref, e_hbm, w_hbm, *refs):
    y_ref, own_ref, send_ref, back_hbm, dm_ref, do_ref, dgain_ref, w_s, acts, gu, back, e_s, sems, others = refs
    loads = weight_copies(w_hbm, w_s, sems, first)
    spread = pltpu.make_async_copy(e_hbm, e_s, others.at[0])
    for copy in [loads[0]] + sum(loads[1], []) + loads[2] + [spread]:
        copy.start()
    mixed, gates = ffn_up(x_ref[...], op_ref[...], na_ref[...], gain_ref[...], w_s, acts, loads)
    for i, pair in enumerate(gates):
        for j in range(2):
            gu[j, :, i * WIDE : (i + 1) * WIDE] = pair[j]
    y_ref[...] = ffn_down(mixed, w_s, acts, loads[2])
    done = Loaded()
    loads = (done, [[done, done]] * (FF // WIDE), [done, done])
    halves = lambda h: [gu[j, :, h * FF // 2 : (h + 1) * FF // 2] for j in range(2)]
    dm_ref[...], dgain_ref[...], do_ref[...] = ffn_back_body(
        dy_ref[...], mixed, gain_ref[...], halves, e_s, w_s, back, loads, spread
    )
    send = pltpu.make_async_copy(back, back_hbm, others.at[1])
    send.start()
    turn_acts(place[0], acts, own_ref, send_ref)
    send.wait()


def ffn_both(place, op, x, na, gain, dy, e, weights, first):
    count = x.shape[0]
    shards = weights.shape[0]
    later = (OUT_BLOCKS + 2 * FF_BLOCKS) * (PADDED // shards) + OUT_BLOCKS * (FF // shards)
    turned = jax.ShapeDtypeStruct((ACTS // 2, count), BF)
    return pl.pallas_call(
        functools.partial(ffn_both_kernel, first),
        out_shape=(
            jax.ShapeDtypeStruct((count, PADDED), BF),
            turned,
            turned,
            jax.ShapeDtypeStruct((count, BACK), BF),
            jax.ShapeDtypeStruct((count, PADDED), F32),
            jax.ShapeDtypeStruct((count, D), BF),
            jax.ShapeDtypeStruct((1, PADDED), F32),
        ),
        in_specs=[SMEM] + [VMEM] * 5 + [ANY] * 2,
        out_specs=[VMEM] * 3 + [ANY] + [VMEM] * 3,
        scratch_shapes=[
            pltpu.VMEM((shards, later, LANES), BF),
            pltpu.VMEM((count, ACTS), BF),
            pltpu.VMEM((2, count, FF), BF),
            pltpu.VMEM((count, BACK), BF),
            pltpu.VMEM((D, PADDED), BF),
            pltpu.SemaphoreType.DMA((3 + 2 * (FF // WIDE),)),
            pltpu.SemaphoreType.DMA((2,)),
        ],
        compiler_params=BIG,
        cost_estimate=cost(20),
        name="ffn_both",
    )(place, op, x, na, gain, dy, e, weights)


def both_back_kernel(base, first, zs, dq_ref, cos_ref, sin_ref, x_ref, gain_ref, dm_ref, *refs):
    shares, refs = refs[:zs], refs[zs:]
    dgf_ref, m_ref, gain_f_ref, gu_hbm, e_hbm, wa_hbm, wf_hbm = refs[:7]
    dkv_ref, low_ref, back_hbm, dm_out, do_ref, dgain_ref, wa_s, wf_s, back, gu, e_s, sem, sems, others = refs[7:]
    copy = pltpu.make_async_copy(wa_hbm.at[:, pl.ds(base, wa_s.shape[1]), :], wa_s, sem)
    loads = weight_copies(wf_hbm, wf_s, sems, first)
    load = pltpu.make_async_copy(gu_hbm, gu, others.at[0])
    spread = pltpu.make_async_copy(e_hbm, e_s, others.at[1])
    for each in [copy] + loads[2] + [load] + sum(loads[1], []) + [loads[0], spread]:
        each.start()
    dx = qkv_back_body(dq_ref, shares, cos_ref[...], sin_ref[...], x_ref, gain_ref, dm_ref, dgf_ref, copy, wa_s, dkv_ref)
    low = dx.astype(BF)
    low_ref[...] = low
    load.wait()
    halves = lambda h: [gu[j, :, h * FF // 2 : (h + 1) * FF // 2] for j in range(2)]
    dm_out[...], dgain_ref[...], do_ref[...] = ffn_back_body(
        low, m_ref[...], gain_f_ref[...], halves, e_s, wf_s, back, loads, spread
    )
    send = pltpu.make_async_copy(back, back_hbm, others.at[2])
    send.start()
    send.wait()


def both_back(dq, shares, cos, sin, x, gain, dm, dgf, w_a, base, mixed, gain_f, gu, e, w_f, first):
    count = x.shape[0]
    shards = w_a.shape[0]
    rows = PADDED // shards
    later = (OUT_BLOCKS + 2 * FF_BLOCKS) * rows + OUT_BLOCKS * (FF // shards)
    return pl.pallas_call(
        functools.partial(both_back_kernel, base, first, len(shares)),
        out_shape=(
            jax.ShapeDtypeStruct((count + EXTRA, KVW), BF),
            jax.ShapeDtypeStruct((count, PADDED), BF),
            jax.ShapeDtypeStruct((count, BACK), BF),
            jax.ShapeDtypeStruct((count, PADDED), F32),
            jax.ShapeDtypeStruct((count, D), BF),
            jax.ShapeDtypeStruct((1, PADDED), F32),
        ),
        in_specs=[VMEM] * (9 + len(shares)) + [ANY] * 4,
        out_specs=[VMEM, VMEM, ANY] + [VMEM] * 3,
        scratch_shapes=[
            pltpu.VMEM((shards, QKV_BLOCKS * rows, LANES), BF),
            pltpu.VMEM((shards, later, LANES), BF),
            pltpu.VMEM((count, BACK), BF),
            pltpu.VMEM((2, count, FF), BF),
            pltpu.VMEM((D, PADDED), BF),
            pltpu.SemaphoreType.DMA,
            pltpu.SemaphoreType.DMA((3 + 2 * (FF // WIDE),)),
            pltpu.SemaphoreType.DMA((3,)),
        ],
        compiler_params=BIG,
        cost_estimate=cost(18),
        name="both_back",
    )(dq, cos, sin, x, gain, dm, *shares, dgf, mixed, gain_f, gu, e, w_a, w_f)


def qkv_back_body(dq_ref, shares, cos, sin, x_ref, gain_ref, dm_ref, dgf_ref, copy, w_s, dkv_ref):
    count = x_ref.shape[0]
    rows = w_s.shape[1] // QKV_BLOCKS
    for j in range(KVW // LANES):
        at = slice(j * LANES, (j + 1) * LANES)
        grad = shares[0][:, at].astype(F32)
        for share in shares[1:]:
            grad = grad + share[:, at].astype(F32)
        turned = grad * cos - half_of(grad * sin) if j < 3 else grad
        if j == 2:
            lane = lax.broadcasted_iota(jnp.int32, grad.shape, 1)
            turned = jnp.where(lane < HD, turned, grad)
        dkv_ref[:count, at] = turned.astype(BF)
    copy.wait()
    kv_blocks = KVW // LANES
    d_normed = dot_nt(dkv_ref[:count, :], columns(w_s, 0, kv_blocks, rows))
    d_normed = d_normed + dot_nt(dq_ref[...], columns(w_s, kv_blocks * rows, QKV_BLOCKS - kv_blocks, rows))
    back, dgain = norm_back(d_normed, x_ref[...].astype(F32), gain_ref[...])
    dkv_ref[count:, :] = gain_rows(dgain, dgf_ref[...])
    return dm_ref[...] + back


def qkv_back_kernel(base, zs, dq_ref, cos_ref, sin_ref, x_ref, gain_ref, dm_ref, *refs):
    shares, (dgf_ref, w_hbm, dkv_ref, dx_ref, low_ref, w_s, sem) = refs[:zs], refs[zs:]
    copy = pltpu.make_async_copy(w_hbm.at[:, pl.ds(base, w_s.shape[1]), :], w_s, sem)
    copy.start()
    dx = qkv_back_body(dq_ref, shares, cos_ref[...], sin_ref[...], x_ref, gain_ref, dm_ref, dgf_ref, copy, w_s, dkv_ref)
    dx_ref[...] = dx
    low_ref[...] = dx.astype(BF)


def gain_rows(first, second):
    half = PADDED // 2
    rows = [first[:, :half], first[:, half:], second[:, :half], second[:, half:]]
    rows = jnp.concatenate(rows + [jnp.zeros((EXTRA - 4, half), F32)], 0)
    return jnp.concatenate([rows, jnp.zeros((EXTRA, KVW - half), F32)], 1).astype(BF)


def gain_columns(own, other):
    total = own.astype(F32) + other.astype(F32)
    half = PADDED // 2
    rows = [jnp.concatenate([total[2 * i : 2 * i + 1, :half], total[2 * i + 1 : 2 * i + 2, :half]], 1) for i in range(2)]
    return jnp.concatenate(rows + [jnp.zeros((LANES - 2, PADDED), F32)], 0).T.astype(BF)


def qkv_backward(dq, shares, cos, sin, x, gain, dm, dgf, weights, base):
    count = x.shape[0]
    shards = weights.shape[0]
    rows = PADDED // shards
    return pl.pallas_call(
        functools.partial(qkv_back_kernel, base, len(shares)),
        out_shape=(
            jax.ShapeDtypeStruct((count + EXTRA, KVW), BF),
            jax.ShapeDtypeStruct((count, PADDED), F32),
            jax.ShapeDtypeStruct((count, PADDED), BF),
        ),
        in_specs=[VMEM] * (7 + len(shares)) + [ANY],
        out_specs=[VMEM] * 3,
        scratch_shapes=[pltpu.VMEM((shards, QKV_BLOCKS * rows, LANES), BF), pltpu.SemaphoreType.DMA],
        compiler_params=BIG,
        cost_estimate=cost(6),
        name="qkv_backward",
    )(dq, cos, sin, x, gain, dm, *shares, dgf, weights)


def own_rows(turned, core, rows):
    split = turned.reshape(-1, 2, rows, turned.shape[-1])
    first, second = split[:, 0].reshape(-1, turned.shape[-1]), split[:, 1].reshape(-1, turned.shape[-1])
    return jnp.where(core == 0, first, second), jnp.where(core == 0, second, first)


def turn_kernel(place, acts_ref, own_ref, send_ref):
    turn_acts(place[0], acts_ref, own_ref, send_ref)


def turn(place, acts):
    shape = jax.ShapeDtypeStruct((ACTS // 2, acts.shape[0]), BF)
    return pl.pallas_call(
        turn_kernel,
        out_shape=(shape, shape),
        in_specs=[SMEM, VMEM],
        out_specs=[VMEM] * 2,
        compiler_params=BIG,
        cost_estimate=cost(4),
        name="turn",
    )(place, acts)


def write_split(out, keep_ref, send_ref, at, rows, half):
    for i in range(out.shape[1] // LANES):
        block = out[:, i * LANES : (i + 1) * LANES].reshape(2, -1, rows, LANES)
        place = slice(at + i * rows, at + (i + 1) * rows)
        keep_ref[:, place, :] = jnp.where(half == 0, block[0], block[1])
        send_ref[:, place, :] = jnp.where(half == 0, block[1], block[0])


def grad_ffn_kernel(place, own_hbm, other_hbm, back_hbm, back_other_hbm, *refs):
    outs, (left, back, *held, sems, out_sems) = refs[:8], refs[8:]
    keep_a, send_a, keep_u, send_u = held[:2], held[2:4], held[4:6], held[6:8]
    half, section = place[1], place[2]
    count = back.shape[0] // 2
    chips = keep_a[0].shape[0]
    rows, ff_rows = PADDED // (2 * chips), FF // (2 * chips)
    steps = FF // CHUNK
    hd, op, nf = (0, FF // 2), (FF // 2, PADDED // 2), ((FF + PADDED) // 2, PADDED // 2)
    loads = []

    def load(at, width, height, first):
        group = []
        for side, (turned, wide) in enumerate(((own_hbm, back_hbm), (other_hbm, back_other_hbm))):
            place_l = (pl.ds(height[0], height[1]), pl.ds(side * count, count))
            place_b = (pl.ds(side * count, count), pl.ds(at, width))
            if first:
                group.append(pltpu.make_async_copy(turned.at[place_l[0], :], left.at[place_l], sems.at[4 * len(loads) + 2 * side]))
            group.append(pltpu.make_async_copy(wide.at[:, place_b[1]], back.at[place_b], sems.at[4 * len(loads) + 2 * side + 1]))
        loads.append(group)
        for copy in group:
            copy.start()

    load(0, FF, nf, True)
    load(2 * FF + PADDED, PADDED, hd, True)
    load(FF, FF, nf, False)
    load(2 * FF, PADDED, op, True)

    def ready(i):
        for copy in loads[i]:
            copy.wait()

    def product(which, at, width):
        return dot(left[which[0] : which[0] + which[1], :], back[:, at : at + width]).astype(BF)

    def as_blocks(out, height):
        width = out.shape[1] // LANES
        return [out[:, i * LANES : (i + 1) * LANES].reshape(chips, height, LANES) for i in range(width)]

    sent = []

    def finish(*which):
        for i in which:
            sent.append(pltpu.make_async_copy(held[i], outs[i], out_sems.at[i]))
            sent[-1].start()

    ready(0)
    ready(1)
    block = CHUNK // LANES * rows
    narrow_width = PADDED // steps
    for j in range(steps):
        gate = jnp.concatenate(as_blocks(product(nf, j * CHUNK, CHUNK), rows), 1)
        down = jnp.concatenate(as_blocks(product(hd, 2 * FF + PADDED + j * narrow_width, narrow_width), ff_rows), 1)
        at = slice(j % 2 * block, (j % 2 + 1) * block)
        keep_a[j // 2][:, at, :] = jnp.where(section == 0, down, gate)
        send_a[j // 2][:, at, :] = jnp.where(section == 0, gate, down)
        if j % 2:
            finish(j // 2, 2 + j // 2)
    ready(2)
    for j in range(steps):
        h = j // (steps - 1)
        write_split(product(nf, FF + j * CHUNK, CHUNK), keep_u[h], send_u[h], (j - h * (steps - 1)) * block, rows, half)
        if j == steps - 2:
            finish(4, 6)
    ready(3)
    write_split(product(op, 2 * FF, PADDED), keep_u[1], send_u[1], block, rows, half)
    finish(5, 7)
    for copy in sent:
        copy.wait()


def grad_ffn(place, own, other, back, back_other, shards):
    count = own.shape[1]
    chips = shards // 2
    rows = PADDED // shards
    steps = FF // CHUNK
    block = CHUNK // LANES * rows
    shapes = [(chips, 2 * block, LANES)] * 4
    shapes += [(chips // 2, height, LANES) for height in ((steps - 1) * block, block + OUT_BLOCKS * rows) * 2]
    return pl.pallas_call(
        grad_ffn_kernel,
        out_shape=[jax.ShapeDtypeStruct(shape, BF) for shape in shapes],
        in_specs=[SMEM] + [ANY] * 4,
        out_specs=[ANY] * 8,
        scratch_shapes=[pltpu.VMEM((ACTS // 2, 2 * count), BF), pltpu.VMEM((2 * count, BACK), BF)]
        + [pltpu.VMEM(shape, BF) for shape in shapes]
        + [pltpu.SemaphoreType.DMA((16,)), pltpu.SemaphoreType.DMA((8,))],
        compiler_params=BIG,
        cost_estimate=cost(11),
        name="grad_ffn",
    )(place, own, other, back, back_other)


def grad_attn_kernel(place, own, other, *refs):
    grads, keep, send = refs[:-2], refs[-2], refs[-1]
    core, half = place[0], place[1]
    count = own.shape[1]
    rows = PADDED // 16
    na = slice((FF + 2 * PADDED) // 2, ACTS // 2)
    at = 0
    for grad, grad_other in zip(grads[::2], grads[1::2]):
        if len(grad_other.shape) == 3:
            right = jnp.concatenate([grad_other[0], grad_other[1, :, : PADDED - KVW]], 1)
        else:
            right = grad_other[:count, :]
        out = (dot(own[na, :], grad[:count, :]) + dot(other[na, :], right)).astype(BF)
        write_split(out, keep, send, at, rows, half)
        at += grad.shape[1] // LANES * rows
        if grad.shape[0] > count:
            gains = gain_columns(grad[count:, :], grad_other[count:, :])
            write_split(own_rows(gains, core, rows)[0], keep, send, at, rows, half)
            at += rows


def grad_attn(place, own, other, *grads):
    rows = PADDED // 16
    blocks = sum(grad.shape[1] // LANES + (grad.shape[0] > own.shape[1]) for grad in grads[::2])
    shape = jax.ShapeDtypeStruct((4, blocks * rows, LANES), BF)
    return pl.pallas_call(
        grad_attn_kernel,
        out_shape=(shape, shape),
        in_specs=[SMEM] + [VMEM] * (2 + len(grads)),
        out_specs=[VMEM] * 2,
        compiler_params=BIG,
        cost_estimate=cost(4),
        name="grad_attn",
    )(place, own, other, *grads)


def narrow(values, spread):
    if values.dtype == BF:
        return dot_nt(values, spread)
    total, left = None, values
    for _ in range(3):
        part = left.astype(BF)
        left = left - part.astype(F32)
        out = dot_nt(part, spread)
        total = out if total is None else total + out
    return total


def narrow_t(values, spread):
    if values.dtype == BF:
        return dot_nt(spread, values)
    total, left = None, values
    for _ in range(3):
        part = left.astype(BF)
        left = left - part.astype(F32)
        out = dot_nt(spread, part)
        total = out if total is None else total + out
    return total


def sum_block(ref, other, j, height):
    at = slice(j * height, (j + 1) * height)
    out = ref[at, :].astype(F32)
    return out if other is None else out + other[at, :].astype(F32)


def sum_matrix(ref, other, first, count, height):
    return jnp.concatenate([sum_block(ref, other, first + j, height) for j in range(count)], 1)


def unpack_up_kernel(place, *refs):
    parts, (e_ref, up_ref, o_ref) = refs[:-3], refs[-3:]
    size, rows = up_ref.shape[0], parts[0].shape[0] // (FF_BLOCKS - CHUNK // LANES)
    cut = FF_BLOCKS - CHUNK // LANES
    for layer in range(2):

        @pl.when(place[2] == layer)
        def _():
            u, got_u, v, got_v = parts[4 * layer : 4 * layer + 4]
            for j in range(FF_BLOCKS):
                block = sum_block(u, got_u, j, rows) if j < cut else sum_block(v, got_v, j - cut, rows)
                up_ref[:, 0, j * LANES : (j + 1) * LANES] = block[:size]
            o_ref[:, 0, :] = narrow(sum_matrix(v, got_v, FF_BLOCKS - cut, OUT_BLOCKS, rows), e_ref[...])[:size]


def unpack_down_kernel(place, *refs):
    parts, (e_ref, gate_ref, down_ref) = refs[:-3], refs[-3:]
    size, ff_rows = gate_ref.shape[0], down_ref.shape[0]
    rows = parts[0].shape[0] // FF_BLOCKS
    for layer in range(2):

        @pl.when(place[2] == layer)
        def _():
            a, got_a = parts[2 * layer : 2 * layer + 2]
            down, gate = (a, got_a) if layer == 0 else (got_a, a)
            for j in range(FF_BLOCKS):
                gate_ref[:, 0, j * LANES : (j + 1) * LANES] = sum_block(gate, None, j, rows)[:size]
            down_ref[...] = narrow(sum_matrix(down, None, 0, OUT_BLOCKS, ff_rows), e_ref[...])


def unpack_qkv_kernel(place, *refs):
    parts, (q_ref, k_ref, v_ref, gain_ref) = refs[:-4], refs[-4:]
    size = q_ref.shape[0]
    kv_blocks = KVW // LANES
    rows = parts[0].shape[0] // (OUT_BLOCKS + kv_blocks + 1)
    for layer in range(2):

        @pl.when(place[2] == layer)
        def _():
            s, got = parts[2 * layer : 2 * layer + 2]
            q_ref[:, 0, :] = sum_matrix(s, got, 0, OUT_BLOCKS, rows)[:size, :D]
            both = sum_matrix(s, got, OUT_BLOCKS, kv_blocks, rows)
            k_ref[:, 0, :] = both[:size, : KV * HD]
            v_ref[:, 0, :] = both[:size, KV * HD :]
            gain_ref[...] = sum_block(s, got, OUT_BLOCKS + kv_blocks, rows).T


def unpack(kernel, name, place, parts, shapes):
    return pl.pallas_call(
        kernel,
        out_shape=[jax.ShapeDtypeStruct(shape, F32) for shape in shapes],
        in_specs=[SMEM] + [VMEM] * len(parts),
        out_specs=[VMEM] * len(shapes),
        compiler_params=BIG,
        cost_estimate=cost(4),
        name=name,
    )(place, *parts)


def join_kernel(place, own0, own1, got, e_ref, out_ref):
    section = place[2]
    for layer, own in enumerate((own0, own1)):

        @pl.when(section == layer)
        def _():
            out_ref[layer] = narrow_t(own[...], e_ref[...]).astype(out_ref.dtype)
            out_ref[1 - layer] = narrow_t(got[...], e_ref[...]).astype(out_ref.dtype)


def join(place, own0, own1, got, spread, dtype):
    return pl.pallas_call(
        join_kernel,
        out_shape=jax.ShapeDtypeStruct((2, D, own0.shape[0]), dtype),
        in_specs=[SMEM] + [VMEM] * 4,
        out_specs=VMEM,
        compiler_params=BIG,
        cost_estimate=cost(4),
        name="join",
    )(place, own0, own1, got, spread).transpose(0, 2, 1)


def spread_matrix(shards):
    size, room = D // shards, PADDED // shards
    feature = lax.broadcasted_iota(jnp.int32, (D, PADDED), 0)
    place = lax.broadcasted_iota(jnp.int32, (D, PADDED), 1)
    return (feature // size * room + feature % size == place).astype(BF)


def to_blocks(matrix):
    rows, width = matrix.shape
    return matrix.reshape(rows, width // LANES, LANES).transpose(1, 0, 2).reshape(-1, LANES)


def from_blocks(blocks, rows):
    return blocks.reshape(-1, rows, LANES).transpose(1, 0, 2).reshape(rows, -1)


def plus(left, right):
    return (left.astype(F32) + right.astype(F32)).astype(BF)


def after(value, *earlier):
    return lax.optimization_barrier((value,) + earlier)[0]


def scatter_z(parts):
    return lax.psum_scatter(parts, "z", scatter_dimension=0, tiled=False)


def scatter_z_small(parts, *before_last):
    count, me = lax.axis_size("z"), lax.axis_index("z")
    while parts.shape[0] > 1:
        step = parts.shape[0] // 2
        split = parts.reshape((2, step) + parts.shape[1:])
        bit = lax.rem(lax.div(me, step), 2)
        keep = lax.dynamic_index_in_dim(split, bit, 0, False)
        send = lax.dynamic_index_in_dim(split, 1 - bit, 0, False)
        if step == 1 and before_last:
            send = after(send, *before_last)
        parts = plus(keep, lax.ppermute(send, "z", [(i, i ^ step) for i in range(count)]))
    return parts[0]


def to_owner(part, layer):
    return lax.ppermute(part, "section", [(1 - layer, layer)])


def per_device_blocks(tokens, cotangent, positions, attn_gain, w_query, w_key, w_value, w_out, ffn_gain, w_gate, w_up, w_down):
    section, half = lax.axis_index("section"), lax.axis_index("dp")
    z_index, core = lax.axis_index("z"), lax.axis_index("core")
    plane = ("dp", "z", "core")
    size, ff_rows = w_query.shape[1], w_down.shape[1]
    shards = D // size
    room = PADDED // shards
    chips = shards // 2
    qkv_rows = QKV_BLOCKS * room
    block_range = jnp.stack([2 - core, 2 * z_index + 2]).astype(jnp.int32)
    place = jnp.stack([core, half, section]).astype(jnp.int32)
    spread = spread_matrix(shards)

    def mine(array_in):
        return lax.dynamic_index_in_dim(array_in, section, 0, keepdims=False)

    def widen(array_in):
        return project(array_in, spread).astype(BF)

    def padded(array_in):
        return jnp.pad(array_in, ((0, room - size), (0, 0)))

    gains = jnp.concatenate([attn_gain, ffn_gain], 0).T
    qkv = jnp.concatenate([w_key[0], w_value[0], w_query[0], gains, jnp.zeros((size, HD - 2), BF)], -1)
    narrow = jnp.concatenate([qkv, widen(w_out[0]), w_gate[0], w_up[0]], -1)
    shard = jnp.concatenate([to_blocks(padded(narrow)), to_blocks(widen(w_down[0]))], 0)
    first, rest = shard[:qkv_rows], shard[qkv_rows:]
    got_first = swap(first, "section")
    got_rest = swap(after(rest, got_first), "section")

    def layer_shard(own, got, layer):
        return jnp.where(section == layer, own, got)

    def gathered(*pieces):
        block = pieces[0] if len(pieces) == 1 else jnp.concatenate(pieces, 0)
        return lax.all_gather(block, plane, axis=0)

    def gains_at(whole, base):
        at = base + (QKV_BLOCKS - 1) * room
        gain = whole[:, at : at + room, HD : HD + 2].reshape(-1, 2).T.astype(F32)
        return gain[:1], gain[1:]

    early = gathered(layer_shard(first, got_first, 0))
    middle = gathered(layer_shard(rest, got_rest, 0), after(layer_shard(first, got_first, 1), early))
    base1 = rest.shape[0]
    w0 = (early, 0, middle, 0) + gains_at(early, 0)
    angle_cos, angle_sin = rope_tables(mine(positions))
    cos = jnp.concatenate([angle_cos[:, 0]] * 2, -1)
    sin = jnp.concatenate([angle_sin[:, 0]] * 2, -1)

    def attention(x, layer, *earlier):
        w_a, at_a, gain_a = layer[0], layer[1], layer[4]
        na, q, kv = qkv_forward(x, gain_a, cos, sin, w_a, at_a)
        kv_all = spread_kv(kv)
        o, op, lse = attend(block_range, after(q, *earlier) if earlier else q, kv_all, spread)
        return na, op, (x, q, kv_all, o, lse)

    x0 = widen(mine(tokens))
    na0, op0, saved0 = attention(x0, w0)
    late = gathered(after(layer_shard(rest, got_rest, 1), *saved0[2][0]))
    w1 = (middle, base1, late, 0) + gains_at(middle, base1)
    acts0, mixed0, gu0, y0 = ffn_forward(op0, x0, na0, w0[5], w0[2], w0[3])
    own0, send0 = turn(place, acts0)
    na1, op1, saved1 = attention(y0, w1, own0)
    y1, own1, send1, back1, dm1, do1, dgf1 = ffn_both(
        place, op1, y0, na1, w1[5], widen(mine(cotangent)), spread, w1[2], w1[3]
    )

    def backward_attn(do, saved):
        x, q, kv_all, o, lse = saved
        return attend_back(block_range, q, o, do, lse, cos, sin, kv_all)

    def backward_qkv(dq, shares, dm, dgf, layer, saved):
        w_a, at_a, w_f, at_f, gain_a, gain_f = layer
        return qkv_backward(dq, shares, cos, sin, saved[0], gain_a, dm, dgf, w_a, at_a)

    def halve(total):
        split = total.reshape((2, chips // 2) + total.shape[1:])
        return lax.dynamic_index_in_dim(split, half, 0, False), lax.dynamic_index_in_dim(split, 1 - half, 0, False)

    def scatter(*pieces, joined=None):
        if joined is None:
            joined = jnp.concatenate(pieces, 1) if len(pieces) > 1 else pieces[0]
        total = scatter_z(joined)
        cuts, at = [], 0
        for piece in pieces:
            cuts.append(total[at : at + piece.shape[1]])
            at += piece.shape[1]
        return cuts

    def cross(keep, got):
        keep, send = halve(plus(keep, got))
        return keep, swap(send, "dp")

    def swap_all(sends, axis):
        return [swap(send, axis) for send in sends]

    def all_after(values, *earlier):
        return [after(value, *earlier) for value in values]

    other0, other1 = swap(send0, "core"), swap(send1, "core")

    def swap_all(sends, axis):
        return [swap(send, axis) for send in sends]

    def query_grads(own, got):
        return own, got[-2:]

    got_y = swap(jnp.where(section == 0, y1, y0), "section")
    back_other1 = swap(back1, "core")
    dq1, dkv1, away1 = backward_attn(do1, saved1)
    got1 = swap(away1, "core")
    grads1 = grad_ffn(place, own1, other1, after(back1, dkv1), back_other1, shards)
    keep_a1, send_a1, keep_u1, send_u1 = grads1[:2], grads1[2:4], grads1[4:6], grads1[6:8]
    got_a1, got_u1 = swap_all(send_a1, "section"), swap_all(send_u1, "dp")
    shares1, _ = collect_kv(dkv1, got1, [(got_a1[0], got_u1[0]), (), (send_u1[0],)])
    dq1 = after(dq1, got_y)
    dkv_low1, dx1_low, back0, dm0, do0, dgf0 = both_back(
        dq1, shares1, cos, sin, y0, w1[4], dm1, dgf1, w1[0], w1[1], mixed0, w0[5], gu0, spread, w0[2], w0[3]
    )

    back0 = after(back0, got_a1[1], got_u1[1])
    keep_a1, keep_u1 = all_after(keep_a1, dkv_low1), all_after(keep_u1, dkv_low1)
    in_u1 = list(map(plus, keep_u1, got_u1))
    joined_u1 = jnp.concatenate(in_u1, 1)
    sum_u1 = scatter(*in_u1, joined=joined_u1)
    back_other0 = swap(back0, "core")
    grads0 = grad_ffn(place, own0, other0, after(back0, joined_u1), back_other0, shards)
    keep_a0, send_a0, keep_u0, send_u0 = grads0[:2], grads0[2:4], grads0[4:6], grads0[6:8]
    (keep_b1, got_b1), (keep_c1, got_c1) = map(cross, keep_a1, got_a1)
    got1 = after(got1, send_u0[0])
    keep_s1, send_s1 = grad_attn(place, own1, other1, *query_grads(dq1, got1), dkv_low1, swap(dkv_low1, "core"))
    got_a0 = swap_all(send_a0, "section")
    got_u0 = [swap(send_u0[0], "dp"), swap(jnp.concatenate([send_u0[1], send_s1], 1), "dp")]
    away_u1 = to_owner(jnp.concatenate(sum_u1, 0), 1)
    dq0, dkv0, away0 = backward_attn(after(do0, send_s1), saved0)
    away0 = after(away0, got_a0[0], got_u0[0], got_b1, got_c1, *sum_u1)
    keep_b1, keep_c1 = after(keep_b1, away0), after(keep_c1, away0)
    sum_a1 = scatter(plus(keep_b1, got_b1), plus(keep_c1, got_c1))
    got0 = swap(away0, "core")
    shares0, last = collect_kv(dkv0, got0, [(got_a0[1], got_u0[1])])
    keep_q0, send_q0 = grad_attn(place, own0, other0, *query_grads(dq0, got0))
    keep_b0, got_b0 = cross(after(keep_a0[0], away0), got_a0[0])
    kept = after(jnp.concatenate([keep_u0[1], keep_s1], 1), last)
    late0 = [plus(after(keep_u0[0], last), got_u0[0]), plus(kept, got_u0[1])]
    joined0 = jnp.concatenate(late0, 1)
    away_a1 = to_owner(jnp.concatenate(sum_a1, 0), 1)
    dq0 = after(dq0, send_q0, joined0, away_u1, got_b0)
    dkv_low0, dx0, dx0_low = backward_qkv(dq0, shares0, dm0, dgf0, w0, saved0)
    got_q0 = swap(after(send_q0, shares0[-1]), "dp")
    keep_c0, got_c0 = cross(after(keep_a0[1], shares0[-1]), got_a0[1])
    sum_v0, sum_w0 = scatter(*late0, joined=joined0)
    keep_k0, send_k0 = grad_attn(place, own0, other0, after(dkv_low0, got_c0), swap(dkv_low0, "core"))
    last0 = [plus(after(keep, sum_w0), got) for keep, got in ((keep_b0, got_b0), (keep_c0, got_c0))]
    sum_a0 = jnp.concatenate(scatter(*last0), 0)
    got_k0 = swap(send_k0, "dp")
    keep_q0, keep_k0 = after(keep_q0, away_a1, *last0), after(keep_k0, *last0)
    pieces = [plus(keep_q0, got_q0), plus(keep_k0, got_k0)]

    cut = send_u0[1].shape[1]
    sum_s1, sum_w0 = sum_w0[cut:], sum_w0[:cut]
    away_s1 = to_owner(sum_s1, 1)
    wide = lambda width: (size, 1, width)
    parts = [part for own in (sum_v0, sum_w0) for part in (own, to_owner(own, 0))]
    cut_u = sum_u1[0].shape[0]
    parts += [sum_u1[0], away_u1[:cut_u], sum_u1[1], away_u1[cut_u:]]
    g_up, g_o = unpack(unpack_up_kernel, "unpack_up", place, parts + [spread], (wide(FF), wide(D)))
    away_a0 = to_owner(sum_a0, 0)
    sum_s0 = scatter_z_small(jnp.concatenate(pieces, 1), g_up, away_a0)
    parts = [sum_a0, away_a0, jnp.concatenate(sum_a1, 0), away_a1]
    g_gate, g_down = unpack(unpack_down_kernel, "unpack_down", place, parts + [spread], (wide(FF), (ff_rows, D)))
    parts = [after(sum_s0, g_gate), to_owner(sum_s0, 0), sum_s1, away_s1]
    shapes = (wide(D), wide(KV * HD), wide(KV * HD), (LANES, room))
    g_q, g_k, g_v, gains = unpack(unpack_qkv_kernel, "unpack_qkv", place, parts, shapes)
    section_out = join(place, y0, y1, got_y, spread, BF)
    got = swap(jnp.where(section == 0, dx1_low, dx0_low), "section")
    input_grad = join(place, dx0, dx1_low, got, spread, F32)
    flat = lambda part: part.transpose(1, 0, 2)[0]
    g_q, g_k, g_v, g_o, g_gate, g_up = map(flat, (g_q, g_k, g_v, g_o, g_gate, g_up))
    outs = (section_out, input_grad, gains[0, :size], g_q, g_k, g_v, g_o, gains[1, :size], g_gate, g_up, g_down)
    return tuple(part[None] for part in outs)


def solution(mesh):
    sizes = mesh.devices.shape
    grid = Mesh(mesh.devices.reshape(sizes[0], sizes[1], sizes[2] // 2, 2), ("section", "dp", "z", "core"))
    ctx = ("z", "core")
    plane = ("dp", "z", "core")
    vector = P("section", plane)
    matrix = P("section", plane, None)
    in_specs = (
        P("dp", ctx, None),
        P("dp", ctx, None),
        P("dp", ctx),
        vector,
        matrix,
        matrix,
        matrix,
        matrix,
        vector,
        matrix,
        matrix,
        matrix,
    )
    acts = P("section", "dp", ctx, None)
    out_specs = (acts, acts, vector, matrix, matrix, matrix, matrix, vector, matrix, matrix, matrix)
    shards = sizes[1] * sizes[2]
    aligned = shards == 16
    return jax.shard_map(per_device_blocks if aligned else per_device, mesh=grid, in_specs=in_specs, out_specs=out_specs, check_vma=False)
```

```python
import functools

import jax
import jax.numpy as jnp
from jax import lax
from jax.experimental import pallas as pl
from jax.experimental.pallas import tpu as pltpu
from jax.sharding import Mesh
from jax.sharding import PartitionSpec as P

D = 960
H = 15
KV = 5
G = H // KV
HD = 64
FF = 2560
EPS = 1e-05
F32 = jnp.float32
BF = jnp.bfloat16


def dot(a,b): return jnp.dot(a,b,preferred_element_type=F32)

def fwd_kernel(rng, q_ref, kv_ref, o_ref, lse_ref, qt, vt, m_s, l_s, acc):
    T=q_ref.shape[0]; W=G*T
    qt[...]=q_ref[...].astype(F32).T.astype(BF)
    nb=kv_ref.shape[0]
    def step(b, first):
        vt[...]=kv_ref[b,:,KV*HD:].astype(F32).T.astype(BF)
        for g in range(KV):
            qg=jnp.concatenate([qt[(g*G+j)*HD:(g*G+j+1)*HD,:] for j in range(G)],1)
            s=dot(kv_ref[b,:,g*HD:(g+1)*HD],qg)
            if first:
                key=lax.broadcasted_iota(jnp.int32,(T,W),0)
                qry=lax.broadcasted_iota(jnp.int32,(T,W),1)%T
                s=jnp.where(key<=qry,s,-1e30)
                m=jnp.max(s,0,keepdims=True)
                p=jnp.exp(s-m)
                l_s[g:g+1,:]=jnp.sum(p,0,keepdims=True)
                acc[g*HD:(g+1)*HD,:]=dot(vt[g*HD:(g+1)*HD,:],p.astype(BF))
            else:
                mo=m_s[g:g+1,:]
                m=jnp.maximum(mo,jnp.max(s,0,keepdims=True))
                p=jnp.exp(s-m); al=jnp.exp(mo-m)
                l_s[g:g+1,:]=l_s[g:g+1,:]*al+jnp.sum(p,0,keepdims=True)
                acc[g*HD:(g+1)*HD,:]=acc[g*HD:(g+1)*HD,:]*al+dot(vt[g*HD:(g+1)*HD,:],p.astype(BF))
            m_s[g:g+1,:]=m
    step(0,True)
    def body(b,_):
        step(b,False); return 0
    lax.fori_loop(rng[0],rng[1],body,0)
    for g in range(KV):
        inv=1.0/l_s[g:g+1,:]
        lse_ref[g:g+1,:]=m_s[g:g+1,:]+jnp.log(l_s[g:g+1,:])
        og=acc[g*HD:(g+1)*HD,:]*inv
        for j in range(G):
            h=g*G+j
            o_ref[:,h*HD:(h+1)*HD]=og[:,j*T:(j+1)*T].T.astype(BF)

def attn_fwd(rng,q,kv):
    T=q.shape[0]; W=G*T
    return pl.pallas_call(fwd_kernel,
      out_shape=(jax.ShapeDtypeStruct((T,H*HD),BF),jax.ShapeDtypeStruct((KV,W),F32)),
      in_specs=[pl.BlockSpec(memory_space=pltpu.SMEM)]+[pl.BlockSpec(memory_space=pltpu.VMEM)]*2,
      out_specs=[pl.BlockSpec(memory_space=pltpu.VMEM)]*2,
      scratch_shapes=[pltpu.VMEM((H*HD,T),BF),pltpu.VMEM((KV*HD,T),BF),pltpu.VMEM((KV,W),F32),pltpu.VMEM((KV,W),F32),pltpu.VMEM((KV*HD,W),F32)],
      compiler_params=pltpu.CompilerParams(vmem_limit_bytes=48<<20),
    )(rng,q,kv)

def bwd_kernel(rng, q_ref, kv_ref, o_ref, do_ref, lse_ref, dq_ref, dkv_ref, qt, dot_, qn, don, kt, dl, dqa):
    T=q_ref.shape[0]; W=G*T
    nb=kv_ref.shape[0]
    qt[...]=q_ref[...].astype(F32).T.astype(BF)
    doT=do_ref[...].astype(F32).T
    dot_[...]=doT.astype(BF)
    oT=o_ref[...].astype(F32).T
    prod=doT*oT
    for h in range(H):
        g,j=divmod(h,G)
        dl[g:g+1,j*T:(j+1)*T]=jnp.sum(prod[h*HD:(h+1)*HD,:],0,keepdims=True)
        qn[g,j*T:(j+1)*T,:]=q_ref[:,h*HD:(h+1)*HD]
        don[g,j*T:(j+1)*T,:]=do_ref[:,h*HD:(h+1)*HD]
    def step(b, first):
        kt[...]=kv_ref[b,:,:KV*HD].astype(F32).T.astype(BF)
        for g in range(KV):
            qg=jnp.concatenate([qt[(g*G+j)*HD:(g*G+j+1)*HD,:] for j in range(G)],1)
            dg=jnp.concatenate([dot_[(g*G+j)*HD:(g*G+j+1)*HD,:] for j in range(G)],1)
            s=dot(kv_ref[b,:,g*HD:(g+1)*HD],qg)
            p=jnp.exp(s-lse_ref[g:g+1,:])
            if first:
                key=lax.broadcasted_iota(jnp.int32,(T,W),0)
                qry=lax.broadcasted_iota(jnp.int32,(T,W),1)%T
                p=jnp.where(key<=qry,p,0.0)
            dp=dot(kv_ref[b,:,(KV+g)*HD:(KV+g+1)*HD],dg)
            dz=(p*(dp-dl[g:g+1,:])).astype(BF)
            dkv_ref[b,:,(KV+g)*HD:(KV+g+1)*HD]=dot(p.astype(BF),don[g]).astype(BF)
            dkv_ref[b,:,g*HD:(g+1)*HD]=dot(dz,qn[g]).astype(BF)
            dq=dot(kt[g*HD:(g+1)*HD,:],dz)
            if first: dqa[g*HD:(g+1)*HD,:]=dq
            else: dqa[g*HD:(g+1)*HD,:]+=dq
    step(0,True)
    def body(b,_):
        step(b,False); return 0
    lax.fori_loop(rng[0],rng[1],body,0)
    def zero(b,_):
        dkv_ref[b]=jnp.zeros((T,2*KV*HD),BF); return 0
    lax.fori_loop(1,rng[0],zero,0)
    lax.fori_loop(rng[1],nb,zero,0)
    for g in range(KV):
        for j in range(G):
            h=g*G+j
            dq_ref[:,h*HD:(h+1)*HD]=(dqa[g*HD:(g+1)*HD,j*T:(j+1)*T]*HD**-0.5).T

def attn_bwd(rng,q,kv,o,do,lse):
    T=q.shape[0]; W=G*T
    return pl.pallas_call(bwd_kernel,
      out_shape=(jax.ShapeDtypeStruct((T,H*HD),F32),jax.ShapeDtypeStruct(kv.shape,BF)),
      in_specs=[pl.BlockSpec(memory_space=pltpu.SMEM)]+[pl.BlockSpec(memory_space=pltpu.VMEM)]*5,
      out_specs=[pl.BlockSpec(memory_space=pltpu.VMEM)]*2,
      scratch_shapes=[pltpu.VMEM((H*HD,T),BF),pltpu.VMEM((H*HD,T),BF),pltpu.VMEM((KV,W,HD),BF),pltpu.VMEM((KV,W,HD),BF),
        pltpu.VMEM((KV*HD,T),BF),pltpu.VMEM((KV,W),F32),pltpu.VMEM((KV*HD,W),F32)],
      compiler_params=pltpu.CompilerParams(vmem_limit_bytes=48<<20),
    )(rng,q,kv,o,do,lse)


def rotate_half(vector):
    half_dim = vector.shape[-1] // 2
    return jnp.concatenate([-vector[..., half_dim:], vector[..., :half_dim]], -1)


def rope_tables(seq_pos):
    half_dim = HD // 2
    inv_freq = 10000.0 ** (-(jnp.arange(half_dim, dtype=F32) * 2.0) / HD)
    angles = seq_pos.astype(F32)[..., None] * inv_freq
    angle_pair = jnp.concatenate([angles, angles], -1)[..., None, :]
    return (jnp.cos(angle_pair), jnp.sin(angle_pair))


def norm_forward(values_in, gain_vec):
    factor = lax.rsqrt(jnp.mean(values_in * values_in, -1, keepdims=True) + EPS)
    return (values_in * factor * gain_vec, factor)


def norm_backward(grad_in, values_in, factor, gain_vec):
    scaled = grad_in * gain_vec
    grad_back = factor * scaled - values_in * factor * factor * factor * jnp.mean(
        scaled * values_in, -1, keepdims=True
    )
    return (grad_back, jnp.sum(grad_in * values_in * factor, 0))


def swap(block, axis):
    return lax.ppermute(block, axis, [(0, 1), (1, 0)])


def move_z(block, distance):
    count = lax.axis_size("z")
    route = [(i, i + distance) for i in range(count) if 0 <= i + distance < count]
    return lax.ppermute(block, "z", route)


def gather_kv(block):
    count = lax.axis_size("z")
    own = [block] + [move_z(block, d) for d in range(1, count)]
    own = jnp.stack(own)
    other = swap(own, "core")
    return jnp.stack([own, other], 1).reshape((2 * count,) + block.shape)


def reduce_kv(blocks):
    count = lax.axis_size("z")
    blocks = blocks.reshape((count, 2) + blocks.shape[1:])
    mine = blocks[:, 0].astype(F32) + swap(blocks[:, 1], "core").astype(F32)
    total = mine[0]
    for d in range(1, count):
        total = total + move_z(mine[d].astype(BF), -d).astype(F32)
    return total


def project(left, right):
    return jnp.dot(left, right, preferred_element_type=F32)


def project_t(left, right):
    return lax.dot_general(left, right, (((1,), (1,)), ((), ())), preferred_element_type=F32)


def outer(left, right):
    return lax.dot_general(left, right, (((0,), (0,)), ((), ())), preferred_element_type=F32)


def rope(values, cosine, sine):
    count = values.shape[0]
    values = values.reshape(count, -1, HD)
    return (values * cosine + rotate_half(values) * sine).reshape(count, -1)


def rope_t(values, cosine, sine):
    count = values.shape[0]
    values = values.reshape(count, -1, HD)
    return (values * cosine - rotate_half(values * sine)).reshape(count, -1)


def layer_forward(rows, tables, weights, block_range):
    gain_a, w_qkv, w_o, gain_f, w_g, w_u, w_d = weights
    cosine, sine = tables
    normed_a, factor_a = norm_forward(rows, gain_a)
    normed_a = normed_a.astype(BF)
    qkv = project(normed_a, w_qkv)
    queries = (rope(qkv[:, :D], cosine, sine)).astype(BF) * BF(HD**-0.5)
    keys = rope(qkv[:, D : D + KV * HD], cosine, sine).astype(BF)
    values = qkv[:, D + KV * HD :].astype(BF)
    kv_all = gather_kv(jnp.concatenate([keys, values], -1))
    attended, log_total = attn_fwd(block_range, queries, kv_all)
    mixed = rows + project(attended, w_o)
    normed_f, factor_f = norm_forward(mixed, gain_f)
    normed_f = normed_f.astype(BF)
    gate_act = project(normed_f, w_g)
    up_proj = project(normed_f, w_u)
    hidden = (jax.nn.silu(gate_act) * up_proj).astype(BF)
    out = (mixed + project(hidden, w_d)).astype(BF)
    saved = (rows, factor_a, normed_a, queries, kv_all, log_total, attended, mixed, factor_f, normed_f, gate_act, up_proj, hidden)
    return out, saved


def layer_backward(grad_low, saved, tables, weights, block_range):
    gain_a, w_qkv, w_o, gain_f, w_g, w_u, w_d = weights
    cosine, sine = tables
    rows, factor_a, normed_a, queries, kv_all, log_total, attended, mixed, factor_f, normed_f, gate_act, up_proj, hidden = saved
    d_hidden = project_t(grad_low, w_d)
    sig = jax.nn.sigmoid(gate_act)
    d_gate = (d_hidden * up_proj * sig * (1.0 + gate_act * (1.0 - sig))).astype(BF)
    d_up = (d_hidden * gate_act * sig).astype(BF)
    d_normed_f = project_t(d_gate, w_g) + project_t(d_up, w_u)
    d_norm, d_gain_f = norm_backward(d_normed_f, mixed, factor_f, gain_f)
    d_mixed = grad_low.astype(F32) + d_norm
    mix_low = d_mixed.astype(BF)
    d_attended = project_t(mix_low, w_o).astype(BF)
    d_query, d_kv = attn_bwd(block_range, queries, kv_all, attended, d_attended, log_total)
    d_kv = reduce_kv(d_kv)
    d_query = rope_t(d_query, cosine, sine).astype(BF)
    d_key = rope_t(d_kv[:, : KV * HD], cosine, sine).astype(BF)
    d_value = d_kv[:, KV * HD :].astype(BF)
    d_qkv = jnp.concatenate([d_query, d_key, d_value], -1)
    d_normed_a = project_t(d_qkv, w_qkv)
    d_norm_a, d_gain_a = norm_backward(d_normed_a, rows, factor_a, gain_a)
    d_rows = d_mixed + d_norm_a
    grads = dict(
        gate=outer(normed_f, d_gate).astype(BF),
        up=outer(normed_f, d_up).astype(BF),
        down=outer(hidden, grad_low).astype(BF),
        out=outer(attended, mix_low).astype(BF),
        qkv=outer(normed_a, d_qkv).astype(BF),
        gains=jnp.stack([d_gain_a, d_gain_f]),
    )
    return d_rows, grads


def per_device(tokens, cotangent, positions, attn_gain, w_query, w_key, w_value, w_out, ffn_gain, w_gate, w_up, w_down):
    section = lax.axis_index("section")
    z_index, core = lax.axis_index("z"), lax.axis_index("core")
    plane = ("dp", "z", "core")
    group = tokens.shape[0]
    local = tokens.shape[1]
    block_range = jnp.stack([2 - core, 2 * z_index + 2]).astype(jnp.int32)

    def mine(array_in):
        return lax.dynamic_index_in_dim(array_in, section, 0, keepdims=False)

    rows = tokens.shape[1]
    shard_rows = w_query.shape[1]
    ff_rows = w_down.shape[1]
    half = ff_rows // 2
    qkvo = jnp.concatenate([w_query[0], w_key[0], w_value[0], w_out[0]], -1)
    down = jnp.concatenate([w_down[0, :half], jnp.zeros((half, 64), BF), w_down[0, half:], jnp.zeros((half, 576), BF)], -1)
    gains = jnp.concatenate([attn_gain, ffn_gain], -1)
    shard = jnp.concatenate([qkvo, w_gate[0], w_up[0], down], 0)
    shard = lax.dynamic_update_slice(shard, gains, (3 * shard_rows, 2048))
    other = swap(shard, "section")

    def assemble(block):
        whole = lax.all_gather(block, plane, axis=0)
        n = shard_rows

        def piece(lo, hi):
            return whole[:, lo : lo + n, :hi].reshape(-1, hi) if hi <= FF else None

        attn = whole[:, :n, :].reshape(n * whole.shape[0], FF)
        w_g = whole[:, n : 2 * n, :].reshape(-1, FF)
        w_u = whole[:, 2 * n : 3 * n, :].reshape(-1, FF)
        w_d = jnp.concatenate([whole[:, 3 * n :, :D], whole[:, 3 * n :, 1024 : 1024 + D]], 1).reshape(-1, D)
        gain_rows = whole[:, 3 * n, 2048 : 2048 + 2 * n].astype(F32)
        gain_a = gain_rows[:, :n].reshape(-1)
        gain_f = gain_rows[:, n:].reshape(-1)
        return gain_a, attn[:, : D + 2 * KV * HD], attn[:, D + 2 * KV * HD :], gain_f, w_g, w_u, w_d

    w0 = assemble(jnp.where(section == 0, shard, other))
    w1 = assemble(jnp.where(section == 1, shard, other))
    tables = rope_tables(mine(positions))
    out0, saved0 = layer_forward(mine(tokens).astype(F32), tables, w0, block_range)
    out1, saved1 = layer_forward(out0.astype(F32), tables, w1, block_range)
    d1, g1 = layer_backward(mine(cotangent), saved1, tables, w1, block_range)
    d1_low = d1.astype(BF)
    d0, g0 = layer_backward(d1_low, saved0, tables, w0, block_range)

    def pair(own, got):
        return jnp.where(section == 0, jnp.stack([own, got]), jnp.stack([got, own]))

    got = swap(jnp.where(section == 0, out1, out0), "section")
    section_out = pair(jnp.where(section == 0, out0, out1), got)
    got = swap(jnp.where(section == 0, d1_low, d0.astype(BF)), "section").astype(F32)
    input_grad = pair(jnp.where(section == 0, d0, d1_low.astype(F32)), got)

    def reduce(first, second):
        def scatter(part):
            return lax.psum_scatter(part, plane, scatter_dimension=0, tiled=True)

        s0, s1 = scatter(first), scatter(second)
        got = swap(jnp.where(section == 0, s1, s0), "section")
        return jnp.where(section == 0, s0, s1).astype(F32) + got.astype(F32)

    grads = {name: reduce(g0[name], g1[name]) for name in ("gate", "up", "down", "out", "qkv")}
    gain_grad = reduce(g0["gains"].T, g1["gains"].T)
    qkv = grads["qkv"]
    kd = KV * HD
    outs = (
        section_out,
        input_grad,
        gain_grad[:, 0],
        qkv[:, :D],
        qkv[:, D : D + kd],
        qkv[:, D + kd :],
        grads["out"],
        gain_grad[:, 1],
        grads["gate"],
        grads["up"],
        grads["down"],
    )
    return tuple(part[None] for part in outs)


LANES = 128
PADDED = 1024
CHUNK = 640
WIDE = 512
KVW = 2 * KV * HD
QKV_BLOCKS = 13
EXTRA = 16
ACTS = FF + 3 * PADDED
BACK = 2 * FF + 2 * PADDED
OUT_BLOCKS = PADDED // LANES
FF_BLOCKS = FF // LANES
VMEM = pl.BlockSpec(memory_space=pltpu.VMEM)
ANY = pl.BlockSpec(memory_space=pl.ANY)
SMEM = pl.BlockSpec(memory_space=pltpu.SMEM)
BIG = pltpu.CompilerParams(vmem_limit_bytes=56 << 20)


def cost(microseconds):
    return pl.CostEstimate(flops=int(microseconds * 1.15e9), bytes_accessed=int(microseconds * 3.69e6), transcendentals=0)


def dot_nt(left, right):
    return lax.dot_general(left, right, (((1,), (1,)), ((), ())), preferred_element_type=F32)


def columns(ref, first, count, rows):
    parts = [
        ref[:, first + i * rows : first + (i + 1) * rows, :].reshape(-1, LANES) for i in range(count)
    ]
    return parts[0] if count == 1 else jnp.concatenate(parts, 1)


def half_of(values):
    lane = lax.broadcasted_iota(jnp.int32, values.shape, 1)
    back = pltpu.roll(values, LANES - HD // 2, 1)
    ahead = pltpu.roll(values, HD // 2, 1)
    return jnp.where(lane % HD < HD // 2, -back, ahead)


def rms(values):
    return lax.rsqrt(jnp.sum(values * values, -1, keepdims=True) / D + EPS)


def norm_back(grad, values, gain):
    factor = rms(values)
    scaled = grad * gain
    mean = jnp.sum(scaled * values, -1, keepdims=True) / D
    back = factor * scaled - values * (factor * factor * factor * mean)
    return back, jnp.sum(grad * values * factor, 0, keepdims=True)


def load_kv(blocks, other, kv_s, sems):
    copies = [pltpu.make_async_copy(block, kv_s.at[0, d], sems.at[d]) for d, block in enumerate(blocks)]
    copies.append(pltpu.make_async_copy(other, kv_s.at[1], sems.at[len(blocks)]))
    for copy in copies:
        copy.start()
    return copies


def attend_kernel(zs, rng, q_ref, *refs):
    blocks, (other, e_hbm, o_ref, op_ref, lse_ref, kv_s, qt, vt, m_s, l_s, acc, e_s, sems) = refs[:zs], refs[zs:]
    T = q_ref.shape[0]
    W = G * T
    copies = load_kv(blocks, other, kv_s, sems)
    spread = pltpu.make_async_copy(e_hbm, e_s, sems.at[zs + 1])
    spread.start()
    qt[...] = q_ref[...].astype(F32).T.astype(BF)
    for copy in copies:
        copy.wait()

    def step(b, first):
        kv = kv_s.at[lax.rem(b, 2), lax.div(b, 2)] if not first else kv_s.at[0, 0]
        vt[...] = kv[:, KV * HD :].astype(F32).T.astype(BF)
        ats = [slice(g * HD, (g + 1) * HD) for g in range(KV)]
        scores = []
        for g in range(KV):
            qg = jnp.concatenate([qt[(g * G + j) * HD : (g * G + j + 1) * HD, :] for j in range(G)], 1)
            s = dot(kv[:, ats[g]], qg)
            if first:
                key = lax.broadcasted_iota(jnp.int32, (T, W), 0)
                query = lax.broadcasted_iota(jnp.int32, (T, W), 1) % T
                s = jnp.where(key <= query, s, -1e30)
            scores.append(s)
        probs, scales = [], []
        for g in range(KV):
            top = jnp.max(scores[g], 0, keepdims=True)
            if not first:
                old = m_s[g : g + 1, :]
                top = jnp.maximum(old, top)
                scales.append(jnp.exp(old - top))
            p = jnp.exp(scores[g] - top)
            total = jnp.sum(p, 0, keepdims=True)
            l_s[g : g + 1, :] = total if first else l_s[g : g + 1, :] * scales[g] + total
            m_s[g : g + 1, :] = top
            probs.append(p.astype(BF))
        for g in range(KV):
            out = dot(vt[ats[g], :], probs[g])
            acc[ats[g], :] = out if first else acc[ats[g], :] * scales[g] + out

    step(0, True)

    def body(b, _):
        step(b, False)
        return 0

    lax.fori_loop(rng[0], rng[1], body, 0)
    for g in range(KV):
        lse_ref[g : g + 1, :] = m_s[g : g + 1, :] + jnp.log(l_s[g : g + 1, :])
        og = acc[g * HD : (g + 1) * HD, :] / l_s[g : g + 1, :]
        for j in range(G):
            h = g * G + j
            o_ref[:, h * HD : (h + 1) * HD] = og[:, j * T : (j + 1) * T].T.astype(BF)
    spread.wait()
    op_ref[...] = dot(o_ref[...], e_s[...]).astype(BF)


def attend(rng, q, kv_all, e):
    blocks, other = kv_all
    T, zs = q.shape[0], len(blocks)
    W = G * T
    return pl.pallas_call(
        functools.partial(attend_kernel, zs),
        out_shape=(
            jax.ShapeDtypeStruct((T, D), BF),
            jax.ShapeDtypeStruct((T, PADDED), BF),
            jax.ShapeDtypeStruct((KV, W), F32),
        ),
        in_specs=[SMEM, VMEM] + [ANY] * (zs + 2),
        out_specs=[VMEM] * 3,
        scratch_shapes=[
            pltpu.VMEM((2, zs, T, KVW), BF),
            pltpu.VMEM((D, T), BF),
            pltpu.VMEM((KV * HD, T), BF),
            pltpu.VMEM((KV, W), F32),
            pltpu.VMEM((KV, W), F32),
            pltpu.VMEM((KV * HD, W), F32),
            pltpu.VMEM((D, PADDED), BF),
            pltpu.SemaphoreType.DMA((zs + 2,)),
        ],
        compiler_params=BIG,
        cost_estimate=cost(24),
        name="attend",
    )(rng, q, *blocks, other, e)


def attend_back_kernel(zs, rng, q_ref, o_ref, do_ref, lse_ref, cos_ref, sin_ref, *refs):
    blocks, (other, dq_ref, own_ref, send_ref, kv_s, qt, dot_, qn, don, kt, dl, dqa, sems, dkv_ref, out_sems) = (
        refs[:zs],
        refs[zs:],
    )
    T = q_ref.shape[0]
    W = G * T
    copies = load_kv(blocks, other, kv_s, sems)
    qt[...] = q_ref[...].astype(F32).T.astype(BF)
    do_t = do_ref[...].astype(F32).T
    dot_[...] = do_t.astype(BF)
    prod = do_t * o_ref[...].astype(F32).T
    for h in range(H):
        g, j = divmod(h, G)
        rows = slice(j * T, (j + 1) * T)
        dl[g : g + 1, rows] = jnp.sum(prod[h * HD : (h + 1) * HD, :], 0, keepdims=True)
        qn[g, rows, :] = q_ref[:, h * HD : (h + 1) * HD]
        don[g, rows, :] = do_ref[:, h * HD : (h + 1) * HD]
    for copy in copies:
        copy.wait()

    def step(b, first):
        side, far = (0, 0) if first else (lax.rem(b, 2), lax.div(b, 2))
        kv = kv_s.at[side, far]
        out = dkv_ref.at[side, far]
        kt[...] = kv[:, : KV * HD].astype(F32).T.astype(BF)
        for g in range(KV):
            at = slice(g * HD, (g + 1) * HD)
            vat = slice((KV + g) * HD, (KV + g + 1) * HD)
            heads = [slice((g * G + j) * HD, (g * G + j + 1) * HD) for j in range(G)]
            s = dot(kv[:, at], jnp.concatenate([qt[h, :] for h in heads], 1))
            p = jnp.exp(s - lse_ref[g : g + 1, :])
            if first:
                key = lax.broadcasted_iota(jnp.int32, (T, W), 0)
                query = lax.broadcasted_iota(jnp.int32, (T, W), 1) % T
                p = jnp.where(key <= query, p, 0.0)
            dp = dot(kv[:, vat], jnp.concatenate([dot_[h, :] for h in heads], 1))
            dz = (p * (dp - dl[g : g + 1, :])).astype(BF)
            out[:, vat] = dot(p.astype(BF), don[g]).astype(BF)
            out[:, at] = dot(dz, qn[g]).astype(BF)
            dq = dot(kt[at, :], dz)
            if first:
                dqa[at, :] = dq
            else:
                dqa[at, :] += dq

    step(0, True)

    def body(b, _):
        step(b, False)
        return 0

    def zero(b, _):
        dkv_ref[lax.rem(b, 2), lax.div(b, 2)] = jnp.zeros((T, KVW), BF)
        return 0

    lax.fori_loop(rng[0], rng[1], body, 0)
    lax.fori_loop(1, rng[0], zero, 0)
    lax.fori_loop(rng[1], 2 * zs, zero, 0)
    cos, sin = cos_ref[...], sin_ref[...]
    for pair in range(PADDED // LANES):
        parts = []
        for h in (2 * pair, 2 * pair + 1):
            g, j = divmod(h, G)
            if h < H:
                parts.append(dqa[g * HD : (g + 1) * HD, j * T : (j + 1) * T] * HD**-0.5)
            else:
                parts.append(jnp.zeros((HD, T), F32))
        grad = jnp.concatenate(parts, 0).T
        turned = grad * cos - half_of(grad * sin)
        dq_ref[:, pair * LANES : (pair + 1) * LANES] = turned.astype(BF)
    kv_s[0, 0] = dq_ref[:, :KVW]
    kv_s[0, 1, :, : PADDED - KVW] = dq_ref[:, KVW:]
    copies = [
        pltpu.make_async_copy(dkv_ref.at[0], own_ref, out_sems.at[0]),
        pltpu.make_async_copy(dkv_ref.at[1], send_ref.at[pl.ds(0, zs)], out_sems.at[1]),
        pltpu.make_async_copy(kv_s.at[0, pl.ds(0, 2)], send_ref.at[pl.ds(zs, 2)], out_sems.at[2]),
    ]
    for copy in copies:
        copy.start()
    for copy in copies:
        copy.wait()


def attend_back(rng, q, o, do, lse, cos, sin, kv_all):
    blocks, other = kv_all
    T, zs = q.shape[0], len(blocks)
    W = G * T
    return pl.pallas_call(
        functools.partial(attend_back_kernel, zs),
        out_shape=(
            jax.ShapeDtypeStruct((T, PADDED), BF),
            jax.ShapeDtypeStruct((zs, T, KVW), BF),
            jax.ShapeDtypeStruct((zs + 2, T, KVW), BF),
        ),
        in_specs=[SMEM] + [VMEM] * 6 + [ANY] * (zs + 1),
        out_specs=[VMEM, ANY, ANY],
        scratch_shapes=[
            pltpu.VMEM((2, zs, T, KVW), BF),
            pltpu.VMEM((D, T), BF),
            pltpu.VMEM((D, T), BF),
            pltpu.VMEM((KV, W, HD), BF),
            pltpu.VMEM((KV, W, HD), BF),
            pltpu.VMEM((KV * HD, T), BF),
            pltpu.VMEM((KV, W), F32),
            pltpu.VMEM((KV * HD, W), F32),
            pltpu.SemaphoreType.DMA((zs + 1,)),
            pltpu.VMEM((2, zs, T, KVW), BF),
            pltpu.SemaphoreType.DMA((3,)),
        ],
        compiler_params=BIG,
        cost_estimate=cost(24),
        name="attend_back",
    )(rng, q, o, do, lse, cos, sin, *blocks, other)


def spread_kv(block):
    blocks = [block] + [move_z(block, d) for d in range(1, lax.axis_size("z"))]
    return blocks, swap(jnp.stack(blocks), "core")


def collect_kv(grads, got, before=()):
    count = lax.axis_size("z")
    moving = plus(grads[count - 1], got[count - 1])
    for d in range(count - 2, -1, -1):
        moving = after(moving, *before[d]) if d < len(before) else moving
        moved = move_z(moving, -1)
        own = plus(grads[d], got[d])
        if d == 0:
            return [own, moved], moving
        moving = plus(own, moved)


def qkv_kernel(base, x_ref, gain_ref, cos_ref, sin_ref, w_hbm, na_ref, q_ref, kv_ref, w_s, sem):
    rows = w_s.shape[1] // QKV_BLOCKS
    copy = pltpu.make_async_copy(w_hbm.at[:, pl.ds(base, w_s.shape[1]), :], w_s, sem)
    copy.start()
    x = x_ref[...].astype(F32)
    normed = (x * rms(x) * gain_ref[...]).astype(BF)
    na_ref[...] = normed
    copy.wait()
    cos, sin = cos_ref[...], sin_ref[...]
    for j in range(QKV_BLOCKS):
        out = dot(normed, columns(w_s, j * rows, 1, rows))
        if j < 5:
            turned = out * cos + half_of(out) * sin if j < 3 else out
            if j == 2:
                lane = lax.broadcasted_iota(jnp.int32, out.shape, 1)
                turned = jnp.where(lane < HD, turned, out)
            kv_ref[:, j * LANES : (j + 1) * LANES] = turned.astype(BF)
        else:
            turned = (out * cos + half_of(out) * sin).astype(BF) * BF(HD**-0.5)
            at = (j - 5) * LANES
            width = min(LANES, D - at)
            q_ref[:, at : at + width] = turned[:, :width]


def qkv_forward(x, gain, cos, sin, weights, base):
    count = x.shape[0]
    shards = weights.shape[0]
    rows = PADDED // shards
    return pl.pallas_call(
        functools.partial(qkv_kernel, base),
        out_shape=(
            jax.ShapeDtypeStruct((count, PADDED), BF),
            jax.ShapeDtypeStruct((count, D), BF),
            jax.ShapeDtypeStruct((count, KVW), BF),
        ),
        in_specs=[VMEM] * 4 + [ANY],
        out_specs=[VMEM] * 3,
        scratch_shapes=[pltpu.VMEM((shards, QKV_BLOCKS * rows, LANES), BF), pltpu.SemaphoreType.DMA],
        compiler_params=BIG,
        cost_estimate=cost(6),
        name="qkv_forward",
    )(x, gain, cos, sin, weights)


def weight_copies(w_hbm, w_s, sems, first):
    shards = w_hbm.shape[0]
    rows, ff_rows = PADDED // shards, FF // shards
    gate = OUT_BLOCKS * rows
    up = gate + FF_BLOCKS * rows
    down = up + FF_BLOCKS * rows
    step = WIDE // LANES * rows
    everyone = pl.ds(0, shards)
    places = [(everyone, 0, gate)]
    places += [(everyone, at + i * step, step) for i in range(FF // WIDE) for at in (gate, up)]
    places += [(pl.ds(h * shards // 2, shards // 2), down, OUT_BLOCKS * ff_rows) for h in range(2)]
    copies = []
    for i, (who, at, height) in enumerate(places):
        source, target = w_hbm.at[who, pl.ds(first + at, height), :], w_s.at[who, pl.ds(at, height), :]
        copies.append(pltpu.make_async_copy(source, target, sems.at[i]))
    pairs = [copies[1 + 2 * i : 3 + 2 * i] for i in range(FF // WIDE)]
    return copies[0], pairs, copies[-2:]


def gate_up(w_s, i):
    rows = PADDED // w_s.shape[0]
    at = OUT_BLOCKS * rows + i * (WIDE // LANES) * rows
    return [columns(w_s, at + j * FF_BLOCKS * rows, WIDE // LANES, rows) for j in range(2)]


def down_half(w_s, h):
    shards = w_s.shape[0]
    rows, ff_rows = PADDED // shards, FF // shards
    at = (OUT_BLOCKS + 2 * FF_BLOCKS) * rows
    who = slice(h * shards // 2, (h + 1) * shards // 2)
    parts = [w_s[who, at + i * ff_rows : at + (i + 1) * ff_rows, :].reshape(-1, LANES) for i in range(OUT_BLOCKS)]
    return jnp.concatenate(parts, 1)


def ffn_up(x, op, na, gain, w_s, acts, loads):
    out, pairs, downs = loads
    rows = PADDED // w_s.shape[0]
    acts[:, FF : FF + PADDED] = op
    acts[:, FF + 2 * PADDED :] = na
    out.wait()
    mixed = x.astype(F32) + dot(op, columns(w_s, 0, OUT_BLOCKS, rows))
    normed = (mixed * rms(mixed) * gain).astype(BF)
    acts[:, FF + PADDED : FF + 2 * PADDED] = normed
    gates = []
    for i in range(FF // WIDE):
        for copy in pairs[i]:
            copy.wait()
        gate, up = gate_up(w_s, i)
        g, u = dot(normed, gate), dot(normed, up)
        acts[:, i * WIDE : (i + 1) * WIDE] = (g * jax.nn.sigmoid(g) * u).astype(BF)
        gates.append((g.astype(BF), u.astype(BF)))
    return mixed, gates


def ffn_down(mixed, w_s, acts, downs):
    total = mixed
    for h in range(2):
        downs[h].wait()
        total = total + dot(acts[:, h * FF // 2 : (h + 1) * FF // 2], down_half(w_s, h))
    return total.astype(BF)


def ffn_kernel(first, op_ref, x_ref, na_ref, gain_ref, w_hbm, acts_hbm, m_ref, gu_hbm, y_ref, w_s, acts, gu, sems, outs):
    loads = weight_copies(w_hbm, w_s, sems, first)
    for copy in [loads[0]] + sum(loads[1], []) + loads[2]:
        copy.start()
    mixed, gates = ffn_up(x_ref[...], op_ref[...], na_ref[...], gain_ref[...], w_s, acts, loads)
    m_ref[...] = mixed
    for i, pair in enumerate(gates):
        for j in range(2):
            gu[j, :, i * WIDE : (i + 1) * WIDE] = pair[j]
    sends = [pltpu.make_async_copy(acts, acts_hbm, outs.at[0]), pltpu.make_async_copy(gu, gu_hbm, outs.at[1])]
    for copy in sends:
        copy.start()
    y_ref[...] = ffn_down(mixed, w_s, acts, loads[2])
    for copy in sends:
        copy.wait()


def ffn_forward(op, x, na, gain, weights, first):
    count = x.shape[0]
    shards = weights.shape[0]
    later = (OUT_BLOCKS + 2 * FF_BLOCKS) * (PADDED // shards) + OUT_BLOCKS * (FF // shards)
    return pl.pallas_call(
        functools.partial(ffn_kernel, first),
        out_shape=(
            jax.ShapeDtypeStruct((count, ACTS), BF),
            jax.ShapeDtypeStruct((count, PADDED), F32),
            jax.ShapeDtypeStruct((2, count, FF), BF),
            jax.ShapeDtypeStruct((count, PADDED), BF),
        ),
        in_specs=[VMEM] * 4 + [ANY],
        out_specs=[ANY, VMEM, ANY, VMEM],
        scratch_shapes=[
            pltpu.VMEM((shards, later, LANES), BF),
            pltpu.VMEM((count, ACTS), BF),
            pltpu.VMEM((2, count, FF), BF),
            pltpu.SemaphoreType.DMA((3 + 2 * (FF // WIDE),)),
            pltpu.SemaphoreType.DMA((2,)),
        ],
        compiler_params=BIG,
        cost_estimate=cost(9),
        name="ffn_forward",
    )(op, x, na, gain, weights)


def ffn_back_body(dy, mixed, gain, gates, e_s, w_s, back, loads, spread):
    out, pairs, downs = loads
    rows = PADDED // w_s.shape[0]
    back[:, 2 * FF + PADDED :] = dy
    for h in range(2):
        downs[h].wait()
        at = h * FF // 2
        d_hidden = dot_nt(dy, down_half(w_s, h))
        g, u = (part.astype(F32) for part in gates(h))
        sig = jax.nn.sigmoid(g)
        back[:, at : at + FF // 2] = (d_hidden * u * sig * (1.0 + g * (1.0 - sig))).astype(BF)
        back[:, FF + at : FF + at + FF // 2] = (d_hidden * g * sig).astype(BF)
    grad = None
    for i in range(FF // WIDE):
        for copy in pairs[i]:
            copy.wait()
        gate, up = gate_up(w_s, i)
        part = dot_nt(back[:, i * WIDE : (i + 1) * WIDE], gate) + dot_nt(back[:, FF + i * WIDE : FF + (i + 1) * WIDE], up)
        grad = part if grad is None else grad + part
    norm, dgain = norm_back(grad, mixed, gain)
    d_mixed = dy.astype(F32) + norm
    low = d_mixed.astype(BF)
    back[:, 2 * FF : 2 * FF + PADDED] = low
    out.wait()
    d_padded = dot_nt(low, columns(w_s, 0, OUT_BLOCKS, rows)).astype(BF)
    spread.wait()
    return d_mixed, dgain, dot_nt(d_padded, e_s[...]).astype(BF)


class Loaded:
    def wait(self):
        pass


def turn_acts(core, acts, own_ref, send_ref):
    at, to = 0, 0
    for width in (FF, PADDED, PADDED, PADDED):
        turned = acts[:, at : at + width].astype(F32).T.astype(BF)
        own, send = own_rows(turned, core, width // 16)
        own_ref[to : to + width // 2, :] = own
        send_ref[to : to + width // 2, :] = send
        at, to = at + width, to + width // 2


def ffn_both_kernel(first, place, op_ref, x_ref, na_ref, gain_ref, dy_ref, e_hbm, w_hbm, *refs):
    y_ref, own_ref, send_ref, back_hbm, dm_ref, do_ref, dgain_ref, w_s, acts, gu, back, e_s, sems, others = refs
    loads = weight_copies(w_hbm, w_s, sems, first)
    spread = pltpu.make_async_copy(e_hbm, e_s, others.at[0])
    for copy in [loads[0]] + sum(loads[1], []) + loads[2] + [spread]:
        copy.start()
    mixed, gates = ffn_up(x_ref[...], op_ref[...], na_ref[...], gain_ref[...], w_s, acts, loads)
    for i, pair in enumerate(gates):
        for j in range(2):
            gu[j, :, i * WIDE : (i + 1) * WIDE] = pair[j]
    y_ref[...] = ffn_down(mixed, w_s, acts, loads[2])
    done = Loaded()
    loads = (done, [[done, done]] * (FF // WIDE), [done, done])
    halves = lambda h: [gu[j, :, h * FF // 2 : (h + 1) * FF // 2] for j in range(2)]
    dm_ref[...], dgain_ref[...], do_ref[...] = ffn_back_body(
        dy_ref[...], mixed, gain_ref[...], halves, e_s, w_s, back, loads, spread
    )
    send = pltpu.make_async_copy(back, back_hbm, others.at[1])
    send.start()
    turn_acts(place[0], acts, own_ref, send_ref)
    send.wait()


def ffn_both(place, op, x, na, gain, dy, e, weights, first):
    count = x.shape[0]
    shards = weights.shape[0]
    later = (OUT_BLOCKS + 2 * FF_BLOCKS) * (PADDED // shards) + OUT_BLOCKS * (FF // shards)
    turned = jax.ShapeDtypeStruct((ACTS // 2, count), BF)
    return pl.pallas_call(
        functools.partial(ffn_both_kernel, first),
        out_shape=(
            jax.ShapeDtypeStruct((count, PADDED), BF),
            turned,
            turned,
            jax.ShapeDtypeStruct((count, BACK), BF),
            jax.ShapeDtypeStruct((count, PADDED), F32),
            jax.ShapeDtypeStruct((count, D), BF),
            jax.ShapeDtypeStruct((1, PADDED), F32),
        ),
        in_specs=[SMEM] + [VMEM] * 5 + [ANY] * 2,
        out_specs=[VMEM] * 3 + [ANY] + [VMEM] * 3,
        scratch_shapes=[
            pltpu.VMEM((shards, later, LANES), BF),
            pltpu.VMEM((count, ACTS), BF),
            pltpu.VMEM((2, count, FF), BF),
            pltpu.VMEM((count, BACK), BF),
            pltpu.VMEM((D, PADDED), BF),
            pltpu.SemaphoreType.DMA((3 + 2 * (FF // WIDE),)),
            pltpu.SemaphoreType.DMA((2,)),
        ],
        compiler_params=BIG,
        cost_estimate=cost(20),
        name="ffn_both",
    )(place, op, x, na, gain, dy, e, weights)


def both_back_kernel(base, first, zs, dq_ref, cos_ref, sin_ref, x_ref, gain_ref, dm_ref, *refs):
    shares, refs = refs[:zs], refs[zs:]
    dgf_ref, m_ref, gain_f_ref, gu_hbm, e_hbm, wa_hbm, wf_hbm = refs[:7]
    dkv_ref, low_ref, back_hbm, dm_out, do_ref, dgain_ref, wa_s, wf_s, back, gu, e_s, sem, sems, others = refs[7:]
    copy = pltpu.make_async_copy(wa_hbm.at[:, pl.ds(base, wa_s.shape[1]), :], wa_s, sem)
    loads = weight_copies(wf_hbm, wf_s, sems, first)
    load = pltpu.make_async_copy(gu_hbm, gu, others.at[0])
    spread = pltpu.make_async_copy(e_hbm, e_s, others.at[1])
    for each in [copy] + loads[2] + [load] + sum(loads[1], []) + [loads[0], spread]:
        each.start()
    dx = qkv_back_body(dq_ref, shares, cos_ref[...], sin_ref[...], x_ref, gain_ref, dm_ref, dgf_ref, copy, wa_s, dkv_ref)
    low = dx.astype(BF)
    low_ref[...] = low
    load.wait()
    halves = lambda h: [gu[j, :, h * FF // 2 : (h + 1) * FF // 2] for j in range(2)]
    dm_out[...], dgain_ref[...], do_ref[...] = ffn_back_body(
        low, m_ref[...], gain_f_ref[...], halves, e_s, wf_s, back, loads, spread
    )
    send = pltpu.make_async_copy(back, back_hbm, others.at[2])
    send.start()
    send.wait()


def both_back(dq, shares, cos, sin, x, gain, dm, dgf, w_a, base, mixed, gain_f, gu, e, w_f, first):
    count = x.shape[0]
    shards = w_a.shape[0]
    rows = PADDED // shards
    later = (OUT_BLOCKS + 2 * FF_BLOCKS) * rows + OUT_BLOCKS * (FF // shards)
    return pl.pallas_call(
        functools.partial(both_back_kernel, base, first, len(shares)),
        out_shape=(
            jax.ShapeDtypeStruct((count + EXTRA, KVW), BF),
            jax.ShapeDtypeStruct((count, PADDED), BF),
            jax.ShapeDtypeStruct((count, BACK), BF),
            jax.ShapeDtypeStruct((count, PADDED), F32),
            jax.ShapeDtypeStruct((count, D), BF),
            jax.ShapeDtypeStruct((1, PADDED), F32),
        ),
        in_specs=[VMEM] * (9 + len(shares)) + [ANY] * 4,
        out_specs=[VMEM, VMEM, ANY] + [VMEM] * 3,
        scratch_shapes=[
            pltpu.VMEM((shards, QKV_BLOCKS * rows, LANES), BF),
            pltpu.VMEM((shards, later, LANES), BF),
            pltpu.VMEM((count, BACK), BF),
            pltpu.VMEM((2, count, FF), BF),
            pltpu.VMEM((D, PADDED), BF),
            pltpu.SemaphoreType.DMA,
            pltpu.SemaphoreType.DMA((3 + 2 * (FF // WIDE),)),
            pltpu.SemaphoreType.DMA((3,)),
        ],
        compiler_params=BIG,
        cost_estimate=cost(18),
        name="both_back",
    )(dq, cos, sin, x, gain, dm, *shares, dgf, mixed, gain_f, gu, e, w_a, w_f)


def qkv_back_body(dq_ref, shares, cos, sin, x_ref, gain_ref, dm_ref, dgf_ref, copy, w_s, dkv_ref):
    count = x_ref.shape[0]
    rows = w_s.shape[1] // QKV_BLOCKS
    for j in range(KVW // LANES):
        at = slice(j * LANES, (j + 1) * LANES)
        grad = shares[0][:, at].astype(F32)
        for share in shares[1:]:
            grad = grad + share[:, at].astype(F32)
        turned = grad * cos - half_of(grad * sin) if j < 3 else grad
        if j == 2:
            lane = lax.broadcasted_iota(jnp.int32, grad.shape, 1)
            turned = jnp.where(lane < HD, turned, grad)
        dkv_ref[:count, at] = turned.astype(BF)
    copy.wait()
    kv_blocks = KVW // LANES
    d_normed = dot_nt(dkv_ref[:count, :], columns(w_s, 0, kv_blocks, rows))
    d_normed = d_normed + dot_nt(dq_ref[...], columns(w_s, kv_blocks * rows, QKV_BLOCKS - kv_blocks, rows))
    back, dgain = norm_back(d_normed, x_ref[...].astype(F32), gain_ref[...])
    dkv_ref[count:, :] = gain_rows(dgain, dgf_ref[...])
    return dm_ref[...] + back


def qkv_back_kernel(base, zs, dq_ref, cos_ref, sin_ref, x_ref, gain_ref, dm_ref, *refs):
    shares, (dgf_ref, w_hbm, dkv_ref, dx_ref, low_ref, w_s, sem) = refs[:zs], refs[zs:]
    copy = pltpu.make_async_copy(w_hbm.at[:, pl.ds(base, w_s.shape[1]), :], w_s, sem)
    copy.start()
    dx = qkv_back_body(dq_ref, shares, cos_ref[...], sin_ref[...], x_ref, gain_ref, dm_ref, dgf_ref, copy, w_s, dkv_ref)
    dx_ref[...] = dx
    low_ref[...] = dx.astype(BF)


def gain_rows(first, second):
    half = PADDED // 2
    rows = [first[:, :half], first[:, half:], second[:, :half], second[:, half:]]
    rows = jnp.concatenate(rows + [jnp.zeros((EXTRA - 4, half), F32)], 0)
    return jnp.concatenate([rows, jnp.zeros((EXTRA, KVW - half), F32)], 1).astype(BF)


def gain_columns(own, other):
    total = own.astype(F32) + other.astype(F32)
    half = PADDED // 2
    rows = [jnp.concatenate([total[2 * i : 2 * i + 1, :half], total[2 * i + 1 : 2 * i + 2, :half]], 1) for i in range(2)]
    return jnp.concatenate(rows + [jnp.zeros((LANES - 2, PADDED), F32)], 0).T.astype(BF)


def qkv_backward(dq, shares, cos, sin, x, gain, dm, dgf, weights, base):
    count = x.shape[0]
    shards = weights.shape[0]
    rows = PADDED // shards
    return pl.pallas_call(
        functools.partial(qkv_back_kernel, base, len(shares)),
        out_shape=(
            jax.ShapeDtypeStruct((count + EXTRA, KVW), BF),
            jax.ShapeDtypeStruct((count, PADDED), F32),
            jax.ShapeDtypeStruct((count, PADDED), BF),
        ),
        in_specs=[VMEM] * (7 + len(shares)) + [ANY],
        out_specs=[VMEM] * 3,
        scratch_shapes=[pltpu.VMEM((shards, QKV_BLOCKS * rows, LANES), BF), pltpu.SemaphoreType.DMA],
        compiler_params=BIG,
        cost_estimate=cost(6),
        name="qkv_backward",
    )(dq, cos, sin, x, gain, dm, *shares, dgf, weights)


def own_rows(turned, core, rows):
    split = turned.reshape(-1, 2, rows, turned.shape[-1])
    first, second = split[:, 0].reshape(-1, turned.shape[-1]), split[:, 1].reshape(-1, turned.shape[-1])
    return jnp.where(core == 0, first, second), jnp.where(core == 0, second, first)


def turn_kernel(place, acts_ref, own_ref, send_ref):
    turn_acts(place[0], acts_ref, own_ref, send_ref)


def turn(place, acts):
    shape = jax.ShapeDtypeStruct((ACTS // 2, acts.shape[0]), BF)
    return pl.pallas_call(
        turn_kernel,
        out_shape=(shape, shape),
        in_specs=[SMEM, VMEM],
        out_specs=[VMEM] * 2,
        compiler_params=BIG,
        cost_estimate=cost(4),
        name="turn",
    )(place, acts)


def write_split(out, keep_ref, send_ref, at, rows, half):
    for i in range(out.shape[1] // LANES):
        block = out[:, i * LANES : (i + 1) * LANES].reshape(2, -1, rows, LANES)
        place = slice(at + i * rows, at + (i + 1) * rows)
        keep_ref[:, place, :] = jnp.where(half == 0, block[0], block[1])
        send_ref[:, place, :] = jnp.where(half == 0, block[1], block[0])


def grad_ffn_kernel(place, own_hbm, other_hbm, back_hbm, back_other_hbm, *refs):
    outs, (left, back, *held, sems, out_sems) = refs[:8], refs[8:]
    keep_a, send_a, keep_u, send_u = held[:2], held[2:4], held[4:6], held[6:8]
    half, section = place[1], place[2]
    count = back.shape[0] // 2
    chips = keep_a[0].shape[0]
    rows, ff_rows = PADDED // (2 * chips), FF // (2 * chips)
    steps = FF // CHUNK
    hd, op, nf = (0, FF // 2), (FF // 2, PADDED // 2), ((FF + PADDED) // 2, PADDED // 2)
    loads = []

    def load(at, width, height, first):
        group = []
        for side, (turned, wide) in enumerate(((own_hbm, back_hbm), (other_hbm, back_other_hbm))):
            place_l = (pl.ds(height[0], height[1]), pl.ds(side * count, count))
            place_b = (pl.ds(side * count, count), pl.ds(at, width))
            if first:
                group.append(pltpu.make_async_copy(turned.at[place_l[0], :], left.at[place_l], sems.at[4 * len(loads) + 2 * side]))
            group.append(pltpu.make_async_copy(wide.at[:, place_b[1]], back.at[place_b], sems.at[4 * len(loads) + 2 * side + 1]))
        loads.append(group)
        for copy in group:
            copy.start()

    load(0, FF, nf, True)
    load(2 * FF + PADDED, PADDED, hd, True)
    load(FF, FF, nf, False)
    load(2 * FF, PADDED, op, True)

    def ready(i):
        for copy in loads[i]:
            copy.wait()

    def product(which, at, width):
        return dot(left[which[0] : which[0] + which[1], :], back[:, at : at + width]).astype(BF)

    def as_blocks(out, height):
        width = out.shape[1] // LANES
        return [out[:, i * LANES : (i + 1) * LANES].reshape(chips, height, LANES) for i in range(width)]

    sent = []

    def finish(*which):
        for i in which:
            sent.append(pltpu.make_async_copy(held[i], outs[i], out_sems.at[i]))
            sent[-1].start()

    ready(0)
    ready(1)
    block = CHUNK // LANES * rows
    narrow_width = PADDED // steps
    for j in range(steps):
        gate = jnp.concatenate(as_blocks(product(nf, j * CHUNK, CHUNK), rows), 1)
        down = jnp.concatenate(as_blocks(product(hd, 2 * FF + PADDED + j * narrow_width, narrow_width), ff_rows), 1)
        at = slice(j % 2 * block, (j % 2 + 1) * block)
        keep_a[j // 2][:, at, :] = jnp.where(section == 0, down, gate)
        send_a[j // 2][:, at, :] = jnp.where(section == 0, gate, down)
        if j % 2:
            finish(j // 2, 2 + j // 2)
    ready(2)
    for j in range(steps):
        h = j // (steps - 1)
        write_split(product(nf, FF + j * CHUNK, CHUNK), keep_u[h], send_u[h], (j - h * (steps - 1)) * block, rows, half)
        if j == steps - 2:
            finish(4, 6)
    ready(3)
    write_split(product(op, 2 * FF, PADDED), keep_u[1], send_u[1], block, rows, half)
    finish(5, 7)
    for copy in sent:
        copy.wait()


def grad_ffn(place, own, other, back, back_other, shards):
    count = own.shape[1]
    chips = shards // 2
    rows = PADDED // shards
    steps = FF // CHUNK
    block = CHUNK // LANES * rows
    shapes = [(chips, 2 * block, LANES)] * 4
    shapes += [(chips // 2, height, LANES) for height in ((steps - 1) * block, block + OUT_BLOCKS * rows) * 2]
    return pl.pallas_call(
        grad_ffn_kernel,
        out_shape=[jax.ShapeDtypeStruct(shape, BF) for shape in shapes],
        in_specs=[SMEM] + [ANY] * 4,
        out_specs=[ANY] * 8,
        scratch_shapes=[pltpu.VMEM((ACTS // 2, 2 * count), BF), pltpu.VMEM((2 * count, BACK), BF)]
        + [pltpu.VMEM(shape, BF) for shape in shapes]
        + [pltpu.SemaphoreType.DMA((16,)), pltpu.SemaphoreType.DMA((8,))],
        compiler_params=BIG,
        cost_estimate=cost(11),
        name="grad_ffn",
    )(place, own, other, back, back_other)


def grad_attn_kernel(place, own, other, *refs):
    grads, keep, send = refs[:-2], refs[-2], refs[-1]
    core, half = place[0], place[1]
    count = own.shape[1]
    rows = PADDED // 16
    na = slice((FF + 2 * PADDED) // 2, ACTS // 2)
    at = 0
    for grad, grad_other in zip(grads[::2], grads[1::2]):
        if len(grad_other.shape) == 3:
            right = jnp.concatenate([grad_other[0], grad_other[1, :, : PADDED - KVW]], 1)
        else:
            right = grad_other[:count, :]
        out = (dot(own[na, :], grad[:count, :]) + dot(other[na, :], right)).astype(BF)
        write_split(out, keep, send, at, rows, half)
        at += grad.shape[1] // LANES * rows
        if grad.shape[0] > count:
            gains = gain_columns(grad[count:, :], grad_other[count:, :])
            write_split(own_rows(gains, core, rows)[0], keep, send, at, rows, half)
            at += rows


def grad_attn(place, own, other, *grads):
    rows = PADDED // 16
    blocks = sum(grad.shape[1] // LANES + (grad.shape[0] > own.shape[1]) for grad in grads[::2])
    shape = jax.ShapeDtypeStruct((4, blocks * rows, LANES), BF)
    return pl.pallas_call(
        grad_attn_kernel,
        out_shape=(shape, shape),
        in_specs=[SMEM] + [VMEM] * (2 + len(grads)),
        out_specs=[VMEM] * 2,
        compiler_params=BIG,
        cost_estimate=cost(4),
        name="grad_attn",
    )(place, own, other, *grads)


def narrow(values, spread):
    if values.dtype == BF:
        return dot_nt(values, spread)
    total, left = None, values
    for _ in range(3):
        part = left.astype(BF)
        left = left - part.astype(F32)
        out = dot_nt(part, spread)
        total = out if total is None else total + out
    return total


def narrow_t(values, spread):
    if values.dtype == BF:
        return dot_nt(spread, values)
    total, left = None, values
    for _ in range(3):
        part = left.astype(BF)
        left = left - part.astype(F32)
        out = dot_nt(spread, part)
        total = out if total is None else total + out
    return total


def sum_block(ref, other, j, height):
    at = slice(j * height, (j + 1) * height)
    out = ref[at, :].astype(F32)
    return out if other is None else out + other[at, :].astype(F32)


def sum_matrix(ref, other, first, count, height):
    return jnp.concatenate([sum_block(ref, other, first + j, height) for j in range(count)], 1)


def unpack_up_kernel(place, *refs):
    parts, (e_ref, up_ref, o_ref) = refs[:-3], refs[-3:]
    size, rows = up_ref.shape[0], parts[0].shape[0] // (FF_BLOCKS - CHUNK // LANES)
    cut = FF_BLOCKS - CHUNK // LANES
    for layer in range(2):

        @pl.when(place[2] == layer)
        def _():
            u, got_u, v, got_v = parts[4 * layer : 4 * layer + 4]
            for j in range(FF_BLOCKS):
                block = sum_block(u, got_u, j, rows) if j < cut else sum_block(v, got_v, j - cut, rows)
                up_ref[:, 0, j * LANES : (j + 1) * LANES] = block[:size]
            o_ref[:, 0, :] = narrow(sum_matrix(v, got_v, FF_BLOCKS - cut, OUT_BLOCKS, rows), e_ref[...])[:size]


def unpack_down_kernel(place, *refs):
    parts, (e_ref, gate_ref, down_ref) = refs[:-3], refs[-3:]
    size, ff_rows = gate_ref.shape[0], down_ref.shape[0]
    rows = parts[0].shape[0] // FF_BLOCKS
    for layer in range(2):

        @pl.when(place[2] == layer)
        def _():
            a, got_a = parts[2 * layer : 2 * layer + 2]
            down, gate = (a, got_a) if layer == 0 else (got_a, a)
            for j in range(FF_BLOCKS):
                gate_ref[:, 0, j * LANES : (j + 1) * LANES] = sum_block(gate, None, j, rows)[:size]
            down_ref[...] = narrow(sum_matrix(down, None, 0, OUT_BLOCKS, ff_rows), e_ref[...])


def unpack_qkv_kernel(place, *refs):
    parts, (q_ref, k_ref, v_ref, gain_ref) = refs[:-4], refs[-4:]
    size = q_ref.shape[0]
    kv_blocks = KVW // LANES
    rows = parts[0].shape[0] // (OUT_BLOCKS + kv_blocks + 1)
    for layer in range(2):

        @pl.when(place[2] == layer)
        def _():
            s, got = parts[2 * layer : 2 * layer + 2]
            q_ref[:, 0, :] = sum_matrix(s, got, 0, OUT_BLOCKS, rows)[:size, :D]
            both = sum_matrix(s, got, OUT_BLOCKS, kv_blocks, rows)
            k_ref[:, 0, :] = both[:size, : KV * HD]
            v_ref[:, 0, :] = both[:size, KV * HD :]
            gain_ref[...] = sum_block(s, got, OUT_BLOCKS + kv_blocks, rows).T


def unpack(kernel, name, place, parts, shapes):
    return pl.pallas_call(
        kernel,
        out_shape=[jax.ShapeDtypeStruct(shape, F32) for shape in shapes],
        in_specs=[SMEM] + [VMEM] * len(parts),
        out_specs=[VMEM] * len(shapes),
        compiler_params=BIG,
        cost_estimate=cost(4),
        name=name,
    )(place, *parts)


def join_kernel(place, own0, own1, got, e_ref, out_ref):
    section = place[2]
    for layer, own in enumerate((own0, own1)):

        @pl.when(section == layer)
        def _():
            out_ref[layer] = narrow_t(own[...], e_ref[...]).astype(out_ref.dtype)
            out_ref[1 - layer] = narrow_t(got[...], e_ref[...]).astype(out_ref.dtype)


def join(place, own0, own1, got, spread, dtype):
    return pl.pallas_call(
        join_kernel,
        out_shape=jax.ShapeDtypeStruct((2, D, own0.shape[0]), dtype),
        in_specs=[SMEM] + [VMEM] * 4,
        out_specs=VMEM,
        compiler_params=BIG,
        cost_estimate=cost(4),
        name="join",
    )(place, own0, own1, got, spread).transpose(0, 2, 1)


def spread_matrix(shards):
    size, room = D // shards, PADDED // shards
    feature = lax.broadcasted_iota(jnp.int32, (D, PADDED), 0)
    place = lax.broadcasted_iota(jnp.int32, (D, PADDED), 1)
    return (feature // size * room + feature % size == place).astype(BF)


def to_blocks(matrix):
    rows, width = matrix.shape
    return matrix.reshape(rows, width // LANES, LANES).transpose(1, 0, 2).reshape(-1, LANES)


def from_blocks(blocks, rows):
    return blocks.reshape(-1, rows, LANES).transpose(1, 0, 2).reshape(rows, -1)


def plus(left, right):
    return (left.astype(F32) + right.astype(F32)).astype(BF)


def after(value, *earlier):
    return lax.optimization_barrier((value,) + earlier)[0]


def scatter_z(parts):
    return lax.psum_scatter(parts, "z", scatter_dimension=0, tiled=False)


def scatter_z_small(parts, *before_last):
    count, me = lax.axis_size("z"), lax.axis_index("z")
    while parts.shape[0] > 1:
        step = parts.shape[0] // 2
        split = parts.reshape((2, step) + parts.shape[1:])
        bit = lax.rem(lax.div(me, step), 2)
        keep = lax.dynamic_index_in_dim(split, bit, 0, False)
        send = lax.dynamic_index_in_dim(split, 1 - bit, 0, False)
        if step == 1 and before_last:
            send = after(send, *before_last)
        parts = plus(keep, lax.ppermute(send, "z", [(i, i ^ step) for i in range(count)]))
    return parts[0]


def to_owner(part, layer):
    return lax.ppermute(part, "section", [(1 - layer, layer)])


def per_device_blocks(tokens, cotangent, positions, attn_gain, w_query, w_key, w_value, w_out, ffn_gain, w_gate, w_up, w_down):
    section, half = lax.axis_index("section"), lax.axis_index("dp")
    z_index, core = lax.axis_index("z"), lax.axis_index("core")
    plane = ("dp", "z", "core")
    size, ff_rows = w_query.shape[1], w_down.shape[1]
    shards = D // size
    room = PADDED // shards
    chips = shards // 2
    qkv_rows = QKV_BLOCKS * room
    block_range = jnp.stack([2 - core, 2 * z_index + 2]).astype(jnp.int32)
    place = jnp.stack([core, half, section]).astype(jnp.int32)
    spread = spread_matrix(shards)

    def mine(array_in):
        return lax.dynamic_index_in_dim(array_in, section, 0, keepdims=False)

    def widen(array_in):
        return project(array_in, spread).astype(BF)

    def padded(array_in):
        return jnp.pad(array_in, ((0, room - size), (0, 0)))

    gains = jnp.concatenate([attn_gain, ffn_gain], 0).T
    qkv = jnp.concatenate([w_key[0], w_value[0], w_query[0], gains, jnp.zeros((size, HD - 2), BF)], -1)
    narrow = jnp.concatenate([qkv, widen(w_out[0]), w_gate[0], w_up[0]], -1)
    shard = jnp.concatenate([to_blocks(padded(narrow)), to_blocks(widen(w_down[0]))], 0)
    first, rest = shard[:qkv_rows], shard[qkv_rows:]
    got_first = swap(first, "section")
    got_rest = swap(after(rest, got_first), "section")

    def layer_shard(own, got, layer):
        return jnp.where(section == layer, own, got)

    def gathered(*pieces):
        block = pieces[0] if len(pieces) == 1 else jnp.concatenate(pieces, 0)
        return lax.all_gather(block, plane, axis=0)

    def gains_at(whole, base):
        at = base + (QKV_BLOCKS - 1) * room
        gain = whole[:, at : at + room, HD : HD + 2].reshape(-1, 2).T.astype(F32)
        return gain[:1], gain[1:]

    early = gathered(layer_shard(first, got_first, 0))
    middle = gathered(layer_shard(rest, got_rest, 0), after(layer_shard(first, got_first, 1), early))
    base1 = rest.shape[0]
    w0 = (early, 0, middle, 0) + gains_at(early, 0)
    angle_cos, angle_sin = rope_tables(mine(positions))
    cos = jnp.concatenate([angle_cos[:, 0]] * 2, -1)
    sin = jnp.concatenate([angle_sin[:, 0]] * 2, -1)

    def attention(x, layer, *earlier):
        w_a, at_a, gain_a = layer[0], layer[1], layer[4]
        na, q, kv = qkv_forward(x, gain_a, cos, sin, w_a, at_a)
        kv_all = spread_kv(kv)
        o, op, lse = attend(block_range, after(q, *earlier) if earlier else q, kv_all, spread)
        return na, op, (x, q, kv_all, o, lse)

    x0 = widen(mine(tokens))
    na0, op0, saved0 = attention(x0, w0)
    late = gathered(after(layer_shard(rest, got_rest, 1), *saved0[2][0]))
    w1 = (middle, base1, late, 0) + gains_at(middle, base1)
    acts0, mixed0, gu0, y0 = ffn_forward(op0, x0, na0, w0[5], w0[2], w0[3])
    own0, send0 = turn(place, acts0)
    na1, op1, saved1 = attention(y0, w1, own0)
    y1, own1, send1, back1, dm1, do1, dgf1 = ffn_both(
        place, op1, y0, na1, w1[5], widen(mine(cotangent)), spread, w1[2], w1[3]
    )

    def backward_attn(do, saved):
        x, q, kv_all, o, lse = saved
        return attend_back(block_range, q, o, do, lse, cos, sin, kv_all)

    def backward_qkv(dq, shares, dm, dgf, layer, saved):
        w_a, at_a, w_f, at_f, gain_a, gain_f = layer
        return qkv_backward(dq, shares, cos, sin, saved[0], gain_a, dm, dgf, w_a, at_a)

    def halve(total):
        split = total.reshape((2, chips // 2) + total.shape[1:])
        return lax.dynamic_index_in_dim(split, half, 0, False), lax.dynamic_index_in_dim(split, 1 - half, 0, False)

    def scatter(*pieces, joined=None):
        if joined is None:
            joined = jnp.concatenate(pieces, 1) if len(pieces) > 1 else pieces[0]
        total = scatter_z(joined)
        cuts, at = [], 0
        for piece in pieces:
            cuts.append(total[at : at + piece.shape[1]])
            at += piece.shape[1]
        return cuts

    def cross(keep, got):
        keep, send = halve(plus(keep, got))
        return keep, swap(send, "dp")

    def swap_all(sends, axis):
        return [swap(send, axis) for send in sends]

    def all_after(values, *earlier):
        return [after(value, *earlier) for value in values]

    other0, other1 = swap(send0, "core"), swap(send1, "core")

    def swap_all(sends, axis):
        return [swap(send, axis) for send in sends]

    def query_grads(own, got):
        return own, got[-2:]

    back_other1 = swap(back1, "core")
    dq1, dkv1, away1 = backward_attn(do1, saved1)
    got1 = swap(away1, "core")
    grads1 = grad_ffn(place, own1, other1, after(back1, dkv1), back_other1, shards)
    keep_a1, send_a1, keep_u1, send_u1 = grads1[:2], grads1[2:4], grads1[4:6], grads1[6:8]
    got_a1, got_u1 = swap_all(send_a1, "section"), swap_all(send_u1, "dp")
    shares1, _ = collect_kv(dkv1, got1, [(got_a1[0], got_u1[0]), (), (send_u1[0],)])
    dkv_low1, dx1_low, back0, dm0, do0, dgf0 = both_back(
        dq1, shares1, cos, sin, y0, w1[4], dm1, dgf1, w1[0], w1[1], mixed0, w0[5], gu0, spread, w0[2], w0[3]
    )

    back0 = after(back0, got_a1[1], got_u1[1])
    got_y = swap(after(jnp.where(section == 0, y1, y0), back0), "section")
    keep_a1, keep_u1 = all_after(keep_a1, dkv_low1), all_after(keep_u1, dkv_low1)
    in_u1 = list(map(plus, keep_u1, got_u1))
    joined_u1 = jnp.concatenate(in_u1, 1)
    sum_u1 = scatter(*in_u1, joined=joined_u1)
    back_other0 = swap(back0, "core")
    grads0 = grad_ffn(place, own0, other0, after(back0, joined_u1), back_other0, shards)
    keep_a0, send_a0, keep_u0, send_u0 = grads0[:2], grads0[2:4], grads0[4:6], grads0[6:8]
    (keep_b1, got_b1), (keep_c1, got_c1) = map(cross, keep_a1, got_a1)
    got1 = after(got1, send_u0[0])
    keep_s1, send_s1 = grad_attn(place, own1, other1, *query_grads(dq1, got1), dkv_low1, swap(dkv_low1, "core"))
    got_a0 = swap_all(send_a0, "section")
    got_u0 = [swap(send_u0[0], "dp"), swap(jnp.concatenate([send_u0[1], send_s1], 1), "dp")]
    away_u1 = to_owner(jnp.concatenate(sum_u1, 0), 1)
    dq0, dkv0, away0 = backward_attn(after(do0, send_s1, got_y), saved0)
    away0 = after(away0, got_a0[0], got_u0[0], got_b1, got_c1, *sum_u1)
    keep_b1, keep_c1 = after(keep_b1, away0), after(keep_c1, away0)
    sum_a1 = scatter(plus(keep_b1, got_b1), plus(keep_c1, got_c1))
    got0 = swap(away0, "core")
    shares0, last = collect_kv(dkv0, got0, [(got_a0[1], got_u0[1])])
    keep_q0, send_q0 = grad_attn(place, own0, other0, *query_grads(dq0, got0))
    keep_b0, got_b0 = cross(after(keep_a0[0], away0), got_a0[0])
    kept = after(jnp.concatenate([keep_u0[1], keep_s1], 1), last)
    late0 = [plus(after(keep_u0[0], last), got_u0[0]), plus(kept, got_u0[1])]
    joined0 = jnp.concatenate(late0, 1)
    away_a1 = to_owner(jnp.concatenate(sum_a1, 0), 1)
    dq0 = after(dq0, send_q0, joined0, away_u1, got_b0)
    dkv_low0, dx0, dx0_low = backward_qkv(dq0, shares0, dm0, dgf0, w0, saved0)
    got_q0 = swap(after(send_q0, shares0[-1]), "dp")
    keep_c0, got_c0 = cross(after(keep_a0[1], shares0[-1]), got_a0[1])
    sum_v0, sum_w0 = scatter(*late0, joined=joined0)
    keep_k0, send_k0 = grad_attn(place, own0, other0, after(dkv_low0, got_c0), swap(dkv_low0, "core"))
    last0 = [plus(after(keep, sum_w0), got) for keep, got in ((keep_b0, got_b0), (keep_c0, got_c0))]
    sum_a0 = jnp.concatenate(scatter(*last0), 0)
    got_k0 = swap(send_k0, "dp")
    keep_q0, keep_k0 = after(keep_q0, away_a1, *last0), after(keep_k0, *last0)
    pieces = [plus(keep_q0, got_q0), plus(keep_k0, got_k0)]

    cut = send_u0[1].shape[1]
    sum_s1, sum_w0 = sum_w0[cut:], sum_w0[:cut]
    away_s1 = to_owner(sum_s1, 1)
    wide = lambda width: (size, 1, width)
    parts = [part for own in (sum_v0, sum_w0) for part in (own, to_owner(own, 0))]
    cut_u = sum_u1[0].shape[0]
    parts += [sum_u1[0], away_u1[:cut_u], sum_u1[1], away_u1[cut_u:]]
    g_up, g_o = unpack(unpack_up_kernel, "unpack_up", place, parts + [spread], (wide(FF), wide(D)))
    away_a0 = to_owner(sum_a0, 0)
    sum_s0 = scatter_z_small(jnp.concatenate(pieces, 1), g_up, away_a0)
    parts = [sum_a0, away_a0, jnp.concatenate(sum_a1, 0), away_a1]
    g_gate, g_down = unpack(unpack_down_kernel, "unpack_down", place, parts + [spread], (wide(FF), (ff_rows, D)))
    parts = [after(sum_s0, g_gate), to_owner(sum_s0, 0), sum_s1, away_s1]
    shapes = (wide(D), wide(KV * HD), wide(KV * HD), (LANES, room))
    g_q, g_k, g_v, gains = unpack(unpack_qkv_kernel, "unpack_qkv", place, parts, shapes)
    section_out = join(place, y0, y1, got_y, spread, BF)
    got = swap(jnp.where(section == 0, dx1_low, dx0_low), "section")
    input_grad = join(place, dx0, dx1_low, got, spread, F32)
    flat = lambda part: part.transpose(1, 0, 2)[0]
    g_q, g_k, g_v, g_o, g_gate, g_up = map(flat, (g_q, g_k, g_v, g_o, g_gate, g_up))
    outs = (section_out, input_grad, gains[0, :size], g_q, g_k, g_v, g_o, gains[1, :size], g_gate, g_up, g_down)
    return tuple(part[None] for part in outs)


def solution(mesh):
    sizes = mesh.devices.shape
    grid = Mesh(mesh.devices.reshape(sizes[0], sizes[1], sizes[2] // 2, 2), ("section", "dp", "z", "core"))
    ctx = ("z", "core")
    plane = ("dp", "z", "core")
    vector = P("section", plane)
    matrix = P("section", plane, None)
    in_specs = (
        P("dp", ctx, None),
        P("dp", ctx, None),
        P("dp", ctx),
        vector,
        matrix,
        matrix,
        matrix,
        matrix,
        vector,
        matrix,
        matrix,
        matrix,
    )
    acts = P("section", "dp", ctx, None)
    out_specs = (acts, acts, vector, matrix, matrix, matrix, matrix, vector, matrix, matrix, matrix)
    shards = sizes[1] * sizes[2]
    aligned = shards == 16
    return jax.shard_map(per_device_blocks if aligned else per_device, mesh=grid, in_specs=in_specs, out_specs=out_specs, check_vma=False)
```

```python
import functools

import jax
import jax.numpy as jnp
from jax import lax
from jax.experimental import pallas as pl
from jax.experimental.pallas import tpu as pltpu
from jax.sharding import Mesh
from jax.sharding import PartitionSpec as P

D = 960
H = 15
KV = 5
G = H // KV
HD = 64
FF = 2560
EPS = 1e-05
F32 = jnp.float32
BF = jnp.bfloat16


def dot(a,b): return jnp.dot(a,b,preferred_element_type=F32)

def fwd_kernel(rng, q_ref, kv_ref, o_ref, lse_ref, qt, vt, m_s, l_s, acc):
    T=q_ref.shape[0]; W=G*T
    qt[...]=q_ref[...].astype(F32).T.astype(BF)
    nb=kv_ref.shape[0]
    def step(b, first):
        vt[...]=kv_ref[b,:,KV*HD:].astype(F32).T.astype(BF)
        for g in range(KV):
            qg=jnp.concatenate([qt[(g*G+j)*HD:(g*G+j+1)*HD,:] for j in range(G)],1)
            s=dot(kv_ref[b,:,g*HD:(g+1)*HD],qg)
            if first:
                key=lax.broadcasted_iota(jnp.int32,(T,W),0)
                qry=lax.broadcasted_iota(jnp.int32,(T,W),1)%T
                s=jnp.where(key<=qry,s,-1e30)
                m=jnp.max(s,0,keepdims=True)
                p=jnp.exp(s-m)
                l_s[g:g+1,:]=jnp.sum(p,0,keepdims=True)
                acc[g*HD:(g+1)*HD,:]=dot(vt[g*HD:(g+1)*HD,:],p.astype(BF))
            else:
                mo=m_s[g:g+1,:]
                m=jnp.maximum(mo,jnp.max(s,0,keepdims=True))
                p=jnp.exp(s-m); al=jnp.exp(mo-m)
                l_s[g:g+1,:]=l_s[g:g+1,:]*al+jnp.sum(p,0,keepdims=True)
                acc[g*HD:(g+1)*HD,:]=acc[g*HD:(g+1)*HD,:]*al+dot(vt[g*HD:(g+1)*HD,:],p.astype(BF))
            m_s[g:g+1,:]=m
    step(0,True)
    def body(b,_):
        step(b,False); return 0
    lax.fori_loop(rng[0],rng[1],body,0)
    for g in range(KV):
        inv=1.0/l_s[g:g+1,:]
        lse_ref[g:g+1,:]=m_s[g:g+1,:]+jnp.log(l_s[g:g+1,:])
        og=acc[g*HD:(g+1)*HD,:]*inv
        for j in range(G):
            h=g*G+j
            o_ref[:,h*HD:(h+1)*HD]=og[:,j*T:(j+1)*T].T.astype(BF)

def attn_fwd(rng,q,kv):
    T=q.shape[0]; W=G*T
    return pl.pallas_call(fwd_kernel,
      out_shape=(jax.ShapeDtypeStruct((T,H*HD),BF),jax.ShapeDtypeStruct((KV,W),F32)),
      in_specs=[pl.BlockSpec(memory_space=pltpu.SMEM)]+[pl.BlockSpec(memory_space=pltpu.VMEM)]*2,
      out_specs=[pl.BlockSpec(memory_space=pltpu.VMEM)]*2,
      scratch_shapes=[pltpu.VMEM((H*HD,T),BF),pltpu.VMEM((KV*HD,T),BF),pltpu.VMEM((KV,W),F32),pltpu.VMEM((KV,W),F32),pltpu.VMEM((KV*HD,W),F32)],
      compiler_params=pltpu.CompilerParams(vmem_limit_bytes=48<<20),
    )(rng,q,kv)

def bwd_kernel(rng, q_ref, kv_ref, o_ref, do_ref, lse_ref, dq_ref, dkv_ref, qt, dot_, qn, don, kt, dl, dqa):
    T=q_ref.shape[0]; W=G*T
    nb=kv_ref.shape[0]
    qt[...]=q_ref[...].astype(F32).T.astype(BF)
    doT=do_ref[...].astype(F32).T
    dot_[...]=doT.astype(BF)
    oT=o_ref[...].astype(F32).T
    prod=doT*oT
    for h in range(H):
        g,j=divmod(h,G)
        dl[g:g+1,j*T:(j+1)*T]=jnp.sum(prod[h*HD:(h+1)*HD,:],0,keepdims=True)
        qn[g,j*T:(j+1)*T,:]=q_ref[:,h*HD:(h+1)*HD]
        don[g,j*T:(j+1)*T,:]=do_ref[:,h*HD:(h+1)*HD]
    def step(b, first):
        kt[...]=kv_ref[b,:,:KV*HD].astype(F32).T.astype(BF)
        for g in range(KV):
            qg=jnp.concatenate([qt[(g*G+j)*HD:(g*G+j+1)*HD,:] for j in range(G)],1)
            dg=jnp.concatenate([dot_[(g*G+j)*HD:(g*G+j+1)*HD,:] for j in range(G)],1)
            s=dot(kv_ref[b,:,g*HD:(g+1)*HD],qg)
            p=jnp.exp(s-lse_ref[g:g+1,:])
            if first:
                key=lax.broadcasted_iota(jnp.int32,(T,W),0)
                qry=lax.broadcasted_iota(jnp.int32,(T,W),1)%T
                p=jnp.where(key<=qry,p,0.0)
            dp=dot(kv_ref[b,:,(KV+g)*HD:(KV+g+1)*HD],dg)
            dz=(p*(dp-dl[g:g+1,:])).astype(BF)
            dkv_ref[b,:,(KV+g)*HD:(KV+g+1)*HD]=dot(p.astype(BF),don[g]).astype(BF)
            dkv_ref[b,:,g*HD:(g+1)*HD]=dot(dz,qn[g]).astype(BF)
            dq=dot(kt[g*HD:(g+1)*HD,:],dz)
            if first: dqa[g*HD:(g+1)*HD,:]=dq
            else: dqa[g*HD:(g+1)*HD,:]+=dq
    step(0,True)
    def body(b,_):
        step(b,False); return 0
    lax.fori_loop(rng[0],rng[1],body,0)
    def zero(b,_):
        dkv_ref[b]=jnp.zeros((T,2*KV*HD),BF); return 0
    lax.fori_loop(1,rng[0],zero,0)
    lax.fori_loop(rng[1],nb,zero,0)
    for g in range(KV):
        for j in range(G):
            h=g*G+j
            dq_ref[:,h*HD:(h+1)*HD]=(dqa[g*HD:(g+1)*HD,j*T:(j+1)*T]*HD**-0.5).T

def attn_bwd(rng,q,kv,o,do,lse):
    T=q.shape[0]; W=G*T
    return pl.pallas_call(bwd_kernel,
      out_shape=(jax.ShapeDtypeStruct((T,H*HD),F32),jax.ShapeDtypeStruct(kv.shape,BF)),
      in_specs=[pl.BlockSpec(memory_space=pltpu.SMEM)]+[pl.BlockSpec(memory_space=pltpu.VMEM)]*5,
      out_specs=[pl.BlockSpec(memory_space=pltpu.VMEM)]*2,
      scratch_shapes=[pltpu.VMEM((H*HD,T),BF),pltpu.VMEM((H*HD,T),BF),pltpu.VMEM((KV,W,HD),BF),pltpu.VMEM((KV,W,HD),BF),
        pltpu.VMEM((KV*HD,T),BF),pltpu.VMEM((KV,W),F32),pltpu.VMEM((KV*HD,W),F32)],
      compiler_params=pltpu.CompilerParams(vmem_limit_bytes=48<<20),
    )(rng,q,kv,o,do,lse)


def rotate_half(vector):
    half_dim = vector.shape[-1] // 2
    return jnp.concatenate([-vector[..., half_dim:], vector[..., :half_dim]], -1)


def rope_tables(seq_pos):
    half_dim = HD // 2
    inv_freq = 10000.0 ** (-(jnp.arange(half_dim, dtype=F32) * 2.0) / HD)
    angles = seq_pos.astype(F32)[..., None] * inv_freq
    angle_pair = jnp.concatenate([angles, angles], -1)[..., None, :]
    return (jnp.cos(angle_pair), jnp.sin(angle_pair))


def norm_forward(values_in, gain_vec):
    factor = lax.rsqrt(jnp.mean(values_in * values_in, -1, keepdims=True) + EPS)
    return (values_in * factor * gain_vec, factor)


def norm_backward(grad_in, values_in, factor, gain_vec):
    scaled = grad_in * gain_vec
    grad_back = factor * scaled - values_in * factor * factor * factor * jnp.mean(
        scaled * values_in, -1, keepdims=True
    )
    return (grad_back, jnp.sum(grad_in * values_in * factor, 0))


def swap(block, axis):
    return lax.ppermute(block, axis, [(0, 1), (1, 0)])


def move_z(block, distance):
    count = lax.axis_size("z")
    route = [(i, i + distance) for i in range(count) if 0 <= i + distance < count]
    return lax.ppermute(block, "z", route)


def gather_kv(block):
    count = lax.axis_size("z")
    own = [block] + [move_z(block, d) for d in range(1, count)]
    own = jnp.stack(own)
    other = swap(own, "core")
    return jnp.stack([own, other], 1).reshape((2 * count,) + block.shape)


def reduce_kv(blocks):
    count = lax.axis_size("z")
    blocks = blocks.reshape((count, 2) + blocks.shape[1:])
    mine = blocks[:, 0].astype(F32) + swap(blocks[:, 1], "core").astype(F32)
    total = mine[0]
    for d in range(1, count):
        total = total + move_z(mine[d].astype(BF), -d).astype(F32)
    return total


def project(left, right):
    return jnp.dot(left, right, preferred_element_type=F32)


def project_t(left, right):
    return lax.dot_general(left, right, (((1,), (1,)), ((), ())), preferred_element_type=F32)


def outer(left, right):
    return lax.dot_general(left, right, (((0,), (0,)), ((), ())), preferred_element_type=F32)


def rope(values, cosine, sine):
    count = values.shape[0]
    values = values.reshape(count, -1, HD)
    return (values * cosine + rotate_half(values) * sine).reshape(count, -1)


def rope_t(values, cosine, sine):
    count = values.shape[0]
    values = values.reshape(count, -1, HD)
    return (values * cosine - rotate_half(values * sine)).reshape(count, -1)


def layer_forward(rows, tables, weights, block_range):
    gain_a, w_qkv, w_o, gain_f, w_g, w_u, w_d = weights
    cosine, sine = tables
    normed_a, factor_a = norm_forward(rows, gain_a)
    normed_a = normed_a.astype(BF)
    qkv = project(normed_a, w_qkv)
    queries = (rope(qkv[:, :D], cosine, sine)).astype(BF) * BF(HD**-0.5)
    keys = rope(qkv[:, D : D + KV * HD], cosine, sine).astype(BF)
    values = qkv[:, D + KV * HD :].astype(BF)
    kv_all = gather_kv(jnp.concatenate([keys, values], -1))
    attended, log_total = attn_fwd(block_range, queries, kv_all)
    mixed = rows + project(attended, w_o)
    normed_f, factor_f = norm_forward(mixed, gain_f)
    normed_f = normed_f.astype(BF)
    gate_act = project(normed_f, w_g)
    up_proj = project(normed_f, w_u)
    hidden = (jax.nn.silu(gate_act) * up_proj).astype(BF)
    out = (mixed + project(hidden, w_d)).astype(BF)
    saved = (rows, factor_a, normed_a, queries, kv_all, log_total, attended, mixed, factor_f, normed_f, gate_act, up_proj, hidden)
    return out, saved


def layer_backward(grad_low, saved, tables, weights, block_range):
    gain_a, w_qkv, w_o, gain_f, w_g, w_u, w_d = weights
    cosine, sine = tables
    rows, factor_a, normed_a, queries, kv_all, log_total, attended, mixed, factor_f, normed_f, gate_act, up_proj, hidden = saved
    d_hidden = project_t(grad_low, w_d)
    sig = jax.nn.sigmoid(gate_act)
    d_gate = (d_hidden * up_proj * sig * (1.0 + gate_act * (1.0 - sig))).astype(BF)
    d_up = (d_hidden * gate_act * sig).astype(BF)
    d_normed_f = project_t(d_gate, w_g) + project_t(d_up, w_u)
    d_norm, d_gain_f = norm_backward(d_normed_f, mixed, factor_f, gain_f)
    d_mixed = grad_low.astype(F32) + d_norm
    mix_low = d_mixed.astype(BF)
    d_attended = project_t(mix_low, w_o).astype(BF)
    d_query, d_kv = attn_bwd(block_range, queries, kv_all, attended, d_attended, log_total)
    d_kv = reduce_kv(d_kv)
    d_query = rope_t(d_query, cosine, sine).astype(BF)
    d_key = rope_t(d_kv[:, : KV * HD], cosine, sine).astype(BF)
    d_value = d_kv[:, KV * HD :].astype(BF)
    d_qkv = jnp.concatenate([d_query, d_key, d_value], -1)
    d_normed_a = project_t(d_qkv, w_qkv)
    d_norm_a, d_gain_a = norm_backward(d_normed_a, rows, factor_a, gain_a)
    d_rows = d_mixed + d_norm_a
    grads = dict(
        gate=outer(normed_f, d_gate).astype(BF),
        up=outer(normed_f, d_up).astype(BF),
        down=outer(hidden, grad_low).astype(BF),
        out=outer(attended, mix_low).astype(BF),
        qkv=outer(normed_a, d_qkv).astype(BF),
        gains=jnp.stack([d_gain_a, d_gain_f]),
    )
    return d_rows, grads


def per_device(tokens, cotangent, positions, attn_gain, w_query, w_key, w_value, w_out, ffn_gain, w_gate, w_up, w_down):
    section = lax.axis_index("section")
    z_index, core = lax.axis_index("z"), lax.axis_index("core")
    plane = ("dp", "z", "core")
    group = tokens.shape[0]
    local = tokens.shape[1]
    block_range = jnp.stack([2 - core, 2 * z_index + 2]).astype(jnp.int32)

    def mine(array_in):
        return lax.dynamic_index_in_dim(array_in, section, 0, keepdims=False)

    rows = tokens.shape[1]
    shard_rows = w_query.shape[1]
    ff_rows = w_down.shape[1]
    half = ff_rows // 2
    qkvo = jnp.concatenate([w_query[0], w_key[0], w_value[0], w_out[0]], -1)
    down = jnp.concatenate([w_down[0, :half], jnp.zeros((half, 64), BF), w_down[0, half:], jnp.zeros((half, 576), BF)], -1)
    gains = jnp.concatenate([attn_gain, ffn_gain], -1)
    shard = jnp.concatenate([qkvo, w_gate[0], w_up[0], down], 0)
    shard = lax.dynamic_update_slice(shard, gains, (3 * shard_rows, 2048))
    other = swap(shard, "section")

    def assemble(block):
        whole = lax.all_gather(block, plane, axis=0)
        n = shard_rows

        def piece(lo, hi):
            return whole[:, lo : lo + n, :hi].reshape(-1, hi) if hi <= FF else None

        attn = whole[:, :n, :].reshape(n * whole.shape[0], FF)
        w_g = whole[:, n : 2 * n, :].reshape(-1, FF)
        w_u = whole[:, 2 * n : 3 * n, :].reshape(-1, FF)
        w_d = jnp.concatenate([whole[:, 3 * n :, :D], whole[:, 3 * n :, 1024 : 1024 + D]], 1).reshape(-1, D)
        gain_rows = whole[:, 3 * n, 2048 : 2048 + 2 * n].astype(F32)
        gain_a = gain_rows[:, :n].reshape(-1)
        gain_f = gain_rows[:, n:].reshape(-1)
        return gain_a, attn[:, : D + 2 * KV * HD], attn[:, D + 2 * KV * HD :], gain_f, w_g, w_u, w_d

    w0 = assemble(jnp.where(section == 0, shard, other))
    w1 = assemble(jnp.where(section == 1, shard, other))
    tables = rope_tables(mine(positions))
    out0, saved0 = layer_forward(mine(tokens).astype(F32), tables, w0, block_range)
    out1, saved1 = layer_forward(out0.astype(F32), tables, w1, block_range)
    d1, g1 = layer_backward(mine(cotangent), saved1, tables, w1, block_range)
    d1_low = d1.astype(BF)
    d0, g0 = layer_backward(d1_low, saved0, tables, w0, block_range)

    def pair(own, got):
        return jnp.where(section == 0, jnp.stack([own, got]), jnp.stack([got, own]))

    got = swap(jnp.where(section == 0, out1, out0), "section")
    section_out = pair(jnp.where(section == 0, out0, out1), got)
    got = swap(jnp.where(section == 0, d1_low, d0.astype(BF)), "section").astype(F32)
    input_grad = pair(jnp.where(section == 0, d0, d1_low.astype(F32)), got)

    def reduce(first, second):
        def scatter(part):
            return lax.psum_scatter(part, plane, scatter_dimension=0, tiled=True)

        s0, s1 = scatter(first), scatter(second)
        got = swap(jnp.where(section == 0, s1, s0), "section")
        return jnp.where(section == 0, s0, s1).astype(F32) + got.astype(F32)

    grads = {name: reduce(g0[name], g1[name]) for name in ("gate", "up", "down", "out", "qkv")}
    gain_grad = reduce(g0["gains"].T, g1["gains"].T)
    qkv = grads["qkv"]
    kd = KV * HD
    outs = (
        section_out,
        input_grad,
        gain_grad[:, 0],
        qkv[:, :D],
        qkv[:, D : D + kd],
        qkv[:, D + kd :],
        grads["out"],
        gain_grad[:, 1],
        grads["gate"],
        grads["up"],
        grads["down"],
    )
    return tuple(part[None] for part in outs)


LANES = 128
PADDED = 1024
CHUNK = 640
WIDE = 512
KVW = 2 * KV * HD
QKV_BLOCKS = 13
EXTRA = 16
ACTS = FF + 3 * PADDED
BACK = 2 * FF + 2 * PADDED
OUT_BLOCKS = PADDED // LANES
FF_BLOCKS = FF // LANES
VMEM = pl.BlockSpec(memory_space=pltpu.VMEM)
ANY = pl.BlockSpec(memory_space=pl.ANY)
SMEM = pl.BlockSpec(memory_space=pltpu.SMEM)
BIG = pltpu.CompilerParams(vmem_limit_bytes=56 << 20)


def cost(microseconds):
    return pl.CostEstimate(flops=int(microseconds * 1.15e9), bytes_accessed=int(microseconds * 3.69e6), transcendentals=0)


def dot_nt(left, right):
    return lax.dot_general(left, right, (((1,), (1,)), ((), ())), preferred_element_type=F32)


def columns(ref, first, count, rows):
    parts = [
        ref[:, first + i * rows : first + (i + 1) * rows, :].reshape(-1, LANES) for i in range(count)
    ]
    return parts[0] if count == 1 else jnp.concatenate(parts, 1)


def half_of(values):
    lane = lax.broadcasted_iota(jnp.int32, values.shape, 1)
    back = pltpu.roll(values, LANES - HD // 2, 1)
    ahead = pltpu.roll(values, HD // 2, 1)
    return jnp.where(lane % HD < HD // 2, -back, ahead)


def rms(values):
    return lax.rsqrt(jnp.sum(values * values, -1, keepdims=True) / D + EPS)


def norm_back(grad, values, gain):
    factor = rms(values)
    scaled = grad * gain
    mean = jnp.sum(scaled * values, -1, keepdims=True) / D
    back = factor * scaled - values * (factor * factor * factor * mean)
    return back, jnp.sum(grad * values * factor, 0, keepdims=True)


def load_kv(blocks, other, kv_s, sems):
    copies = [pltpu.make_async_copy(block, kv_s.at[0, d], sems.at[d]) for d, block in enumerate(blocks)]
    copies.append(pltpu.make_async_copy(other, kv_s.at[1], sems.at[len(blocks)]))
    for copy in copies:
        copy.start()
    return copies


def attend_kernel(zs, rng, q_ref, *refs):
    blocks, (other, e_hbm, o_ref, op_ref, lse_ref, kv_s, qt, vt, m_s, l_s, acc, e_s, sems) = refs[:zs], refs[zs:]
    T = q_ref.shape[0]
    W = G * T
    copies = load_kv(blocks, other, kv_s, sems)
    spread = pltpu.make_async_copy(e_hbm, e_s, sems.at[zs + 1])
    spread.start()
    qt[...] = q_ref[...].astype(F32).T.astype(BF)
    for copy in copies:
        copy.wait()

    def step(b, first):
        kv = kv_s.at[lax.rem(b, 2), lax.div(b, 2)] if not first else kv_s.at[0, 0]
        vt[...] = kv[:, KV * HD :].astype(F32).T.astype(BF)
        ats = [slice(g * HD, (g + 1) * HD) for g in range(KV)]
        scores = []
        for g in range(KV):
            qg = jnp.concatenate([qt[(g * G + j) * HD : (g * G + j + 1) * HD, :] for j in range(G)], 1)
            s = dot(kv[:, ats[g]], qg)
            if first:
                key = lax.broadcasted_iota(jnp.int32, (T, W), 0)
                query = lax.broadcasted_iota(jnp.int32, (T, W), 1) % T
                s = jnp.where(key <= query, s, -1e30)
            scores.append(s)
        probs, scales = [], []
        for g in range(KV):
            top = jnp.max(scores[g], 0, keepdims=True)
            if not first:
                old = m_s[g : g + 1, :]
                top = jnp.maximum(old, top)
                scales.append(jnp.exp(old - top))
            p = jnp.exp(scores[g] - top)
            total = jnp.sum(p, 0, keepdims=True)
            l_s[g : g + 1, :] = total if first else l_s[g : g + 1, :] * scales[g] + total
            m_s[g : g + 1, :] = top
            probs.append(p.astype(BF))
        for g in range(KV):
            out = dot(vt[ats[g], :], probs[g])
            acc[ats[g], :] = out if first else acc[ats[g], :] * scales[g] + out

    step(0, True)

    def body(b, _):
        step(b, False)
        return 0

    lax.fori_loop(rng[0], rng[1], body, 0)
    for g in range(KV):
        lse_ref[g : g + 1, :] = m_s[g : g + 1, :] + jnp.log(l_s[g : g + 1, :])
        og = acc[g * HD : (g + 1) * HD, :] / l_s[g : g + 1, :]
        for j in range(G):
            h = g * G + j
            o_ref[:, h * HD : (h + 1) * HD] = og[:, j * T : (j + 1) * T].T.astype(BF)
    spread.wait()
    op_ref[...] = dot(o_ref[...], e_s[...]).astype(BF)


def attend(rng, q, kv_all, e):
    blocks, other = kv_all
    T, zs = q.shape[0], len(blocks)
    W = G * T
    return pl.pallas_call(
        functools.partial(attend_kernel, zs),
        out_shape=(
            jax.ShapeDtypeStruct((T, D), BF),
            jax.ShapeDtypeStruct((T, PADDED), BF),
            jax.ShapeDtypeStruct((KV, W), F32),
        ),
        in_specs=[SMEM, VMEM] + [ANY] * (zs + 2),
        out_specs=[VMEM] * 3,
        scratch_shapes=[
            pltpu.VMEM((2, zs, T, KVW), BF),
            pltpu.VMEM((D, T), BF),
            pltpu.VMEM((KV * HD, T), BF),
            pltpu.VMEM((KV, W), F32),
            pltpu.VMEM((KV, W), F32),
            pltpu.VMEM((KV * HD, W), F32),
            pltpu.VMEM((D, PADDED), BF),
            pltpu.SemaphoreType.DMA((zs + 2,)),
        ],
        compiler_params=BIG,
        cost_estimate=cost(24),
        name="attend",
    )(rng, q, *blocks, other, e)


def attend_back_kernel(zs, rng, q_ref, o_ref, do_ref, lse_ref, cos_ref, sin_ref, *refs):
    blocks, (other, dq_ref, own_ref, send_ref, kv_s, qt, dot_, qn, don, kt, dl, dqa, sems, dkv_ref, out_sems) = (
        refs[:zs],
        refs[zs:],
    )
    T = q_ref.shape[0]
    W = G * T
    copies = load_kv(blocks, other, kv_s, sems)
    qt[...] = q_ref[...].astype(F32).T.astype(BF)
    do_t = do_ref[...].astype(F32).T
    dot_[...] = do_t.astype(BF)
    prod = do_t * o_ref[...].astype(F32).T
    for h in range(H):
        g, j = divmod(h, G)
        rows = slice(j * T, (j + 1) * T)
        dl[g : g + 1, rows] = jnp.sum(prod[h * HD : (h + 1) * HD, :], 0, keepdims=True)
        qn[g, rows, :] = q_ref[:, h * HD : (h + 1) * HD]
        don[g, rows, :] = do_ref[:, h * HD : (h + 1) * HD]
    for copy in copies:
        copy.wait()

    def step(b, first):
        side, far = (0, 0) if first else (lax.rem(b, 2), lax.div(b, 2))
        kv = kv_s.at[side, far]
        out = dkv_ref.at[side, far]
        kt[...] = kv[:, : KV * HD].astype(F32).T.astype(BF)
        for g in range(KV):
            at = slice(g * HD, (g + 1) * HD)
            vat = slice((KV + g) * HD, (KV + g + 1) * HD)
            heads = [slice((g * G + j) * HD, (g * G + j + 1) * HD) for j in range(G)]
            s = dot(kv[:, at], jnp.concatenate([qt[h, :] for h in heads], 1))
            p = jnp.exp(s - lse_ref[g : g + 1, :])
            if first:
                key = lax.broadcasted_iota(jnp.int32, (T, W), 0)
                query = lax.broadcasted_iota(jnp.int32, (T, W), 1) % T
                p = jnp.where(key <= query, p, 0.0)
            dp = dot(kv[:, vat], jnp.concatenate([dot_[h, :] for h in heads], 1))
            dz = (p * (dp - dl[g : g + 1, :])).astype(BF)
            out[:, vat] = dot(p.astype(BF), don[g]).astype(BF)
            out[:, at] = dot(dz, qn[g]).astype(BF)
            dq = dot(kt[at, :], dz)
            if first:
                dqa[at, :] = dq
            else:
                dqa[at, :] += dq

    step(0, True)

    def body(b, _):
        step(b, False)
        return 0

    def zero(b, _):
        dkv_ref[lax.rem(b, 2), lax.div(b, 2)] = jnp.zeros((T, KVW), BF)
        return 0

    lax.fori_loop(rng[0], rng[1], body, 0)
    lax.fori_loop(1, rng[0], zero, 0)
    lax.fori_loop(rng[1], 2 * zs, zero, 0)
    cos, sin = cos_ref[...], sin_ref[...]
    for pair in range(PADDED // LANES):
        parts = []
        for h in (2 * pair, 2 * pair + 1):
            g, j = divmod(h, G)
            if h < H:
                parts.append(dqa[g * HD : (g + 1) * HD, j * T : (j + 1) * T] * HD**-0.5)
            else:
                parts.append(jnp.zeros((HD, T), F32))
        grad = jnp.concatenate(parts, 0).T
        turned = grad * cos - half_of(grad * sin)
        dq_ref[:, pair * LANES : (pair + 1) * LANES] = turned.astype(BF)
    kv_s[0, 0] = dq_ref[:, :KVW]
    kv_s[0, 1, :, : PADDED - KVW] = dq_ref[:, KVW:]
    copies = [
        pltpu.make_async_copy(dkv_ref.at[0], own_ref, out_sems.at[0]),
        pltpu.make_async_copy(dkv_ref.at[1], send_ref.at[pl.ds(0, zs)], out_sems.at[1]),
        pltpu.make_async_copy(kv_s.at[0, pl.ds(0, 2)], send_ref.at[pl.ds(zs, 2)], out_sems.at[2]),
    ]
    for copy in copies:
        copy.start()
    for copy in copies:
        copy.wait()


def attend_back(rng, q, o, do, lse, cos, sin, kv_all):
    blocks, other = kv_all
    T, zs = q.shape[0], len(blocks)
    W = G * T
    return pl.pallas_call(
        functools.partial(attend_back_kernel, zs),
        out_shape=(
            jax.ShapeDtypeStruct((T, PADDED), BF),
            jax.ShapeDtypeStruct((zs, T, KVW), BF),
            jax.ShapeDtypeStruct((zs + 2, T, KVW), BF),
        ),
        in_specs=[SMEM] + [VMEM] * 6 + [ANY] * (zs + 1),
        out_specs=[VMEM, ANY, ANY],
        scratch_shapes=[
            pltpu.VMEM((2, zs, T, KVW), BF),
            pltpu.VMEM((D, T), BF),
            pltpu.VMEM((D, T), BF),
            pltpu.VMEM((KV, W, HD), BF),
            pltpu.VMEM((KV, W, HD), BF),
            pltpu.VMEM((KV * HD, T), BF),
            pltpu.VMEM((KV, W), F32),
            pltpu.VMEM((KV * HD, W), F32),
            pltpu.SemaphoreType.DMA((zs + 1,)),
            pltpu.VMEM((2, zs, T, KVW), BF),
            pltpu.SemaphoreType.DMA((3,)),
        ],
        compiler_params=BIG,
        cost_estimate=cost(24),
        name="attend_back",
    )(rng, q, o, do, lse, cos, sin, *blocks, other)


def spread_kv(block):
    blocks = [block] + [move_z(block, d) for d in range(1, lax.axis_size("z"))]
    return blocks, swap(jnp.stack(blocks), "core")


def collect_kv(grads, got, before=()):
    count = lax.axis_size("z")
    moving = plus(grads[count - 1], got[count - 1])
    for d in range(count - 2, -1, -1):
        moving = after(moving, *before[d]) if d < len(before) else moving
        moved = move_z(moving, -1)
        own = plus(grads[d], got[d])
        if d == 0:
            return [own, moved], moving
        moving = plus(own, moved)


def qkv_kernel(base, x_ref, gain_ref, cos_ref, sin_ref, w_hbm, na_ref, q_ref, kv_ref, w_s, sem):
    rows = w_s.shape[1] // QKV_BLOCKS
    copy = pltpu.make_async_copy(w_hbm.at[:, pl.ds(base, w_s.shape[1]), :], w_s, sem)
    copy.start()
    x = x_ref[...].astype(F32)
    normed = (x * rms(x) * gain_ref[...]).astype(BF)
    na_ref[...] = normed
    copy.wait()
    cos, sin = cos_ref[...], sin_ref[...]
    for j in range(QKV_BLOCKS):
        out = dot(normed, columns(w_s, j * rows, 1, rows))
        if j < 5:
            turned = out * cos + half_of(out) * sin if j < 3 else out
            if j == 2:
                lane = lax.broadcasted_iota(jnp.int32, out.shape, 1)
                turned = jnp.where(lane < HD, turned, out)
            kv_ref[:, j * LANES : (j + 1) * LANES] = turned.astype(BF)
        else:
            turned = (out * cos + half_of(out) * sin).astype(BF) * BF(HD**-0.5)
            at = (j - 5) * LANES
            width = min(LANES, D - at)
            q_ref[:, at : at + width] = turned[:, :width]


def qkv_forward(x, gain, cos, sin, weights, base):
    count = x.shape[0]
    shards = weights.shape[0]
    rows = PADDED // shards
    return pl.pallas_call(
        functools.partial(qkv_kernel, base),
        out_shape=(
            jax.ShapeDtypeStruct((count, PADDED), BF),
            jax.ShapeDtypeStruct((count, D), BF),
            jax.ShapeDtypeStruct((count, KVW), BF),
        ),
        in_specs=[VMEM] * 4 + [ANY],
        out_specs=[VMEM] * 3,
        scratch_shapes=[pltpu.VMEM((shards, QKV_BLOCKS * rows, LANES), BF), pltpu.SemaphoreType.DMA],
        compiler_params=BIG,
        cost_estimate=cost(6),
        name="qkv_forward",
    )(x, gain, cos, sin, weights)


def weight_copies(w_hbm, w_s, sems, first):
    shards = w_hbm.shape[0]
    rows, ff_rows = PADDED // shards, FF // shards
    gate = OUT_BLOCKS * rows
    up = gate + FF_BLOCKS * rows
    down = up + FF_BLOCKS * rows
    step = WIDE // LANES * rows
    everyone = pl.ds(0, shards)
    places = [(everyone, 0, gate)]
    places += [(everyone, at + i * step, step) for i in range(FF // WIDE) for at in (gate, up)]
    places += [(pl.ds(h * shards // 2, shards // 2), down, OUT_BLOCKS * ff_rows) for h in range(2)]
    copies = []
    for i, (who, at, height) in enumerate(places):
        source, target = w_hbm.at[who, pl.ds(first + at, height), :], w_s.at[who, pl.ds(at, height), :]
        copies.append(pltpu.make_async_copy(source, target, sems.at[i]))
    pairs = [copies[1 + 2 * i : 3 + 2 * i] for i in range(FF // WIDE)]
    return copies[0], pairs, copies[-2:]


def gate_up(w_s, i):
    rows = PADDED // w_s.shape[0]
    at = OUT_BLOCKS * rows + i * (WIDE // LANES) * rows
    return [columns(w_s, at + j * FF_BLOCKS * rows, WIDE // LANES, rows) for j in range(2)]


def down_half(w_s, h):
    shards = w_s.shape[0]
    rows, ff_rows = PADDED // shards, FF // shards
    at = (OUT_BLOCKS + 2 * FF_BLOCKS) * rows
    who = slice(h * shards // 2, (h + 1) * shards // 2)
    parts = [w_s[who, at + i * ff_rows : at + (i + 1) * ff_rows, :].reshape(-1, LANES) for i in range(OUT_BLOCKS)]
    return jnp.concatenate(parts, 1)


def ffn_up(x, op, na, gain, w_s, acts, loads):
    out, pairs, downs = loads
    rows = PADDED // w_s.shape[0]
    acts[:, FF : FF + PADDED] = op
    acts[:, FF + 2 * PADDED :] = na
    out.wait()
    mixed = x.astype(F32) + dot(op, columns(w_s, 0, OUT_BLOCKS, rows))
    normed = (mixed * rms(mixed) * gain).astype(BF)
    acts[:, FF + PADDED : FF + 2 * PADDED] = normed
    gates = []
    for i in range(FF // WIDE):
        for copy in pairs[i]:
            copy.wait()
        gate, up = gate_up(w_s, i)
        g, u = dot(normed, gate), dot(normed, up)
        acts[:, i * WIDE : (i + 1) * WIDE] = (g * jax.nn.sigmoid(g) * u).astype(BF)
        gates.append((g.astype(BF), u.astype(BF)))
    return mixed, gates


def ffn_down(mixed, w_s, acts, downs):
    total = mixed
    for h in range(2):
        downs[h].wait()
        total = total + dot(acts[:, h * FF // 2 : (h + 1) * FF // 2], down_half(w_s, h))
    return total.astype(BF)


def ffn_kernel(first, op_ref, x_ref, na_ref, gain_ref, w_hbm, acts_hbm, m_ref, gu_hbm, y_ref, w_s, acts, gu, sems, outs):
    loads = weight_copies(w_hbm, w_s, sems, first)
    for copy in [loads[0]] + sum(loads[1], []) + loads[2]:
        copy.start()
    mixed, gates = ffn_up(x_ref[...], op_ref[...], na_ref[...], gain_ref[...], w_s, acts, loads)
    m_ref[...] = mixed
    for i, pair in enumerate(gates):
        for j in range(2):
            gu[j, :, i * WIDE : (i + 1) * WIDE] = pair[j]
    sends = [pltpu.make_async_copy(acts, acts_hbm, outs.at[0]), pltpu.make_async_copy(gu, gu_hbm, outs.at[1])]
    for copy in sends:
        copy.start()
    y_ref[...] = ffn_down(mixed, w_s, acts, loads[2])
    for copy in sends:
        copy.wait()


def ffn_forward(op, x, na, gain, weights, first):
    count = x.shape[0]
    shards = weights.shape[0]
    later = (OUT_BLOCKS + 2 * FF_BLOCKS) * (PADDED // shards) + OUT_BLOCKS * (FF // shards)
    return pl.pallas_call(
        functools.partial(ffn_kernel, first),
        out_shape=(
            jax.ShapeDtypeStruct((count, ACTS), BF),
            jax.ShapeDtypeStruct((count, PADDED), F32),
            jax.ShapeDtypeStruct((2, count, FF), BF),
            jax.ShapeDtypeStruct((count, PADDED), BF),
        ),
        in_specs=[VMEM] * 4 + [ANY],
        out_specs=[ANY, VMEM, ANY, VMEM],
        scratch_shapes=[
            pltpu.VMEM((shards, later, LANES), BF),
            pltpu.VMEM((count, ACTS), BF),
            pltpu.VMEM((2, count, FF), BF),
            pltpu.SemaphoreType.DMA((3 + 2 * (FF // WIDE),)),
            pltpu.SemaphoreType.DMA((2,)),
        ],
        compiler_params=BIG,
        cost_estimate=cost(9),
        name="ffn_forward",
    )(op, x, na, gain, weights)


def ffn_back_body(dy, mixed, gain, gates, e_s, w_s, back, loads, spread):
    out, pairs, downs = loads
    rows = PADDED // w_s.shape[0]
    back[:, 2 * FF + PADDED :] = dy
    for h in range(2):
        downs[h].wait()
        at = h * FF // 2
        d_hidden = dot_nt(dy, down_half(w_s, h))
        g, u = (part.astype(F32) for part in gates(h))
        sig = jax.nn.sigmoid(g)
        back[:, at : at + FF // 2] = (d_hidden * u * sig * (1.0 + g * (1.0 - sig))).astype(BF)
        back[:, FF + at : FF + at + FF // 2] = (d_hidden * g * sig).astype(BF)
    grad = None
    for i in range(FF // WIDE):
        for copy in pairs[i]:
            copy.wait()
        gate, up = gate_up(w_s, i)
        part = dot_nt(back[:, i * WIDE : (i + 1) * WIDE], gate) + dot_nt(back[:, FF + i * WIDE : FF + (i + 1) * WIDE], up)
        grad = part if grad is None else grad + part
    norm, dgain = norm_back(grad, mixed, gain)
    d_mixed = dy.astype(F32) + norm
    low = d_mixed.astype(BF)
    back[:, 2 * FF : 2 * FF + PADDED] = low
    out.wait()
    d_padded = dot_nt(low, columns(w_s, 0, OUT_BLOCKS, rows)).astype(BF)
    spread.wait()
    return d_mixed, dgain, dot_nt(d_padded, e_s[...]).astype(BF)


class Loaded:
    def wait(self):
        pass


def turn_acts(core, acts, own_ref, send_ref):
    at, to = 0, 0
    for width in (FF, PADDED, PADDED, PADDED):
        turned = acts[:, at : at + width].astype(F32).T.astype(BF)
        own, send = own_rows(turned, core, width // 16)
        own_ref[to : to + width // 2, :] = own
        send_ref[to : to + width // 2, :] = send
        at, to = at + width, to + width // 2


def ffn_both_kernel(first, place, op_ref, x_ref, na_ref, gain_ref, dy_ref, e_hbm, w_hbm, *refs):
    y_ref, own_ref, send_ref, back_hbm, dm_ref, do_ref, dgain_ref, w_s, acts, gu, back, e_s, sems, others = refs
    loads = weight_copies(w_hbm, w_s, sems, first)
    spread = pltpu.make_async_copy(e_hbm, e_s, others.at[0])
    for copy in [loads[0]] + sum(loads[1], []) + loads[2] + [spread]:
        copy.start()
    mixed, gates = ffn_up(x_ref[...], op_ref[...], na_ref[...], gain_ref[...], w_s, acts, loads)
    for i, pair in enumerate(gates):
        for j in range(2):
            gu[j, :, i * WIDE : (i + 1) * WIDE] = pair[j]
    y_ref[...] = ffn_down(mixed, w_s, acts, loads[2])
    done = Loaded()
    loads = (done, [[done, done]] * (FF // WIDE), [done, done])
    halves = lambda h: [gu[j, :, h * FF // 2 : (h + 1) * FF // 2] for j in range(2)]
    dm_ref[...], dgain_ref[...], do_ref[...] = ffn_back_body(
        dy_ref[...], mixed, gain_ref[...], halves, e_s, w_s, back, loads, spread
    )
    send = pltpu.make_async_copy(back, back_hbm, others.at[1])
    send.start()
    turn_acts(place[0], acts, own_ref, send_ref)
    send.wait()


def ffn_both(place, op, x, na, gain, dy, e, weights, first):
    count = x.shape[0]
    shards = weights.shape[0]
    later = (OUT_BLOCKS + 2 * FF_BLOCKS) * (PADDED // shards) + OUT_BLOCKS * (FF // shards)
    turned = jax.ShapeDtypeStruct((ACTS // 2, count), BF)
    return pl.pallas_call(
        functools.partial(ffn_both_kernel, first),
        out_shape=(
            jax.ShapeDtypeStruct((count, PADDED), BF),
            turned,
            turned,
            jax.ShapeDtypeStruct((count, BACK), BF),
            jax.ShapeDtypeStruct((count, PADDED), F32),
            jax.ShapeDtypeStruct((count, D), BF),
            jax.ShapeDtypeStruct((1, PADDED), F32),
        ),
        in_specs=[SMEM] + [VMEM] * 5 + [ANY] * 2,
        out_specs=[VMEM] * 3 + [ANY] + [VMEM] * 3,
        scratch_shapes=[
            pltpu.VMEM((shards, later, LANES), BF),
            pltpu.VMEM((count, ACTS), BF),
            pltpu.VMEM((2, count, FF), BF),
            pltpu.VMEM((count, BACK), BF),
            pltpu.VMEM((D, PADDED), BF),
            pltpu.SemaphoreType.DMA((3 + 2 * (FF // WIDE),)),
            pltpu.SemaphoreType.DMA((2,)),
        ],
        compiler_params=BIG,
        cost_estimate=cost(20),
        name="ffn_both",
    )(place, op, x, na, gain, dy, e, weights)


def both_back_kernel(base, first, zs, dq_ref, cos_ref, sin_ref, x_ref, gain_ref, dm_ref, *refs):
    shares, refs = refs[:zs], refs[zs:]
    dgf_ref, m_ref, gain_f_ref, gu_hbm, e_hbm, wa_hbm, wf_hbm = refs[:7]
    dkv_ref, low_ref, back_hbm, dm_out, do_ref, dgain_ref, wa_s, wf_s, back, gu, e_s, sem, sems, others = refs[7:]
    copy = pltpu.make_async_copy(wa_hbm.at[:, pl.ds(base, wa_s.shape[1]), :], wa_s, sem)
    loads = weight_copies(wf_hbm, wf_s, sems, first)
    load = pltpu.make_async_copy(gu_hbm, gu, others.at[0])
    spread = pltpu.make_async_copy(e_hbm, e_s, others.at[1])
    for each in [copy] + loads[2] + [load] + sum(loads[1], []) + [loads[0], spread]:
        each.start()
    dx = qkv_back_body(dq_ref, shares, cos_ref[...], sin_ref[...], x_ref, gain_ref, dm_ref, dgf_ref, copy, wa_s, dkv_ref)
    low = dx.astype(BF)
    low_ref[...] = low
    load.wait()
    halves = lambda h: [gu[j, :, h * FF // 2 : (h + 1) * FF // 2] for j in range(2)]
    dm_out[...], dgain_ref[...], do_ref[...] = ffn_back_body(
        low, m_ref[...], gain_f_ref[...], halves, e_s, wf_s, back, loads, spread
    )
    send = pltpu.make_async_copy(back, back_hbm, others.at[2])
    send.start()
    send.wait()


def both_back(dq, shares, cos, sin, x, gain, dm, dgf, w_a, base, mixed, gain_f, gu, e, w_f, first):
    count = x.shape[0]
    shards = w_a.shape[0]
    rows = PADDED // shards
    later = (OUT_BLOCKS + 2 * FF_BLOCKS) * rows + OUT_BLOCKS * (FF // shards)
    return pl.pallas_call(
        functools.partial(both_back_kernel, base, first, len(shares)),
        out_shape=(
            jax.ShapeDtypeStruct((count + EXTRA, KVW), BF),
            jax.ShapeDtypeStruct((count, PADDED), BF),
            jax.ShapeDtypeStruct((count, BACK), BF),
            jax.ShapeDtypeStruct((count, PADDED), F32),
            jax.ShapeDtypeStruct((count, D), BF),
            jax.ShapeDtypeStruct((1, PADDED), F32),
        ),
        in_specs=[VMEM] * (9 + len(shares)) + [ANY] * 4,
        out_specs=[VMEM, VMEM, ANY] + [VMEM] * 3,
        scratch_shapes=[
            pltpu.VMEM((shards, QKV_BLOCKS * rows, LANES), BF),
            pltpu.VMEM((shards, later, LANES), BF),
            pltpu.VMEM((count, BACK), BF),
            pltpu.VMEM((2, count, FF), BF),
            pltpu.VMEM((D, PADDED), BF),
            pltpu.SemaphoreType.DMA,
            pltpu.SemaphoreType.DMA((3 + 2 * (FF // WIDE),)),
            pltpu.SemaphoreType.DMA((3,)),
        ],
        compiler_params=BIG,
        cost_estimate=cost(18),
        name="both_back",
    )(dq, cos, sin, x, gain, dm, *shares, dgf, mixed, gain_f, gu, e, w_a, w_f)


def qkv_back_body(dq_ref, shares, cos, sin, x_ref, gain_ref, dm_ref, dgf_ref, copy, w_s, dkv_ref):
    count = x_ref.shape[0]
    rows = w_s.shape[1] // QKV_BLOCKS
    for j in range(KVW // LANES):
        at = slice(j * LANES, (j + 1) * LANES)
        grad = shares[0][:, at].astype(F32)
        for share in shares[1:]:
            grad = grad + share[:, at].astype(F32)
        turned = grad * cos - half_of(grad * sin) if j < 3 else grad
        if j == 2:
            lane = lax.broadcasted_iota(jnp.int32, grad.shape, 1)
            turned = jnp.where(lane < HD, turned, grad)
        dkv_ref[:count, at] = turned.astype(BF)
    copy.wait()
    kv_blocks = KVW // LANES
    d_normed = dot_nt(dkv_ref[:count, :], columns(w_s, 0, kv_blocks, rows))
    d_normed = d_normed + dot_nt(dq_ref[...], columns(w_s, kv_blocks * rows, QKV_BLOCKS - kv_blocks, rows))
    back, dgain = norm_back(d_normed, x_ref[...].astype(F32), gain_ref[...])
    dkv_ref[count:, :] = gain_rows(dgain, dgf_ref[...])
    return dm_ref[...] + back


def qkv_back_kernel(base, zs, dq_ref, cos_ref, sin_ref, x_ref, gain_ref, dm_ref, *refs):
    shares, (dgf_ref, w_hbm, dkv_ref, dx_ref, low_ref, w_s, sem) = refs[:zs], refs[zs:]
    copy = pltpu.make_async_copy(w_hbm.at[:, pl.ds(base, w_s.shape[1]), :], w_s, sem)
    copy.start()
    dx = qkv_back_body(dq_ref, shares, cos_ref[...], sin_ref[...], x_ref, gain_ref, dm_ref, dgf_ref, copy, w_s, dkv_ref)
    dx_ref[...] = dx
    low_ref[...] = dx.astype(BF)


def gain_rows(first, second):
    half = PADDED // 2
    rows = [first[:, :half], first[:, half:], second[:, :half], second[:, half:]]
    rows = jnp.concatenate(rows + [jnp.zeros((EXTRA - 4, half), F32)], 0)
    return jnp.concatenate([rows, jnp.zeros((EXTRA, KVW - half), F32)], 1).astype(BF)


def gain_columns(own, other):
    total = own.astype(F32) + other.astype(F32)
    half = PADDED // 2
    rows = [jnp.concatenate([total[2 * i : 2 * i + 1, :half], total[2 * i + 1 : 2 * i + 2, :half]], 1) for i in range(2)]
    return jnp.concatenate(rows + [jnp.zeros((LANES - 2, PADDED), F32)], 0).T.astype(BF)


def qkv_backward(dq, shares, cos, sin, x, gain, dm, dgf, weights, base):
    count = x.shape[0]
    shards = weights.shape[0]
    rows = PADDED // shards
    return pl.pallas_call(
        functools.partial(qkv_back_kernel, base, len(shares)),
        out_shape=(
            jax.ShapeDtypeStruct((count + EXTRA, KVW), BF),
            jax.ShapeDtypeStruct((count, PADDED), F32),
            jax.ShapeDtypeStruct((count, PADDED), BF),
        ),
        in_specs=[VMEM] * (7 + len(shares)) + [ANY],
        out_specs=[VMEM] * 3,
        scratch_shapes=[pltpu.VMEM((shards, QKV_BLOCKS * rows, LANES), BF), pltpu.SemaphoreType.DMA],
        compiler_params=BIG,
        cost_estimate=cost(6),
        name="qkv_backward",
    )(dq, cos, sin, x, gain, dm, *shares, dgf, weights)


def own_rows(turned, core, rows):
    split = turned.reshape(-1, 2, rows, turned.shape[-1])
    first, second = split[:, 0].reshape(-1, turned.shape[-1]), split[:, 1].reshape(-1, turned.shape[-1])
    return jnp.where(core == 0, first, second), jnp.where(core == 0, second, first)


def turn_kernel(place, acts_ref, own_ref, send_ref):
    turn_acts(place[0], acts_ref, own_ref, send_ref)


def turn(place, acts):
    shape = jax.ShapeDtypeStruct((ACTS // 2, acts.shape[0]), BF)
    return pl.pallas_call(
        turn_kernel,
        out_shape=(shape, shape),
        in_specs=[SMEM, VMEM],
        out_specs=[VMEM] * 2,
        compiler_params=BIG,
        cost_estimate=cost(4),
        name="turn",
    )(place, acts)


def write_split(out, keep_ref, send_ref, at, rows, half):
    for i in range(out.shape[1] // LANES):
        block = out[:, i * LANES : (i + 1) * LANES].reshape(2, -1, rows, LANES)
        place = slice(at + i * rows, at + (i + 1) * rows)
        keep_ref[:, place, :] = jnp.where(half == 0, block[0], block[1])
        send_ref[:, place, :] = jnp.where(half == 0, block[1], block[0])


def grad_ffn_kernel(place, own_hbm, other_hbm, back_hbm, back_other_hbm, *refs):
    outs, (left, back, *held, sems, out_sems) = refs[:8], refs[8:]
    keep_a, send_a, keep_u, send_u = held[:2], held[2:4], held[4:6], held[6:8]
    half, section = place[1], place[2]
    count = back.shape[0] // 2
    chips = keep_a[0].shape[0]
    rows, ff_rows = PADDED // (2 * chips), FF // (2 * chips)
    steps = FF // CHUNK
    hd, op, nf = (0, FF // 2), (FF // 2, PADDED // 2), ((FF + PADDED) // 2, PADDED // 2)
    loads = []

    def load(at, width, height, first):
        group = []
        for side, (turned, wide) in enumerate(((own_hbm, back_hbm), (other_hbm, back_other_hbm))):
            place_l = (pl.ds(height[0], height[1]), pl.ds(side * count, count))
            place_b = (pl.ds(side * count, count), pl.ds(at, width))
            if first:
                group.append(pltpu.make_async_copy(turned.at[place_l[0], :], left.at[place_l], sems.at[4 * len(loads) + 2 * side]))
            group.append(pltpu.make_async_copy(wide.at[:, place_b[1]], back.at[place_b], sems.at[4 * len(loads) + 2 * side + 1]))
        loads.append(group)
        for copy in group:
            copy.start()

    load(0, FF, nf, True)
    load(2 * FF + PADDED, PADDED, hd, True)
    load(FF, FF, nf, False)
    load(2 * FF, PADDED, op, True)

    def ready(i):
        for copy in loads[i]:
            copy.wait()

    def product(which, at, width):
        return dot(left[which[0] : which[0] + which[1], :], back[:, at : at + width]).astype(BF)

    def as_blocks(out, height):
        width = out.shape[1] // LANES
        return [out[:, i * LANES : (i + 1) * LANES].reshape(chips, height, LANES) for i in range(width)]

    sent = []

    def finish(*which):
        for i in which:
            sent.append(pltpu.make_async_copy(held[i], outs[i], out_sems.at[i]))
            sent[-1].start()

    ready(0)
    ready(1)
    block = CHUNK // LANES * rows
    narrow_width = PADDED // steps
    for j in range(steps):
        gate = jnp.concatenate(as_blocks(product(nf, j * CHUNK, CHUNK), rows), 1)
        down = jnp.concatenate(as_blocks(product(hd, 2 * FF + PADDED + j * narrow_width, narrow_width), ff_rows), 1)
        at = slice(j % 2 * block, (j % 2 + 1) * block)
        keep_a[j // 2][:, at, :] = jnp.where(section == 0, down, gate)
        send_a[j // 2][:, at, :] = jnp.where(section == 0, gate, down)
        if j % 2:
            finish(j // 2, 2 + j // 2)
    ready(2)
    for j in range(steps):
        h = j // (steps - 1)
        write_split(product(nf, FF + j * CHUNK, CHUNK), keep_u[h], send_u[h], (j - h * (steps - 1)) * block, rows, half)
        if j == steps - 2:
            finish(4, 6)
    ready(3)
    write_split(product(op, 2 * FF, PADDED), keep_u[1], send_u[1], block, rows, half)
    finish(5, 7)
    for copy in sent:
        copy.wait()


def grad_ffn(place, own, other, back, back_other, shards):
    count = own.shape[1]
    chips = shards // 2
    rows = PADDED // shards
    steps = FF // CHUNK
    block = CHUNK // LANES * rows
    shapes = [(chips, 2 * block, LANES)] * 4
    shapes += [(chips // 2, height, LANES) for height in ((steps - 1) * block, block + OUT_BLOCKS * rows) * 2]
    return pl.pallas_call(
        grad_ffn_kernel,
        out_shape=[jax.ShapeDtypeStruct(shape, BF) for shape in shapes],
        in_specs=[SMEM] + [ANY] * 4,
        out_specs=[ANY] * 8,
        scratch_shapes=[pltpu.VMEM((ACTS // 2, 2 * count), BF), pltpu.VMEM((2 * count, BACK), BF)]
        + [pltpu.VMEM(shape, BF) for shape in shapes]
        + [pltpu.SemaphoreType.DMA((16,)), pltpu.SemaphoreType.DMA((8,))],
        compiler_params=BIG,
        cost_estimate=cost(11),
        name="grad_ffn",
    )(place, own, other, back, back_other)


def grad_attn_kernel(place, own, other, *refs):
    grads, keep, send = refs[:-2], refs[-2], refs[-1]
    core, half = place[0], place[1]
    count = own.shape[1]
    rows = PADDED // 16
    na = slice((FF + 2 * PADDED) // 2, ACTS // 2)
    at = 0
    for grad, grad_other in zip(grads[::2], grads[1::2]):
        if len(grad_other.shape) == 3:
            right = jnp.concatenate([grad_other[0], grad_other[1, :, : PADDED - KVW]], 1)
        else:
            right = grad_other[:count, :]
        out = (dot(own[na, :], grad[:count, :]) + dot(other[na, :], right)).astype(BF)
        write_split(out, keep, send, at, rows, half)
        at += grad.shape[1] // LANES * rows
        if grad.shape[0] > count:
            gains = gain_columns(grad[count:, :], grad_other[count:, :])
            write_split(own_rows(gains, core, rows)[0], keep, send, at, rows, half)
            at += rows


def grad_attn(place, own, other, *grads):
    rows = PADDED // 16
    blocks = sum(grad.shape[1] // LANES + (grad.shape[0] > own.shape[1]) for grad in grads[::2])
    shape = jax.ShapeDtypeStruct((4, blocks * rows, LANES), BF)
    return pl.pallas_call(
        grad_attn_kernel,
        out_shape=(shape, shape),
        in_specs=[SMEM] + [VMEM] * (2 + len(grads)),
        out_specs=[VMEM] * 2,
        compiler_params=BIG,
        cost_estimate=cost(4),
        name="grad_attn",
    )(place, own, other, *grads)


def narrow(values, spread):
    if values.dtype == BF:
        return dot_nt(values, spread)
    total, left = None, values
    for _ in range(3):
        part = left.astype(BF)
        left = left - part.astype(F32)
        out = dot_nt(part, spread)
        total = out if total is None else total + out
    return total


def narrow_t(values, spread):
    if values.dtype == BF:
        return dot_nt(spread, values)
    total, left = None, values
    for _ in range(3):
        part = left.astype(BF)
        left = left - part.astype(F32)
        out = dot_nt(spread, part)
        total = out if total is None else total + out
    return total


def sum_block(ref, other, j, height):
    at = slice(j * height, (j + 1) * height)
    out = ref[at, :].astype(F32)
    return out if other is None else out + other[at, :].astype(F32)


def sum_matrix(ref, other, first, count, height):
    return jnp.concatenate([sum_block(ref, other, first + j, height) for j in range(count)], 1)


def unpack_up_kernel(place, *refs):
    parts, (e_ref, up_ref, o_ref) = refs[:-3], refs[-3:]
    size, rows = up_ref.shape[0], parts[0].shape[0] // (FF_BLOCKS - CHUNK // LANES)
    cut = FF_BLOCKS - CHUNK // LANES
    for layer in range(2):

        @pl.when(place[2] == layer)
        def _():
            u, got_u, v, got_v = parts[4 * layer : 4 * layer + 4]
            for j in range(FF_BLOCKS):
                block = sum_block(u, got_u, j, rows) if j < cut else sum_block(v, got_v, j - cut, rows)
                up_ref[:, 0, j * LANES : (j + 1) * LANES] = block[:size]
            o_ref[:, 0, :] = narrow(sum_matrix(v, got_v, FF_BLOCKS - cut, OUT_BLOCKS, rows), e_ref[...])[:size]


def unpack_down_kernel(place, *refs):
    parts, (e_ref, gate_ref, down_ref) = refs[:-3], refs[-3:]
    size, ff_rows = gate_ref.shape[0], down_ref.shape[0]
    rows = parts[0].shape[0] // FF_BLOCKS
    for layer in range(2):

        @pl.when(place[2] == layer)
        def _():
            a, got_a = parts[2 * layer : 2 * layer + 2]
            down, gate = (a, got_a) if layer == 0 else (got_a, a)
            for j in range(FF_BLOCKS):
                gate_ref[:, 0, j * LANES : (j + 1) * LANES] = sum_block(gate, None, j, rows)[:size]
            down_ref[...] = narrow(sum_matrix(down, None, 0, OUT_BLOCKS, ff_rows), e_ref[...])


def unpack_qkv_kernel(place, *refs):
    parts, (q_ref, k_ref, v_ref, gain_ref) = refs[:-4], refs[-4:]
    size = q_ref.shape[0]
    kv_blocks = KVW // LANES
    rows = parts[0].shape[0] // (OUT_BLOCKS + kv_blocks + 1)
    for layer in range(2):

        @pl.when(place[2] == layer)
        def _():
            s, got = parts[2 * layer : 2 * layer + 2]
            q_ref[:, 0, :] = sum_matrix(s, got, 0, OUT_BLOCKS, rows)[:size, :D]
            both = sum_matrix(s, got, OUT_BLOCKS, kv_blocks, rows)
            k_ref[:, 0, :] = both[:size, : KV * HD]
            v_ref[:, 0, :] = both[:size, KV * HD :]
            gain_ref[...] = sum_block(s, got, OUT_BLOCKS + kv_blocks, rows).T


def unpack(kernel, name, place, parts, shapes):
    return pl.pallas_call(
        kernel,
        out_shape=[jax.ShapeDtypeStruct(shape, F32) for shape in shapes],
        in_specs=[SMEM] + [VMEM] * len(parts),
        out_specs=[VMEM] * len(shapes),
        compiler_params=BIG,
        cost_estimate=cost(4),
        name=name,
    )(place, *parts)


def join_kernel(place, own0, own1, got, e_ref, out_ref):
    section = place[2]
    for layer, own in enumerate((own0, own1)):

        @pl.when(section == layer)
        def _():
            out_ref[layer] = narrow_t(own[...], e_ref[...]).astype(out_ref.dtype)
            out_ref[1 - layer] = narrow_t(got[...], e_ref[...]).astype(out_ref.dtype)


def join(place, own0, own1, got, spread, dtype):
    return pl.pallas_call(
        join_kernel,
        out_shape=jax.ShapeDtypeStruct((2, D, own0.shape[0]), dtype),
        in_specs=[SMEM] + [VMEM] * 4,
        out_specs=VMEM,
        compiler_params=BIG,
        cost_estimate=cost(4),
        name="join",
    )(place, own0, own1, got, spread).transpose(0, 2, 1)


def spread_matrix(shards):
    size, room = D // shards, PADDED // shards
    feature = lax.broadcasted_iota(jnp.int32, (D, PADDED), 0)
    place = lax.broadcasted_iota(jnp.int32, (D, PADDED), 1)
    return (feature // size * room + feature % size == place).astype(BF)


def to_blocks(matrix):
    rows, width = matrix.shape
    return matrix.reshape(rows, width // LANES, LANES).transpose(1, 0, 2).reshape(-1, LANES)


def from_blocks(blocks, rows):
    return blocks.reshape(-1, rows, LANES).transpose(1, 0, 2).reshape(rows, -1)


def plus(left, right):
    return (left.astype(F32) + right.astype(F32)).astype(BF)


def after(value, *earlier):
    return lax.optimization_barrier((value,) + earlier)[0]


def scatter_z(parts):
    return lax.psum_scatter(parts, "z", scatter_dimension=0, tiled=False)


def scatter_z_small(parts, *before_last):
    count, me = lax.axis_size("z"), lax.axis_index("z")
    while parts.shape[0] > 1:
        step = parts.shape[0] // 2
        split = parts.reshape((2, step) + parts.shape[1:])
        bit = lax.rem(lax.div(me, step), 2)
        keep = lax.dynamic_index_in_dim(split, bit, 0, False)
        send = lax.dynamic_index_in_dim(split, 1 - bit, 0, False)
        if step == 1 and before_last:
            send = after(send, *before_last)
        parts = plus(keep, lax.ppermute(send, "z", [(i, i ^ step) for i in range(count)]))
    return parts[0]


def to_owner(part, layer):
    return lax.ppermute(part, "section", [(1 - layer, layer)])


def per_device_blocks(tokens, cotangent, positions, attn_gain, w_query, w_key, w_value, w_out, ffn_gain, w_gate, w_up, w_down):
    section, half = lax.axis_index("section"), lax.axis_index("dp")
    z_index, core = lax.axis_index("z"), lax.axis_index("core")
    plane = ("dp", "z", "core")
    size, ff_rows = w_query.shape[1], w_down.shape[1]
    shards = D // size
    room = PADDED // shards
    chips = shards // 2
    qkv_rows = QKV_BLOCKS * room
    block_range = jnp.stack([2 - core, 2 * z_index + 2]).astype(jnp.int32)
    place = jnp.stack([core, half, section]).astype(jnp.int32)
    spread = spread_matrix(shards)

    def mine(array_in):
        return lax.dynamic_index_in_dim(array_in, section, 0, keepdims=False)

    def widen(array_in):
        return project(array_in, spread).astype(BF)

    def padded(array_in):
        return jnp.pad(array_in, ((0, room - size), (0, 0)))

    gains = jnp.concatenate([attn_gain, ffn_gain], 0).T
    qkv = jnp.concatenate([w_key[0], w_value[0], w_query[0], gains, jnp.zeros((size, HD - 2), BF)], -1)
    narrow = jnp.concatenate([qkv, widen(w_out[0]), w_gate[0], w_up[0]], -1)
    shard = jnp.concatenate([to_blocks(padded(narrow)), to_blocks(widen(w_down[0]))], 0)
    first, rest = shard[:qkv_rows], shard[qkv_rows:]
    got_first = swap(first, "section")
    got_rest = swap(after(rest, got_first), "section")

    def layer_shard(own, got, layer):
        return jnp.where(section == layer, own, got)

    def gathered(*pieces):
        block = pieces[0] if len(pieces) == 1 else jnp.concatenate(pieces, 0)
        return lax.all_gather(block, plane, axis=0)

    def gains_at(whole, base):
        at = base + (QKV_BLOCKS - 1) * room
        gain = whole[:, at : at + room, HD : HD + 2].reshape(-1, 2).T.astype(F32)
        return gain[:1], gain[1:]

    early = gathered(layer_shard(first, got_first, 0))
    middle = gathered(layer_shard(rest, got_rest, 0), after(layer_shard(first, got_first, 1), early))
    base1 = rest.shape[0]
    w0 = (early, 0, middle, 0) + gains_at(early, 0)
    angle_cos, angle_sin = rope_tables(mine(positions))
    cos = jnp.concatenate([angle_cos[:, 0]] * 2, -1)
    sin = jnp.concatenate([angle_sin[:, 0]] * 2, -1)

    def attention(x, layer, *earlier):
        w_a, at_a, gain_a = layer[0], layer[1], layer[4]
        na, q, kv = qkv_forward(x, gain_a, cos, sin, w_a, at_a)
        kv_all = spread_kv(kv)
        o, op, lse = attend(block_range, after(q, *earlier) if earlier else q, kv_all, spread)
        return na, op, (x, q, kv_all, o, lse)

    x0 = widen(mine(tokens))
    na0, op0, saved0 = attention(x0, w0)
    late = gathered(after(layer_shard(rest, got_rest, 1), *saved0[2][0]))
    w1 = (middle, base1, late, 0) + gains_at(middle, base1)
    acts0, mixed0, gu0, y0 = ffn_forward(op0, x0, na0, w0[5], w0[2], w0[3])
    own0, send0 = turn(place, acts0)
    na1, op1, saved1 = attention(y0, w1, own0)
    y1, own1, send1, back1, dm1, do1, dgf1 = ffn_both(
        place, op1, y0, na1, w1[5], widen(mine(cotangent)), spread, w1[2], w1[3]
    )

    def backward_attn(do, saved):
        x, q, kv_all, o, lse = saved
        return attend_back(block_range, q, o, do, lse, cos, sin, kv_all)

    def backward_qkv(dq, shares, dm, dgf, layer, saved):
        w_a, at_a, w_f, at_f, gain_a, gain_f = layer
        return qkv_backward(dq, shares, cos, sin, saved[0], gain_a, dm, dgf, w_a, at_a)

    def halve(total):
        split = total.reshape((2, chips // 2) + total.shape[1:])
        return lax.dynamic_index_in_dim(split, half, 0, False), lax.dynamic_index_in_dim(split, 1 - half, 0, False)

    def scatter(*pieces, joined=None):
        if joined is None:
            joined = jnp.concatenate(pieces, 1) if len(pieces) > 1 else pieces[0]
        total = scatter_z(joined)
        cuts, at = [], 0
        for piece in pieces:
            cuts.append(total[at : at + piece.shape[1]])
            at += piece.shape[1]
        return cuts

    def cross(keep, got):
        keep, send = halve(plus(keep, got))
        return keep, swap(send, "dp")

    def swap_all(sends, axis):
        return [swap(send, axis) for send in sends]

    def all_after(values, *earlier):
        return [after(value, *earlier) for value in values]

    other0, other1 = swap(send0, "core"), swap(send1, "core")

    def swap_all(sends, axis):
        return [swap(send, axis) for send in sends]

    def query_grads(own, got):
        return own, got[-2:]

    back_other1 = swap(back1, "core")
    dq1, dkv1, away1 = backward_attn(do1, saved1)
    got1 = swap(away1, "core")
    grads1 = grad_ffn(place, own1, other1, after(back1, dkv1), back_other1, shards)
    keep_a1, send_a1, keep_u1, send_u1 = grads1[:2], grads1[2:4], grads1[4:6], grads1[6:8]
    got_a1, got_u1 = swap_all(send_a1, "section"), swap_all(send_u1, "dp")
    shares1, _ = collect_kv(dkv1, got1, [(), (), (send_u1[0],)])
    dq1 = after(dq1, got_a1[0], got_u1[0])
    dkv_low1, dx1_low, back0, dm0, do0, dgf0 = both_back(
        dq1, shares1, cos, sin, y0, w1[4], dm1, dgf1, w1[0], w1[1], mixed0, w0[5], gu0, spread, w0[2], w0[3]
    )

    back0 = after(back0, got_a1[1], got_u1[1])
    got_y = swap(after(jnp.where(section == 0, y1, y0), back0), "section")
    keep_a1, keep_u1 = all_after(keep_a1, dkv_low1), all_after(keep_u1, dkv_low1)
    in_u1 = list(map(plus, keep_u1, got_u1))
    joined_u1 = jnp.concatenate(in_u1, 1)
    sum_u1 = scatter(*in_u1, joined=joined_u1)
    back_other0 = swap(back0, "core")
    grads0 = grad_ffn(place, own0, other0, after(back0, joined_u1), back_other0, shards)
    keep_a0, send_a0, keep_u0, send_u0 = grads0[:2], grads0[2:4], grads0[4:6], grads0[6:8]
    (keep_b1, got_b1), (keep_c1, got_c1) = map(cross, keep_a1, got_a1)
    got1 = after(got1, send_u0[0])
    keep_s1, send_s1 = grad_attn(place, own1, other1, *query_grads(dq1, got1), dkv_low1, swap(dkv_low1, "core"))
    got_a0 = swap_all(send_a0, "section")
    got_u0 = [swap(send_u0[0], "dp"), swap(jnp.concatenate([send_u0[1], send_s1], 1), "dp")]
    away_u1 = to_owner(jnp.concatenate(sum_u1, 0), 1)
    dq0, dkv0, away0 = backward_attn(after(do0, send_s1, got_y), saved0)
    away0 = after(away0, got_a0[0], got_u0[0], got_b1, got_c1, *sum_u1)
    keep_b1, keep_c1 = after(keep_b1, away0), after(keep_c1, away0)
    sum_a1 = scatter(plus(keep_b1, got_b1), plus(keep_c1, got_c1))
    got0 = swap(away0, "core")
    shares0, last = collect_kv(dkv0, got0, [(got_a0[1], got_u0[1])])
    keep_q0, send_q0 = grad_attn(place, own0, other0, *query_grads(dq0, got0))
    keep_b0, got_b0 = cross(after(keep_a0[0], away0), got_a0[0])
    kept = after(jnp.concatenate([keep_u0[1], keep_s1], 1), last)
    late0 = [plus(after(keep_u0[0], last), got_u0[0]), plus(kept, got_u0[1])]
    joined0 = jnp.concatenate(late0, 1)
    away_a1 = to_owner(jnp.concatenate(sum_a1, 0), 1)
    dq0 = after(dq0, send_q0, joined0, away_u1, got_b0)
    dkv_low0, dx0, dx0_low = backward_qkv(dq0, shares0, dm0, dgf0, w0, saved0)
    got_q0 = swap(after(send_q0, shares0[-1]), "dp")
    keep_c0, got_c0 = cross(after(keep_a0[1], shares0[-1]), got_a0[1])
    sum_v0, sum_w0 = scatter(*late0, joined=joined0)
    keep_k0, send_k0 = grad_attn(place, own0, other0, after(dkv_low0, got_c0), swap(dkv_low0, "core"))
    last0 = [plus(after(keep, sum_w0), got) for keep, got in ((keep_b0, got_b0), (keep_c0, got_c0))]
    sum_a0 = jnp.concatenate(scatter(*last0), 0)
    got_k0 = swap(send_k0, "dp")
    keep_q0, keep_k0 = after(keep_q0, away_a1, *last0), after(keep_k0, *last0)
    pieces = [plus(keep_q0, got_q0), plus(keep_k0, got_k0)]

    cut = send_u0[1].shape[1]
    sum_s1, sum_w0 = sum_w0[cut:], sum_w0[:cut]
    away_s1 = to_owner(sum_s1, 1)
    wide = lambda width: (size, 1, width)
    parts = [part for own in (sum_v0, sum_w0) for part in (own, to_owner(own, 0))]
    cut_u = sum_u1[0].shape[0]
    parts += [sum_u1[0], away_u1[:cut_u], sum_u1[1], away_u1[cut_u:]]
    g_up, g_o = unpack(unpack_up_kernel, "unpack_up", place, parts + [spread], (wide(FF), wide(D)))
    away_a0 = to_owner(sum_a0, 0)
    sum_s0 = scatter_z_small(jnp.concatenate(pieces, 1), g_up, away_a0)
    parts = [sum_a0, away_a0, jnp.concatenate(sum_a1, 0), away_a1]
    g_gate, g_down = unpack(unpack_down_kernel, "unpack_down", place, parts + [spread], (wide(FF), (ff_rows, D)))
    parts = [after(sum_s0, g_gate), to_owner(sum_s0, 0), sum_s1, away_s1]
    shapes = (wide(D), wide(KV * HD), wide(KV * HD), (LANES, room))
    g_q, g_k, g_v, gains = unpack(unpack_qkv_kernel, "unpack_qkv", place, parts, shapes)
    section_out = join(place, y0, y1, got_y, spread, BF)
    got = swap(jnp.where(section == 0, dx1_low, dx0_low), "section")
    input_grad = join(place, dx0, dx1_low, got, spread, F32)
    flat = lambda part: part.transpose(1, 0, 2)[0]
    g_q, g_k, g_v, g_o, g_gate, g_up = map(flat, (g_q, g_k, g_v, g_o, g_gate, g_up))
    outs = (section_out, input_grad, gains[0, :size], g_q, g_k, g_v, g_o, gains[1, :size], g_gate, g_up, g_down)
    return tuple(part[None] for part in outs)


def solution(mesh):
    sizes = mesh.devices.shape
    grid = Mesh(mesh.devices.reshape(sizes[0], sizes[1], sizes[2] // 2, 2), ("section", "dp", "z", "core"))
    ctx = ("z", "core")
    plane = ("dp", "z", "core")
    vector = P("section", plane)
    matrix = P("section", plane, None)
    in_specs = (
        P("dp", ctx, None),
        P("dp", ctx, None),
        P("dp", ctx),
        vector,
        matrix,
        matrix,
        matrix,
        matrix,
        vector,
        matrix,
        matrix,
        matrix,
    )
    acts = P("section", "dp", ctx, None)
    out_specs = (acts, acts, vector, matrix, matrix, matrix, matrix, vector, matrix, matrix, matrix)
    shards = sizes[1] * sizes[2]
    aligned = shards == 16
    return jax.shard_map(per_device_blocks if aligned else per_device, mesh=grid, in_specs=in_specs, out_specs=out_specs, check_vma=False)
```
